32 devices in a mesh: pair: 4 (over y, x), row: 8 (over z, core).
Axes of the slice: x: 2, y: 2, z: 4, core: 2. Of those that a mesh axis runs over, the one named last changes fastest.
Arguments:
- matrix: float32 [2, 32768, 512], P(None, 'row', 'pair'), may hold values from -100 to 100, as said below
Outputs:
- rotated_matrix: float32 [2, 32768, 512], P(None, 'row', 'pair')
The draws below stay inside these ranges and needn't reach their ends.
Inputs may be any that keep to these rules, and one draw needn't show every extreme that they name: `matrix`: entries are real values with column blocks that are far from orthogonal to one another.
All inputs are finite; a program needn't handle non-finite values.
Results may differ from the reference program's by a relative error of at most 0.00014.
Values sent between devices are 32-bit elements; how exact they have to be, the bound alone decides.
No kernel may reach another device: no remote copies, remote signals or barrier semaphores. Data moves between devices by JAX's collectives and lax.ppermute only.
A program may use at most 64 MiB of HBM per device.

```python
import math
import jax
import jax.numpy as jnp
from jax import lax

BW = 128
STEPS = 2
SWEEPS = 2
NEWTON = 3
COLS = 512
ROWS = 32768
N_PAIR = 4


def draw_matrix(key, part):
    subkeys = jax.random.split(key, 5)
    row_scale = jnp.exp(jax.random.uniform(subkeys[0], (ROWS,), jnp.float32, math.log(0.3), math.log(3.0)))
    col_scale = jnp.exp(jax.random.uniform(subkeys[1], (2, 1, COLS), jnp.float32, math.log(0.3), math.log(3.0)))
    common = jnp.clip(jax.random.normal(subkeys[2], (ROWS,), jnp.float32), -3.0, 3.0)
    weight = jnp.clip(jax.random.normal(subkeys[3], (2, 1, COLS), jnp.float32), -3.0, 3.0)
    noise_part = jnp.clip(jax.random.normal(subkeys[4], (2, ROWS, COLS), jnp.float32), -4.0, 4.0)
    inner = 0.7 * common[None, :, None] * weight + noise_part
    return (row_scale[None, :, None] * col_scale * inner).astype(jnp.float32)


def setup_inputs(seed: int = 0) -> dict:
    seeds = jax.random.split(jax.random.key(seed), 2)
    matrix = draw_matrix(jax.random.fold_in(seeds[1], 71), 0)
    return dict(matrix=matrix)


def gram_of(left_cols, right_cols):
    return lax.dot_general(left_cols, right_cols, (((0,), (0,)), ((), ())), precision=lax.Precision.HIGHEST, preferred_element_type=jnp.float32)

def product(left_mat, right_mat):
    return jnp.dot(left_mat, right_mat, precision=lax.Precision.HIGHEST, preferred_element_type=jnp.float32)

def polar_turn(gram_matrix):
    half_width = gram_matrix.shape[0] // 2
    diagonal = jnp.diagonal(gram_matrix)
    inverse = 1.0 / jnp.sqrt(diagonal + 1e-06)
    cross_part = gram_matrix[:half_width, half_width:] * inverse[:half_width, None] * inverse[None, half_width:]
    cross_part = cross_part / (1.0 + jnp.sqrt(jnp.sum(cross_part * cross_part)))
    zero_block = jnp.zeros((half_width, half_width), jnp.float32)
    skew_part = jnp.concatenate([jnp.concatenate([zero_block, cross_part], 1), jnp.concatenate([-cross_part.T, zero_block], 1)], 0)
    identity = jnp.eye(2 * half_width, dtype=jnp.float32)
    factor = identity + skew_part
    for repeat in range(NEWTON):
        factor = product(factor, 1.5 * identity - 0.5 * gram_of(factor, factor))
    return factor

def pair_rotation(gram_matrix):
    rotation = jnp.eye(gram_matrix.shape[0], dtype=jnp.float32)
    current = gram_matrix
    for sweep_index in range(SWEEPS):
        factor = polar_turn(current)
        rotation = product(rotation, factor)
        if sweep_index + 1 < SWEEPS:
            current = gram_of(factor, product(current, factor))
    return rotation

def rotate_pair(blocks):
    upper_block, lower_block = blocks
    pair_cols = jnp.concatenate([upper_block, lower_block], 1)
    rotation = pair_rotation(gram_of(pair_cols, pair_cols))
    rotated = product(pair_cols, rotation)
    return (rotated[:, :BW], rotated[:, BW:])

def reference(matrix):
    row_total = matrix.shape[1]
    upper_stack = matrix[0].reshape(row_total, N_PAIR, BW).transpose(1, 0, 2)
    lower_stack = matrix[1].reshape(row_total, N_PAIR, BW).transpose(1, 0, 2)
    for step_index in range(STEPS):
        upper_stack, lower_stack = lax.map(rotate_pair, (upper_stack, lower_stack))
        new_upper = jnp.concatenate([upper_stack[0:1], lower_stack[0:1], upper_stack[1:N_PAIR - 1]], 0)
        new_lower = jnp.concatenate([lower_stack[1:], upper_stack[N_PAIR - 1:]], 0)
        upper_stack, lower_stack = (new_upper, new_lower)
    upper_flat = upper_stack.transpose(1, 0, 2).reshape(row_total, N_PAIR * BW)
    lower_flat = lower_stack.transpose(1, 0, 2).reshape(row_total, N_PAIR * BW)
    return jnp.stack([upper_flat, lower_flat], 0)
```

```python
import functools

import jax
import jax.numpy as jnp
from jax import lax
from jax.experimental import pallas as pl
from jax.experimental.pallas import tpu as pltpu
from jax.sharding import PartitionSpec as P


F32 = jnp.float32
BF16 = jnp.bfloat16
VMEM_LIMIT = 48 * 1024 * 1024


def after(p, n):
    if p == 0:
        return 1
    if p % 2:
        return n - 2 if p == n - 1 else p + 2
    return p - 2


def halves(x):
    high = x.astype(BF16)
    return high, (x - high.astype(F32)).astype(BF16)


def dot3(left, right, contract):
    def one(a, b):
        return lax.dot_general(a, b, (contract, ((), ())), preferred_element_type=F32)

    return one(left[0], right[0]) + (one(left[0], right[1]) + one(left[1], right[0]))


PLAIN = ((1,), (0,))
LEFT_T = ((0,), (0,))
RIGHT_T = ((1,), (1,))


def eye_of(width):
    rows = lax.broadcasted_iota(jnp.int32, (width, width), 0)
    cols = lax.broadcasted_iota(jnp.int32, (width, width), 1)
    return rows, cols


def polar(cross, sign):
    width = cross.shape[0]
    rows, cols = eye_of(width)
    unit = (rows == cols).astype(F32)
    x = halves(cross)
    squares = [dot3(x, x, RIGHT_T), dot3(x, x, LEFT_T)]
    firsts, lasts, thirds = [], [], []
    for s in squares:
        sh = halves(s)
        s2 = dot3(sh, sh, PLAIN)
        e = 0.75 * s2 - 0.25 * dot3(halves(s2), sh, PLAIN)
        eh = halves(e)
        e2 = dot3(eh, eh, PLAIN)
        z = unit - 0.5 * s + 0.5 * e - 0.25 * dot3(sh, eh, PLAIN)
        f = 0.75 * e2 + 0.25 * dot3(halves(e2), eh, PLAIN)
        fh = halves(f)
        thirds.append(fh)
        firsts.append(z)
        lasts.append(z + 0.5 * dot3(halves(z), fh, PLAIN))
    xz = dot3(x, halves(firsts[1]), PLAIN)
    wide = sign * (xz + 0.5 * dot3(halves(xz), thirds[1], PLAIN))
    return jnp.concatenate(
        [jnp.concatenate([lasts[0], wide], 1), jnp.concatenate([-wide.T, lasts[1]], 1)], 0
    )


def scaled(cross, down, across):
    x = cross * lax.rsqrt(down + 1e-06) * lax.rsqrt(across + 1e-06)
    return x / (1.0 + jnp.sqrt(jnp.sum(x * x)))


def rotation_of(upper, cross, lower, sign):
    width = cross.shape[0]
    rows, cols = eye_of(width)
    same = rows == cols
    zero = jnp.zeros((width, width), F32)
    down = jnp.sum(jnp.where(same, upper, zero), 1, keepdims=True)
    across = jnp.sum(jnp.where(same, lower, zero), 0, keepdims=True)
    first = polar(scaled(cross, down, across), sign)
    gram = jnp.concatenate(
        [jnp.concatenate([upper, cross], 1), jnp.concatenate([cross.T, lower], 1)], 0
    )
    first_halves = halves(first)
    turned = dot3(halves(gram), first_halves, PLAIN)
    second_cross = dot3(halves(first[:, :width]), halves(turned[:, width:]), LEFT_T)
    diagonal = jnp.sum(first * turned, 0, keepdims=True)
    down = jnp.sum(jnp.where(same, diagonal[:, :width], zero), 1, keepdims=True)
    second = polar(scaled(second_cross, down, diagonal[:, width:]), sign)
    return gram, dot3(first_halves, halves(second), PLAIN)


def core_of():
    return lax.rem(lax.axis_index("row"), 2)


def first_is_upper():
    p = lax.axis_index("pair")
    clock_upper = (p == 0) | (lax.rem(p, 2) == 1)
    return (core_of() == 0) == clock_upper


def gram_kernel(matrix_ref, keep_ref, give_ref, main_ref, rest_ref):
    step = pl.program_id(0)
    block = jnp.concatenate([matrix_ref[0], matrix_ref[1]], 1)
    high, low = halves(block)
    main = lax.dot_general(high, high, (LEFT_T, ((), ())), preferred_element_type=F32)
    rest = lax.dot_general(high, low, (LEFT_T, ((), ())), preferred_element_type=F32)

    @pl.when(step == 0)
    def _():
        main_ref[...] = main
        rest_ref[...] = rest

    @pl.when(step > 0)
    def _():
        main_ref[...] += main
        rest_ref[...] += rest

    @pl.when(step == pl.num_programs(0) - 1)
    def _():
        total = main_ref[...] + (rest_ref[...] + rest_ref[...].T)
        width = total.shape[0] // 2
        rows, cols = eye_of(width)
        upper, lower = total[:width, :width], total[width:, width:]
        diagonal = jnp.sum(jnp.where(rows == cols, lower, jnp.zeros_like(lower)), 0, keepdims=True)
        packed = jnp.where(rows <= cols, upper, lower)
        pad = jnp.broadcast_to(diagonal, (8, width))
        cross = total[:width, width:]
        mine = core_of() == 0
        keep_ref[:width] = jnp.where(mine, cross, packed)
        give_ref[:width] = jnp.where(mine, packed, cross)
        keep_ref[width:] = pad
        give_ref[width:] = pad


def local_gram(matrix, chunk):
    rows, width = matrix.shape[1:]
    out = jax.ShapeDtypeStruct((width + 8, width), F32)
    whole = pl.BlockSpec((width + 8, width), lambda i: (0, 0))
    return pl.pallas_call(
        gram_kernel,
        grid=(rows // chunk,),
        in_specs=[pl.BlockSpec((2, chunk, width), lambda i: (0, i, 0))],
        out_specs=[whole, whole],
        out_shape=[out, out],
        scratch_shapes=[pltpu.VMEM((2 * width, 2 * width), F32)] * 2,
        compiler_params=pltpu.CompilerParams(vmem_limit_bytes=VMEM_LIMIT),
        cost_estimate=pl.CostEstimate(flops=16 * rows * width * width, bytes_accessed=8 * rows * width, transcendentals=0),
        name="gram",
    )(matrix)


def rotate_kernel(mine_ref, other_ref, first_ref, second_ref, gram_ref):
    width = mine_ref.shape[1]
    holds_cross = core_of() == 0
    mine, other = mine_ref[...], other_ref[...]
    cross = jnp.where(holds_cross, mine[:width], other[:width])
    packed = jnp.where(holds_cross, other, mine)
    diagonal = packed[width : width + 1]
    packed = packed[:width]
    rows, cols = eye_of(width)
    flipped = packed.T
    upper = jnp.where(rows <= cols, packed, flipped)
    lower = jnp.where(rows > cols, packed, flipped)
    lower = jnp.where(rows == cols, diagonal, lower)
    gram, rotation = rotation_of(upper, cross, lower, 1.0)
    left, right = rotation[:, :width], rotation[:, width:]
    upper_first = first_is_upper()
    first_ref[...] = jnp.where(upper_first, left, right)
    second_ref[...] = jnp.where(upper_first, right, left)
    gram_ref[...] = gram


def first_rotation(mine, other):
    width = mine.shape[1]
    half = jax.ShapeDtypeStruct((2 * width, width), F32)
    return pl.pallas_call(
        rotate_kernel,
        out_shape=[half, half, jax.ShapeDtypeStruct((2 * width, 2 * width), F32)],
        compiler_params=pltpu.CompilerParams(vmem_limit_bytes=VMEM_LIMIT),
        name="first_rotation",
    )(mine, other)


def blocks_kernel(gram_ref, first_ref, second_ref, first_gram_ref, second_gram_ref):
    gram = halves(gram_ref[...])
    for turn_ref, out_ref in ((first_ref, first_gram_ref), (second_ref, second_gram_ref)):
        turn = halves(turn_ref[...])
        out_ref[...] = dot3(turn, halves(dot3(gram, turn, PLAIN)), LEFT_T)


def block_grams(gram, first, second):
    width = first.shape[1]
    out = jax.ShapeDtypeStruct((width, width), F32)
    return pl.pallas_call(
        blocks_kernel,
        out_shape=[out, out],
        compiler_params=pltpu.CompilerParams(vmem_limit_bytes=VMEM_LIMIT),
        name="block_grams",
    )(gram, first, second)


def product_kernel(matrix_ref, turn_ref, out_ref):
    width = out_ref.shape[1]
    turn = halves(turn_ref[...])
    upper, lower = halves(matrix_ref[0]), halves(matrix_ref[1])
    top = tuple(t[:width] for t in turn)
    bottom = tuple(t[width:] for t in turn)
    out_ref[...] = dot3(upper, top, PLAIN) + dot3(lower, bottom, PLAIN)


def rotated(matrix, turn, start, count, chunk):
    width = matrix.shape[2]
    offset = start // chunk
    return pl.pallas_call(
        product_kernel,
        grid=(count // chunk,),
        in_specs=[
            pl.BlockSpec((2, chunk, width), lambda i: (0, i + offset, 0)),
            pl.BlockSpec((2 * width, width), lambda i: (0, 0)),
        ],
        out_specs=pl.BlockSpec((chunk, width), lambda i: (i, 0)),
        out_shape=jax.ShapeDtypeStruct((count, width), F32),
        compiler_params=pltpu.CompilerParams(vmem_limit_bytes=VMEM_LIMIT),
        cost_estimate=pl.CostEstimate(flops=12 * count * width * width, bytes_accessed=12 * count * width, transcendentals=0),
        name="product",
    )(matrix, turn)


def cross_kernel(own_ref, far_ref, total_ref, out_ref):
    part = dot3(halves(own_ref[...]), halves(far_ref[...]), LEFT_T)

    @pl.when(pl.program_id(0) == 0)
    def _():
        out_ref[...] = total_ref[...] + part

    @pl.when(pl.program_id(0) > 0)
    def _():
        out_ref[...] += part


def cross_gram(own, far, total, start, chunk):
    count, width = far.shape
    offset = start // chunk
    return pl.pallas_call(
        cross_kernel,
        grid=(count // chunk,),
        in_specs=[
            pl.BlockSpec((chunk, width), lambda i: (i + offset, 0)),
            pl.BlockSpec((chunk, width), lambda i: (i, 0)),
            pl.BlockSpec((width, width), lambda i: (0, 0)),
        ],
        out_specs=pl.BlockSpec((width, width), lambda i: (0, 0)),
        out_shape=jax.ShapeDtypeStruct((width, width), F32),
        compiler_params=pltpu.CompilerParams(vmem_limit_bytes=VMEM_LIMIT),
        cost_estimate=pl.CostEstimate(flops=6 * count * width * width, bytes_accessed=8 * count * width, transcendentals=0),
        name="cross_gram",
    )(own, far, total)


def second_kernel(own_gram_ref, far_gram_ref, here_ref, there_ref, out_ref):
    width = out_ref.shape[1]
    p, n = lax.axis_index("pair"), lax.axis_size("pair")
    odd = lax.rem(p, 2) == 1
    outward = core_of() == 1
    own_upper_out = (p == 0) | (odd & (p != n - 1))
    own_upper = (outward & own_upper_out) | (jnp.logical_not(outward) & jnp.logical_not(odd))
    sign = jnp.where(own_upper, 1.0, -1.0).astype(F32)
    cross = here_ref[...] + there_ref[...].T
    _, rotation = rotation_of(own_gram_ref[...], cross, far_gram_ref[...], sign)
    keeps_own = (outward & (p == 0)) | (jnp.logical_not(outward) & (p == 1))
    out_ref[...] = jnp.where(keeps_own, rotation[:, :width], rotation[:, width:])


def second_rotation(own_gram, far_gram, here, there):
    width = here.shape[1]
    return pl.pallas_call(
        second_kernel,
        out_shape=jax.ShapeDtypeStruct((2 * width, width), F32),
        compiler_params=pltpu.CompilerParams(vmem_limit_bytes=VMEM_LIMIT),
        name="second_rotation",
    )(own_gram, far_gram, here, there)


def last_kernel(slot_ref, own_ref, *rest):
    del slot_ref
    far_refs, turn_ref, out_ref = rest[:-2], rest[-2], rest[-1]
    width = own_ref.shape[1]
    turn = halves(turn_ref[...])
    top = tuple(t[:width] for t in turn)
    bottom = tuple(t[width:] for t in turn)
    step = pl.program_id(0)
    for k, far_ref in enumerate(far_refs):

        @pl.when(step == k)
        def _():
            out_ref[0] = dot3(halves(own_ref[...]), top, PLAIN) + dot3(halves(far_ref[...]), bottom, PLAIN)


def last_first_kernel(slot_ref, own_ref, *rest):
    last_kernel(slot_ref, own_ref, *rest)


def last_second_kernel(slot_ref, own_ref, *rest):
    last_kernel(slot_ref, own_ref, *rest[:-2], rest[-1])


def last_product(slot, own, fars, turn, done):
    rows, width = own.shape
    count = rows // len(fars)
    grid_spec = pltpu.PrefetchScalarGridSpec(
        num_scalar_prefetch=1,
        grid=(len(fars),),
        in_specs=[pl.BlockSpec((count, width), lambda i, s: (i, 0))]
        + [pl.BlockSpec((count, width), lambda i, s: (0, 0))] * len(fars)
        + [pl.BlockSpec((2 * width, width), lambda i, s: (0, 0))]
        + ([pl.BlockSpec(memory_space=pl.ANY)] if done is not None else []),
        out_specs=pl.BlockSpec((1, count, width), lambda i, s: (s[0], i, 0)),
    )
    return pl.pallas_call(
        last_first_kernel if done is None else last_second_kernel,
        grid_spec=grid_spec,
        out_shape=jax.ShapeDtypeStruct((2, rows, width), F32),
        input_output_aliases={} if done is None else {3 + len(fars): 0},
        compiler_params=pltpu.CompilerParams(vmem_limit_bytes=VMEM_LIMIT),
        cost_estimate=pl.CostEstimate(flops=12 * rows * width * width, bytes_accessed=16 * rows * width, transcendentals=0),
        name="last_product",
    )(slot, own, *fars, turn, *([] if done is None else [done]))


def body(pairs_count, rows_count, matrix):
    rows, width = matrix.shape[1:]
    parts = 4
    part = rows // parts
    chunk = min(1024, part)
    flat = [(p, r) for p in range(pairs_count) for r in range(rows_count)]
    ahead = {p: after(p, pairs_count) for p in range(pairs_count)}
    behind = {q: p for p, q in ahead.items()}

    def route(moves):
        return [(p * rows_count + r, q * rows_count + t) for (p, r) in flat for (q, t) in [moves(p, r)]]

    outward = route(lambda p, r: (ahead[p] if r % 2 == 0 else behind[p], r))
    inward = route(lambda p, r: (behind[p] if r % 2 == 0 else ahead[p], r))
    crossing = route(lambda p, r: (behind[p] if r % 2 == 0 else ahead[p], r ^ 1))
    core = [(r, r ^ 1) for r in range(rows_count)]

    def travel(block, moves):
        return lax.ppermute(block, ("pair", "row"), moves)

    def chip_sum(block):
        distance = 2
        while distance < rows_count:
            block = block + lax.ppermute(block, "row", [(r, r ^ distance) for r in range(rows_count)])
            distance *= 2
        return block

    keep, give = local_gram(matrix, chunk)
    mine = chip_sum(keep + lax.ppermute(give, "row", core))
    other = lax.ppermute(mine, "row", core)
    turn_first, turn_second, gram = first_rotation(mine, other)

    sent = [rotated(matrix, turn_first, k * part, part, chunk) for k in range(parts)]
    far_first = [travel(block, outward) for block in sent]
    second = rotated(matrix, turn_second, 0, rows, chunk)
    first_gram, second_gram = block_grams(gram, turn_first, turn_second)
    far_gram = travel(first_gram, outward)

    cross = jnp.zeros((width, width), F32)
    for k in range(parts):
        cross = cross_gram(second, far_first[k], cross, k * part, chunk)
    far_second = [travel(second, inward)]

    here = chip_sum(cross)
    there = travel(here, crossing)
    turn_here = second_rotation(second_gram, far_gram, here, there)
    turn_there = lax.ppermute(turn_here, "row", core)

    p = lax.axis_index("pair")
    c = lax.axis_index("row") % 2
    slot = jnp.where(p % 2 == c, 1, 0).astype(jnp.int32).reshape(1)
    done = last_product(slot, second, far_first, turn_here, None)
    first = jnp.concatenate(sent, 0)
    return last_product(1 - slot, first, far_second, turn_there, done)


def solution(mesh):
    spec = P(None, "row", "pair")
    run = functools.partial(body, mesh.shape["pair"], mesh.shape["row"])
    return jax.shard_map(run, mesh=mesh, in_specs=(spec,), out_specs=spec, check_vma=False)
```

```python
import functools

import jax
import jax.numpy as jnp
from jax import lax
from jax.experimental import pallas as pl
from jax.experimental.pallas import tpu as pltpu
from jax.sharding import PartitionSpec as P


F32 = jnp.float32
BF16 = jnp.bfloat16
SCOPED = 16 * 1024 * 1024
WHOLE = 54 * 1024 * 1024

RAW = (5,)
LAST = 2
BULK = 12
STEP = 2


def after(p, n):
    if p == 0:
        return 1
    if p % 2:
        return n - 2 if p == n - 1 else p + 2
    return p - 2


def halves(x):
    high = x.astype(BF16)
    return high, (x - high.astype(F32)).astype(BF16)


def dot(left, right, contract=((1,), (0,))):
    return lax.dot_general(left, right, (contract, ((), ())), preferred_element_type=F32)


def product(left, right):
    width = right.shape[1]
    twice = jnp.concatenate(halves(right), 1)
    both = dot(jnp.concatenate(halves(left), 1), jnp.concatenate([twice, twice], 0))
    return both[:, :width] + both[:, width:]


def right_parts(right):
    high, low = halves(right)
    return jnp.concatenate([high, low], 1), high


def rows_product(left, parts):
    width = parts[1].shape[1]
    high, low = halves(left)
    both = dot(high, parts[0])
    return both[:, :width] + (both[:, width:] + dot(low, parts[1]))


def eye_of(width):
    rows = lax.broadcasted_iota(jnp.int32, (width, width), 0)
    cols = lax.broadcasted_iota(jnp.int32, (width, width), 1)
    return rows, cols


def polar(cross, sign):
    rows, cols = eye_of(cross.shape[0])
    unit = (rows == cols).astype(F32)
    flipped = cross.T
    s = [product(cross, flipped), product(flipped, cross)]
    s2 = [product(a, a) for a in s]
    e = [0.75 * b - 0.25 * product(b, a) for a, b in zip(s, s2)]
    e2 = [product(a, a) for a in e]
    z = [unit - 0.5 * a + 0.5 * b - 0.25 * product(a, b) for a, b in zip(s, e)]
    f = [0.75 * b + 0.25 * product(b, a) for a, b in zip(e, e2)]
    xz = product(cross, z[1])
    last = [a + 0.5 * product(a, b) for a, b in zip(z, f)]
    wide = sign * (xz + 0.5 * product(xz, f[1]))
    return jnp.concatenate(
        [jnp.concatenate([last[0], wide], 1), jnp.concatenate([-wide.T, last[1]], 1)], 0
    )


def scaled(cross, down, across):
    x = cross * lax.rsqrt(down + 1e-06) * lax.rsqrt(across + 1e-06)
    return x / (1.0 + jnp.sqrt(jnp.sum(x * x)))


def rotation_of(upper, cross, lower, sign):
    width = cross.shape[0]
    rows, cols = eye_of(width)
    same = rows == cols
    zero = jnp.zeros((width, width), F32)
    down = jnp.sum(jnp.where(same, upper, zero), 1, keepdims=True)
    across = jnp.sum(jnp.where(same, lower, zero), 0, keepdims=True)
    first = polar(scaled(cross, down, across), sign)
    gram = jnp.concatenate(
        [jnp.concatenate([upper, cross], 1), jnp.concatenate([cross.T, lower], 1)], 0
    )
    turned = rows_product(gram, right_parts(first))
    second_cross = rows_product(first[:, :width].T, right_parts(turned[:, width:]))
    diagonal = jnp.sum(first * turned, 0, keepdims=True)
    down = jnp.sum(jnp.where(same, diagonal[:, :width], zero), 1, keepdims=True)
    second = polar(scaled(second_cross, down, diagonal[:, width:]), sign)
    return gram, rows_product(first, right_parts(second))


def core_of():
    return lax.rem(lax.axis_index("row"), 2)


def first_is_upper():
    p = lax.axis_index("pair")
    clock_upper = (p == 0) | (lax.rem(p, 2) == 1)
    return (core_of() == 0) == clock_upper


def call(kernel, outs, args, name, flops=0, scratch=(), aliases=None, limit=SCOPED):
    places = [place for _, place in args]
    out_places = [place for _, place in outs]
    return pl.pallas_call(
        kernel,
        in_specs=[pl.BlockSpec(memory_space=place) for place in places],
        out_specs=[pl.BlockSpec(memory_space=place) for place in out_places],
        out_shape=[place(shape, F32) if place == pltpu.VMEM and PIN else jax.ShapeDtypeStruct(shape, F32) for shape, place in outs],
        scratch_shapes=list(scratch),
        input_output_aliases=aliases or {},
        compiler_params=pltpu.CompilerParams(vmem_limit_bytes=limit),
        cost_estimate=pl.CostEstimate(flops=flops if flops == LONG else 0, bytes_accessed=0, transcendentals=0),
        name=name,
    )(*[pltpu.with_memory_space_constraint(array, place) for array, place in args])


PIN = True
LONG = 11500000000
HERE = pltpu.VMEM
FAR = pltpu.HBM


class Rows:
    def __init__(self, *parts):
        self.parts = parts

    @classmethod
    def of(cls, refs, sizes):
        return cls(*[(ref, sum(sizes[:k]), sizes[k], 0) for k, ref in enumerate(refs)])

    def at(self, start, count):
        for ref, first, number, offset in self.parts:
            if first <= start and start + count <= first + number:
                return ref, pl.ds(offset + start - first, count)
        raise ValueError(start)

    def get(self, start, count):
        ref, rows = self.at(start, count)
        return ref[rows, :]

    def pair(self, start, count):
        ref, rows = self.at(start, count)
        return jnp.concatenate([ref[0, rows, :], ref[1, rows, :]], 1)


def spans(start, stop, step, *cuts):
    pieces = []
    while start < stop:
        count = min([step, stop - start] + [cut - start for cut in cuts if cut > start])
        pieces.append((start, count))
        start += count
    return pieces


def local_gram(matrix, sizes, step):
    rows, width = matrix.shape[1:]
    pieces = spans(0, rows, step, *[sum(sizes[:k]) for k in range(len(sizes))])

    def kernel(matrix_ref, *refs):
        part_refs, (keep_ref, give_ref, sems) = refs[: len(sizes)], refs[len(sizes) :]
        local = Rows.of(part_refs, sizes)
        copies = []
        for k, (start, count) in enumerate(pieces):
            ref, place = local.at(start, count)
            copies.append(pltpu.make_async_copy(matrix_ref.at[:, pl.ds(start, count)], ref.at[:, place], sems.at[k]))
            copies[-1].start()
        total = jnp.zeros((2 * width, 4 * width), F32)
        for copy, (start, count) in zip(copies, pieces):
            copy.wait()
            high, low = halves(local.pair(start, count))
            total = total + dot(high, jnp.concatenate([high, low], 1), ((0,), (0,)))
        rest = total[:, 2 * width :]
        total = total[:, : 2 * width] + (rest + rest.T)
        upper, cross, lower = total[:width, :width], total[:width, width:], total[width:, width:]
        r, c = eye_of(width)
        diagonal = jnp.sum(jnp.where(r == c, lower, jnp.zeros_like(lower)), 0, keepdims=True)
        packed = jnp.where(r <= c, upper, lower)
        pad = jnp.broadcast_to(diagonal, (8, width))
        mine = core_of() == 0
        keep_ref[:width] = jnp.where(mine, cross, packed)
        give_ref[:width] = jnp.where(mine, packed, cross)
        keep_ref[width:] = pad
        give_ref[width:] = pad

    outs = [((2, size, width), HERE) for size in sizes] + [((width + 8, width), HERE)] * 2
    return call(
        kernel,
        outs,
        [(matrix, FAR)],
        "gram",
        16 * rows * width * width,
        [pltpu.SemaphoreType.DMA((len(pieces),))],
        limit=WHOLE,
    )


def first_rotation(mine, other):
    width = mine.shape[1]

    def kernel(mine_ref, other_ref, first_ref, second_ref, gram_ref):
        holds_cross = core_of() == 0
        mine, other = mine_ref[...], other_ref[...]
        cross = jnp.where(holds_cross, mine[:width], other[:width])
        packed = jnp.where(holds_cross, other, mine)
        diagonal = packed[width : width + 1]
        packed = packed[:width]
        rows, cols = eye_of(width)
        flipped = packed.T
        upper = jnp.where(rows <= cols, packed, flipped)
        lower = jnp.where(rows > cols, packed, flipped)
        lower = jnp.where(rows == cols, diagonal, lower)
        gram, rotation = rotation_of(upper, cross, lower, 1.0)
        left, right = rotation[:, :width], rotation[:, width:]
        upper_first = first_is_upper()
        first_ref[...] = jnp.where(upper_first, left, right)
        second_ref[...] = jnp.where(upper_first, right, left)
        gram_ref[...] = gram

    half = ((2 * width, width), HERE)
    return call(kernel, [half, half, ((2 * width, 2 * width), HERE)], [(mine, HERE), (other, HERE)], "first_rotation")


def sent_parts(high, first, second, gram, early, last, step):
    width = first.shape[1]
    count = high.shape[1]

    def kernel(high_ref, first_ref, second_ref, gram_ref, main_ref, last_ref, second_gram_ref):
        local = Rows((high_ref, 0, count, 0))
        out = Rows((main_ref, 0, count - last, 2 * width), (last_ref, count - last, last, 0))
        main_ref[: 2 * width] = first_ref[...]
        parts = right_parts(first_ref[...])
        for start, number in spans(0, count, step, count - last):
            ref, place = out.at(start, number)
            ref[place, :] = rows_product(local.pair(start, number), parts)
        gram = gram_ref[...]
        for turn_ref, place in ((first_ref, last_ref.at[pl.ds(last, width), :]), (second_ref, second_gram_ref)):
            turn = turn_ref[...]
            place[...] = rows_product(turn.T, right_parts(rows_product(gram, right_parts(turn))))

    return call(
        kernel,
        [((2 * width + count - last, width), HERE), ((last + width, width), HERE), ((width, width), HERE)],
        [(high, HERE), (first, HERE), (second, HERE), (gram, HERE)],
        "sent_parts",
        12 * count * width * width,
    )


def rest_parts(local, first, second, bulk, early, step):
    width = first.shape[1]
    sizes = [part.shape[1] for part in local]
    rows = sum(sizes)

    def kernel(*refs):
        part_refs, (first_ref, second_ref, bulk_ref, tail_ref, raw_ref) = refs[: len(sizes)], refs[len(sizes) :]
        here = Rows.of(part_refs, sizes)
        out = Rows.of((bulk_ref, tail_ref), (bulk, rows - bulk))
        parts = right_parts(second_ref[...])
        for start, count in spans(0, rows, step, bulk, early):
            ref, place = out.at(start, count)
            ref[place, :] = rows_product(here.pair(start, count), parts)
        parts = right_parts(first_ref[...])
        for start, count in spans(0, early, step):
            raw_ref[pl.ds(start, count), :] = rows_product(here.pair(start, count), parts)

    return call(
        kernel,
        [((bulk, width), HERE), ((rows - bulk, width), HERE), ((early, width), HERE)],
        [(part, HERE) for part in local] + [(first, HERE), (second, HERE)],
        "rest_parts",
        12 * (rows + early) * width * width,
    )


def cross_term(own, far):
    return dot(jnp.concatenate(halves(own), 1), jnp.concatenate(halves(far), 1), ((0,), (0,)))


def cross_sum(total):
    width = total.shape[0] // 2
    return (total[:width, :width] + total[:width, width:]) + (total[width:, :width] + total[width:, width:])


def main_cross(far_raw, far_main, bulk, tail, step):
    width = bulk.shape[1]
    sizes = [part.shape[1] for part in far_raw]
    early, main = sum(sizes), far_main.shape[0] - 2 * width

    def kernel(*refs):
        raw_refs, (main_ref, bulk_ref, tail_ref, far_ref, out_ref) = refs[: len(sizes)], refs[len(sizes) :]
        own = Rows.of((bulk_ref, tail_ref), (bulk.shape[0], tail.shape[0]))
        raw = Rows.of(raw_refs, sizes)
        far = Rows((main_ref, early, main, 2 * width))
        parts = right_parts(main_ref[: 2 * width])
        total = jnp.zeros((2 * width, 2 * width), F32)
        for start, count in spans(0, early + main, step, early, bulk.shape[0]):
            if start < early:
                block = rows_product(raw.pair(start, count), parts)
                far_ref[pl.ds(start, count), :] = block
            else:
                block = far.get(start, count)
            total = total + cross_term(own.get(start, count), block)
        out_ref[...] = cross_sum(total)

    return call(
        kernel,
        [((early, width), HERE), ((width, width), HERE)],
        [(part, HERE) for part in far_raw] + [(far_main, HERE), (bulk, HERE), (tail, HERE)],
        "main_cross",
        12 * (early + main) * width * width,
    )


def last_cross(far_last, bulk, tail, so_far, step):
    width = bulk.shape[1]
    count = far_last.shape[0] - width
    rows = bulk.shape[0] + tail.shape[0]

    def kernel(far_ref, bulk_ref, tail_ref, total_ref, out_ref):
        own = Rows((bulk_ref, 0, bulk.shape[0], 0), (tail_ref, bulk.shape[0], tail.shape[0], 0))
        far = Rows((far_ref, rows - count, count, 0))
        total = jnp.zeros((2 * width, 2 * width), F32)
        for start, number in spans(rows - count, rows, step, bulk.shape[0]):
            total = total + cross_term(own.get(start, number), far.get(start, number))
        out_ref[...] = total_ref[...] + cross_sum(total)

    return call(
        kernel,
        [((width, width), HERE)],
        [(far_last, HERE), (bulk, HERE), (tail, HERE), (so_far, HERE)],
        "last_cross",
        6 * count * width * width,
    )[0]


def second_rotation(own_gram, far_sent, here, there):
    width = here.shape[1]
    place = far_sent.shape[0] - width

    def kernel(own_gram_ref, far_ref, here_ref, there_ref, out_ref):
        p, n = lax.axis_index("pair"), lax.axis_size("pair")
        odd = lax.rem(p, 2) == 1
        outward = core_of() == 1
        own_upper_out = (p == 0) | (odd & (p != n - 1))
        own_upper = (outward & own_upper_out) | (jnp.logical_not(outward) & jnp.logical_not(odd))
        sign = jnp.where(own_upper, 1.0, -1.0).astype(F32)
        cross = here_ref[...] + there_ref[...].T
        _, rotation = rotation_of(own_gram_ref[...], cross, far_ref[pl.ds(place, width), :], sign)
        keeps_own = (outward & (p == 0)) | (jnp.logical_not(outward) & (p == 1))
        out_ref[...] = jnp.where(keeps_own, rotation[:, :width], rotation[:, width:])

    return call(
        kernel,
        [((2 * width, width), HERE)],
        [(own_gram, HERE), (far_sent, HERE), (here, HERE), (there, HERE)],
        "second_rotation",
        LONG,
    )[0]


def last_product(own, far, turn, done, slot_of, start, count, rows, step, name):
    width = turn.shape[1]
    arrays = [array for array, *_ in own + far]
    pieces = spans(start, start + count, step, *[first for _, first, *_ in own + far])

    def kernel(*refs):
        n = len(arrays)
        turn_ref = refs[n]
        out_ref, stage_ref, sems = refs[-3], refs[-2], refs[-1]
        mine = Rows(*[(ref, *where) for ref, (_, *where) in zip(refs[: len(own)], own)])
        others = Rows(*[(ref, *where) for ref, (_, *where) in zip(refs[len(own) : n], far)])
        parts = right_parts(turn_ref[...])
        slot = slot_of()
        copies = []
        for k, (row, number) in enumerate(pieces):
            block = jnp.concatenate([mine.get(row, number), others.get(row, number)], 1)
            place = pl.ds(row - start, number)
            stage_ref[place, :] = rows_product(block, parts)
            copies.append(
                pltpu.make_async_copy(stage_ref.at[place, :], out_ref.at[slot, pl.ds(row, number), :], sems.at[k])
            )
            copies[-1].start()
        for copy in copies:
            copy.wait()

    args = [(array, HERE) for array in arrays] + [(turn, HERE)] + ([] if done is None else [(done, FAR)])
    return call(
        kernel,
        [((2, rows, width), FAR)],
        args,
        name,
        12 * count * width * width,
        [pltpu.VMEM((count, width), F32), pltpu.SemaphoreType.DMA((len(pieces),))],
        None if done is None else {len(args) - 1: 0},
    )[0]


def first_slot():
    return jnp.where(lax.rem(lax.axis_index("pair"), 2) == core_of(), 1, 0)


def body(pairs_count, rows_count, matrix):
    rows, width = matrix.shape[1:]
    unit = rows // 16
    last, bulk, step = LAST * unit, BULK * unit, STEP * unit
    raw_sizes = [part * unit for part in RAW if part]
    early = sum(raw_sizes)
    flat = [(p, r) for p in range(pairs_count) for r in range(rows_count)]
    ahead = {p: after(p, pairs_count) for p in range(pairs_count)}
    behind = {q: p for p, q in ahead.items()}

    def route(moves):
        return [(p * rows_count + r, q * rows_count + t) for (p, r) in flat for (q, t) in [moves(p, r)]]

    outward = route(lambda p, r: (ahead[p] if r % 2 == 0 else behind[p], r))
    inward = route(lambda p, r: (behind[p] if r % 2 == 0 else ahead[p], r))

    core = [(r, r ^ 1) for r in range(rows_count)]

    def travel(block, moves):
        return lax.ppermute(block, ("pair", "row"), moves)

    def chip_sum(block, flip=0):
        distance = 2
        while distance < rows_count:
            steps = [distance] if 2 * distance >= rows_count else [distance, 2 * distance, 3 * distance]
            hops = [d ^ flip for d in steps] + ([1] if flip else [])
            others = [lax.ppermute(block, "row", [(r, r ^ d) for r in range(rows_count)]) for d in hops]
            block = others.pop() if flip else block
            for other in others:
                block = block + other
            distance *= 1 + len(steps)
            flip = 0
        return block

    def other_sum(block):
        return chip_sum(block, 1)

    *local, keep, give = local_gram(matrix, raw_sizes + [rows - early], step)
    high = local[-1]
    far_raw = [travel(part, outward) for part in local[:-1]]
    mine = chip_sum(keep + lax.ppermute(give, "row", core))
    other = lax.ppermute(mine, "row", core)
    turn_first, turn_second, gram = first_rotation(mine, other)
    turn_first, *far_raw = lax.optimization_barrier((turn_first, *far_raw))

    sent_main, sent_last, second_gram = sent_parts(high, turn_first, turn_second, gram, early, last, step)
    far_main, far_last = travel(sent_main, outward), travel(sent_last, outward)
    turn_second, sent_main = lax.optimization_barrier((turn_second, sent_main))
    second_bulk, second_tail, first_raw = rest_parts(local, turn_first, turn_second, bulk, early, step)

    far_rotated, cross = main_cross(far_raw, far_main, second_bulk, second_tail, step)
    cross, later_bulk, later_tail = lax.optimization_barrier((cross, second_bulk, second_tail))
    far_bulk, far_tail = travel(later_bulk, inward), travel(later_tail, inward)
    cross = last_cross(far_last, second_bulk, second_tail, cross, step)

    total = other_sum(cross)
    there = travel(total, outward)
    here = lax.ppermute(total, "row", core)
    turn_here = second_rotation(second_gram, far_last, here, there)
    turn_there = lax.ppermute(turn_here, "row", core)

    main = rows - early - last
    first = [(first_raw, 0, early, 0), (sent_main, early, main, 2 * width), (sent_last, early + main, last, 0)]
    far_first = [(far_rotated, 0, early, 0), (far_main, early, main, 2 * width), (far_last, early + main, last, 0)]
    second = [(second_bulk, 0, bulk, 0), (second_tail, bulk, rows - bulk, 0)]
    done = last_product(second, far_first, turn_here, None, first_slot, 0, rows, rows, step, "here_product")

    def other_slot():
        return 1 - first_slot()

    done = last_product(first, [(far_bulk, 0, bulk, 0)], turn_there, done, other_slot, 0, bulk, rows, step, "bulk_product")
    return last_product(
        first, [(far_tail, bulk, rows - bulk, 0)], turn_there, done, other_slot, bulk, rows - bulk, rows, step, "tail_product"
    )


def solution(mesh):
    spec = P(None, "row", "pair")
    run = functools.partial(body, mesh.shape["pair"], mesh.shape["row"])
    return jax.shard_map(run, mesh=mesh, in_specs=(spec,), out_specs=spec, check_vma=False)
```

```python
import functools

import jax
import jax.numpy as jnp
from jax import lax
from jax.experimental import pallas as pl
from jax.experimental.pallas import tpu as pltpu
from jax.sharding import PartitionSpec as P


F32 = jnp.float32
BF16 = jnp.bfloat16
SCOPED = 16 * 1024 * 1024
WHOLE = 54 * 1024 * 1024

RAW = 6
SMALL = 4
LAST = 2
BULK = 14
STEP = 2


def after(p, n):
    if p == 0:
        return 1
    if p % 2:
        return n - 2 if p == n - 1 else p + 2
    return p - 2


def halves(x):
    high = x.astype(BF16)
    return high, (x - high.astype(F32)).astype(BF16)


def dot(left, right, contract=((1,), (0,))):
    return lax.dot_general(left, right, (contract, ((), ())), preferred_element_type=F32)


def product(left, right):
    width = right.shape[1]
    twice = jnp.concatenate(halves(right), 1)
    both = dot(jnp.concatenate(halves(left), 1), jnp.concatenate([twice, twice], 0))
    return both[:, :width] + both[:, width:]


def right_parts(right):
    high, low = halves(right)
    return jnp.concatenate([high, low], 1), high


def rows_product(left, parts):
    width = parts[1].shape[1]
    high, low = halves(left)
    both = dot(high, parts[0])
    return both[:, :width] + (both[:, width:] + dot(low, parts[1]))


def eye_of(width):
    rows = lax.broadcasted_iota(jnp.int32, (width, width), 0)
    cols = lax.broadcasted_iota(jnp.int32, (width, width), 1)
    return rows, cols


def polar(cross, sign):
    rows, cols = eye_of(cross.shape[0])
    unit = (rows == cols).astype(F32)
    flipped = cross.T
    s = [product(cross, flipped), product(flipped, cross)]
    s2 = [product(a, a) for a in s]
    e = [0.75 * b - 0.25 * product(b, a) for a, b in zip(s, s2)]
    e2 = [product(a, a) for a in e]
    z = [unit - 0.5 * a + 0.5 * b - 0.25 * product(a, b) for a, b in zip(s, e)]
    f = [0.75 * b + 0.25 * product(b, a) for a, b in zip(e, e2)]
    xz = product(cross, z[1])
    last = [a + 0.5 * product(a, b) for a, b in zip(z, f)]
    wide = sign * (xz + 0.5 * product(xz, f[1]))
    return jnp.concatenate(
        [jnp.concatenate([last[0], wide], 1), jnp.concatenate([-wide.T, last[1]], 1)], 0
    )


def scaled(cross, down, across):
    x = cross * lax.rsqrt(down + 1e-06) * lax.rsqrt(across + 1e-06)
    return x / (1.0 + jnp.sqrt(jnp.sum(x * x)))


def rotation_of(upper, cross, lower, sign):
    width = cross.shape[0]
    rows, cols = eye_of(width)
    same = rows == cols
    zero = jnp.zeros((width, width), F32)
    down = jnp.sum(jnp.where(same, upper, zero), 1, keepdims=True)
    across = jnp.sum(jnp.where(same, lower, zero), 0, keepdims=True)
    first = polar(scaled(cross, down, across), sign)
    gram = jnp.concatenate(
        [jnp.concatenate([upper, cross], 1), jnp.concatenate([cross.T, lower], 1)], 0
    )
    turned = rows_product(gram, right_parts(first))
    second_cross = rows_product(first[:, :width].T, right_parts(turned[:, width:]))
    diagonal = jnp.sum(first * turned, 0, keepdims=True)
    down = jnp.sum(jnp.where(same, diagonal[:, :width], zero), 1, keepdims=True)
    second = polar(scaled(second_cross, down, diagonal[:, width:]), sign)
    return gram, rows_product(first, right_parts(second))


def core_of():
    return lax.rem(lax.axis_index("row"), 2)


def first_is_upper():
    p = lax.axis_index("pair")
    clock_upper = (p == 0) | (lax.rem(p, 2) == 1)
    return (core_of() == 0) == clock_upper


def call(kernel, outs, args, name, flops=0, scratch=(), aliases=None, limit=SCOPED):
    places = [place for _, place in args]
    out_places = [place for _, place in outs]
    return pl.pallas_call(
        kernel,
        in_specs=[pl.BlockSpec(memory_space=place) for place in places],
        out_specs=[pl.BlockSpec(memory_space=place) for place in out_places],
        out_shape=[place(shape, F32) if place == pltpu.VMEM and PIN else jax.ShapeDtypeStruct(shape, F32) for shape, place in outs],
        scratch_shapes=list(scratch),
        input_output_aliases=aliases or {},
        compiler_params=pltpu.CompilerParams(vmem_limit_bytes=limit),
        cost_estimate=pl.CostEstimate(flops=flops if flops == LONG else 0, bytes_accessed=0, transcendentals=0),
        name=name,
    )(*[pltpu.with_memory_space_constraint(array, place) for array, place in args])


PIN = True
LONG = 11500000000
HERE = pltpu.VMEM
FAR = pltpu.HBM


class Rows:
    def __init__(self, *parts):
        self.parts = parts

    @classmethod
    def of(cls, refs, sizes):
        return cls(*[(ref, sum(sizes[:k]), sizes[k], 0) for k, ref in enumerate(refs)])

    def at(self, start, count):
        for ref, first, number, offset in self.parts:
            if first <= start and start + count <= first + number:
                return ref, pl.ds(offset + start - first, count)
        raise ValueError(start)

    def get(self, start, count):
        ref, rows = self.at(start, count)
        return ref[rows, :]

    def pair(self, start, count):
        ref, rows = self.at(start, count)
        return jnp.concatenate([ref[0, rows, :], ref[1, rows, :]], 1)


def spans(start, stop, step, *cuts):
    pieces = []
    while start < stop:
        count = min([step, stop - start] + [cut - start for cut in cuts if cut > start])
        pieces.append((start, count))
        start += count
    return pieces


def local_gram(matrix, sizes, step):
    rows, width = matrix.shape[1:]
    pieces = spans(0, rows, step, *[sum(sizes[:k]) for k in range(len(sizes))])

    def kernel(matrix_ref, *refs):
        part_refs, (keep_ref, give_ref, sems) = refs[: len(sizes)], refs[len(sizes) :]
        local = Rows.of(part_refs, sizes)
        copies = []
        for k, (start, count) in enumerate(pieces):
            ref, place = local.at(start, count)
            copies.append(pltpu.make_async_copy(matrix_ref.at[:, pl.ds(start, count)], ref.at[:, place], sems.at[k]))
            copies[-1].start()
        total = jnp.zeros((2 * width, 4 * width), F32)
        for copy, (start, count) in zip(copies, pieces):
            copy.wait()
            high, low = halves(local.pair(start, count))
            total = total + dot(high, jnp.concatenate([high, low], 1), ((0,), (0,)))
        rest = total[:, 2 * width :]
        total = total[:, : 2 * width] + (rest + rest.T)
        upper, cross, lower = total[:width, :width], total[:width, width:], total[width:, width:]
        r, c = eye_of(width)
        diagonal = jnp.sum(jnp.where(r == c, lower, jnp.zeros_like(lower)), 0, keepdims=True)
        packed = jnp.where(r <= c, upper, lower)
        pad = jnp.broadcast_to(diagonal, (8, width))
        mine = core_of() == 0
        keep_ref[:width] = jnp.where(mine, cross, packed)
        give_ref[:width] = jnp.where(mine, packed, cross)
        keep_ref[width:] = pad
        give_ref[width:] = pad

    outs = [((2, size, width), HERE) for size in sizes] + [((width + 8, width), HERE)] * 2
    return call(
        kernel,
        outs,
        [(matrix, FAR)],
        "gram",
        16 * rows * width * width,
        [pltpu.SemaphoreType.DMA((len(pieces),))],
        limit=WHOLE,
    )


def first_rotation(mine, other):
    width = mine.shape[1]

    def kernel(mine_ref, other_ref, first_ref, second_ref, gram_ref):
        holds_cross = core_of() == 0
        mine, other = mine_ref[...], other_ref[...]
        cross = jnp.where(holds_cross, mine[:width], other[:width])
        packed = jnp.where(holds_cross, other, mine)
        diagonal = packed[width : width + 1]
        packed = packed[:width]
        rows, cols = eye_of(width)
        flipped = packed.T
        upper = jnp.where(rows <= cols, packed, flipped)
        lower = jnp.where(rows > cols, packed, flipped)
        lower = jnp.where(rows == cols, diagonal, lower)
        gram, rotation = rotation_of(upper, cross, lower, 1.0)
        left, right = rotation[:, :width], rotation[:, width:]
        upper_first = first_is_upper()
        first_ref[...] = jnp.where(upper_first, left, right)
        second_ref[...] = jnp.where(upper_first, right, left)
        gram_ref[...] = gram

    half = ((2 * width, width), HERE)
    return call(kernel, [half, half, ((2 * width, 2 * width), HERE)], [(mine, HERE), (other, HERE)], "first_rotation")


def small_part(high, turn, small, step):
    width = turn.shape[1]

    def kernel(high_ref, turn_ref, out_ref):
        local = Rows((high_ref, 0, high.shape[1], 0))
        out_ref[: 2 * width] = turn_ref[...]
        parts = right_parts(turn_ref[...])
        for start, number in spans(0, small, step):
            out_ref[pl.ds(2 * width + start, number), :] = rows_product(local.pair(start, number), parts)

    return call(
        kernel, [((2 * width + small, width), HERE)], [(high, HERE), (turn, HERE)], "small_part", 12 * small * width * width
    )[0]


def sent_parts(high, first, second, gram, small, last, step):
    width = first.shape[1]
    count = high.shape[1]

    def kernel(high_ref, first_ref, second_ref, gram_ref, main_ref, last_ref, second_gram_ref):
        local = Rows((high_ref, 0, count, 0))
        out = Rows((main_ref, small, count - small - last, 0), (last_ref, count - last, last, 0))
        parts = right_parts(first_ref[...])
        for start, number in spans(small, count, step, count - last):
            ref, place = out.at(start, number)
            ref[place, :] = rows_product(local.pair(start, number), parts)
        gram = gram_ref[...]
        for turn_ref, place in ((first_ref, last_ref.at[pl.ds(last, width), :]), (second_ref, second_gram_ref)):
            turn = turn_ref[...]
            place[...] = rows_product(turn.T, right_parts(rows_product(gram, right_parts(turn))))

    return call(
        kernel,
        [((count - small - last, width), HERE), ((last + width, width), HERE), ((width, width), HERE)],
        [(high, HERE), (first, HERE), (second, HERE), (gram, HERE)],
        "sent_parts",
        12 * count * width * width,
    )


def rest_parts(local, first, second, bulk, early, step):
    width = first.shape[1]
    sizes = [part.shape[1] for part in local]
    rows = sum(sizes)

    def kernel(*refs):
        part_refs, (first_ref, second_ref, bulk_ref, tail_ref, raw_ref) = refs[: len(sizes)], refs[len(sizes) :]
        here = Rows.of(part_refs, sizes)
        out = Rows.of((bulk_ref, tail_ref), (bulk, rows - bulk))
        parts = right_parts(second_ref[...])
        for start, count in spans(0, rows, step, bulk, early):
            ref, place = out.at(start, count)
            ref[place, :] = rows_product(here.pair(start, count), parts)
        parts = right_parts(first_ref[...])
        for start, count in spans(0, early, step):
            raw_ref[pl.ds(start, count), :] = rows_product(here.pair(start, count), parts)

    return call(
        kernel,
        [((bulk, width), HERE), ((rows - bulk, width), HERE), ((early, width), HERE)],
        [(part, HERE) for part in local] + [(first, HERE), (second, HERE)],
        "rest_parts",
        12 * (rows + early) * width * width,
    )


def cross_term(own, far):
    return dot(jnp.concatenate(halves(own), 1), jnp.concatenate(halves(far), 1), ((0,), (0,)))


def cross_sum(total):
    width = total.shape[0] // 2
    return (total[:width, :width] + total[:width, width:]) + (total[width:, :width] + total[width:, width:])


def raw_cross(far_raw, far_small, bulk, tail, step):
    width = bulk.shape[1]
    early, small = far_raw.shape[1], far_small.shape[0] - 2 * width

    def kernel(raw_ref, small_ref, bulk_ref, tail_ref, far_ref, out_ref):
        own = Rows.of((bulk_ref, tail_ref), (bulk.shape[0], tail.shape[0]))
        raw = Rows((raw_ref, 0, early, 0))
        far = Rows((small_ref, early, small, 2 * width))
        parts = right_parts(small_ref[: 2 * width])
        total = jnp.zeros((2 * width, 2 * width), F32)
        for start, count in spans(0, early + small, step, early, bulk.shape[0]):
            if start < early:
                block = rows_product(raw.pair(start, count), parts)
                far_ref[pl.ds(start, count), :] = block
            else:
                block = far.get(start, count)
            total = total + cross_term(own.get(start, count), block)
        out_ref[...] = cross_sum(total)

    return call(
        kernel,
        [((early, width), HERE), ((width, width), HERE)],
        [(far_raw, HERE), (far_small, HERE), (bulk, HERE), (tail, HERE)],
        "raw_cross",
        12 * (early + small) * width * width,
    )


def more_cross(far, first_row, count, bulk, tail, so_far, step, name):
    width = bulk.shape[1]

    def kernel(far_ref, bulk_ref, tail_ref, total_ref, out_ref):
        own = Rows.of((bulk_ref, tail_ref), (bulk.shape[0], tail.shape[0]))
        part = Rows((far_ref, first_row, count, 0))
        total = jnp.zeros((2 * width, 2 * width), F32)
        for start, number in spans(first_row, first_row + count, step, bulk.shape[0]):
            total = total + cross_term(own.get(start, number), part.get(start, number))
        out_ref[...] = total_ref[...] + cross_sum(total)

    return call(
        kernel,
        [((width, width), HERE)],
        [(far, HERE), (bulk, HERE), (tail, HERE), (so_far, HERE)],
        name,
        6 * count * width * width,
    )[0]


def second_rotation(own_gram, far_sent, here, there):
    width = here.shape[1]
    place = far_sent.shape[0] - width

    def kernel(own_gram_ref, far_ref, here_ref, there_ref, out_ref):
        p, n = lax.axis_index("pair"), lax.axis_size("pair")
        odd = lax.rem(p, 2) == 1
        outward = core_of() == 1
        own_upper_out = (p == 0) | (odd & (p != n - 1))
        own_upper = (outward & own_upper_out) | (jnp.logical_not(outward) & jnp.logical_not(odd))
        sign = jnp.where(own_upper, 1.0, -1.0).astype(F32)
        cross = here_ref[...] + there_ref[...].T
        _, rotation = rotation_of(own_gram_ref[...], cross, far_ref[pl.ds(place, width), :], sign)
        keeps_own = (outward & (p == 0)) | (jnp.logical_not(outward) & (p == 1))
        out_ref[...] = jnp.where(keeps_own, rotation[:, :width], rotation[:, width:])

    return call(
        kernel,
        [((2 * width, width), HERE)],
        [(own_gram, HERE), (far_sent, HERE), (here, HERE), (there, HERE)],
        "second_rotation",
        LONG,
    )[0]


def last_product(own, far, turn, done, slot_of, start, count, rows, step, name):
    width = turn.shape[1]
    arrays = [array for array, *_ in own + far]
    pieces = spans(start, start + count, step, *[first for _, first, *_ in own + far])

    def kernel(*refs):
        n = len(arrays)
        turn_ref = refs[n]
        out_ref, stage_ref, sems = refs[-3], refs[-2], refs[-1]
        mine = Rows(*[(ref, *where) for ref, (_, *where) in zip(refs[: len(own)], own)])
        others = Rows(*[(ref, *where) for ref, (_, *where) in zip(refs[len(own) : n], far)])
        parts = right_parts(turn_ref[...])
        slot = slot_of()
        copies = []
        for k, (row, number) in enumerate(pieces):
            block = jnp.concatenate([mine.get(row, number), others.get(row, number)], 1)
            place = pl.ds(row - start, number)
            stage_ref[place, :] = rows_product(block, parts)
            copies.append(
                pltpu.make_async_copy(stage_ref.at[place, :], out_ref.at[slot, pl.ds(row, number), :], sems.at[k])
            )
            copies[-1].start()
        for copy in copies:
            copy.wait()

    args = [(array, HERE) for array in arrays] + [(turn, HERE)] + ([] if done is None else [(done, FAR)])
    return call(
        kernel,
        [((2, rows, width), FAR)],
        args,
        name,
        12 * count * width * width,
        [pltpu.VMEM((count, width), F32), pltpu.SemaphoreType.DMA((len(pieces),))],
        None if done is None else {len(args) - 1: 0},
    )[0]


def first_slot():
    return jnp.where(lax.rem(lax.axis_index("pair"), 2) == core_of(), 1, 0)


def body(pairs_count, rows_count, matrix):
    rows, width = matrix.shape[1:]
    unit = rows // 16
    early, small, last, bulk, step = (part * unit for part in (RAW, SMALL, LAST, BULK, STEP))
    main = rows - early - small - last
    flat = [(p, r) for p in range(pairs_count) for r in range(rows_count)]
    ahead = {p: after(p, pairs_count) for p in range(pairs_count)}
    behind = {q: p for p, q in ahead.items()}

    def route(moves):
        return [(p * rows_count + r, q * rows_count + t) for (p, r) in flat for (q, t) in [moves(p, r)]]

    outward = route(lambda p, r: (ahead[p] if r % 2 == 0 else behind[p], r))
    inward = route(lambda p, r: (behind[p] if r % 2 == 0 else ahead[p], r))

    core = [(r, r ^ 1) for r in range(rows_count)]

    def travel(block, moves):
        return lax.ppermute(block, ("pair", "row"), moves)

    def chip_sum(block, flip=0):
        distance = 2
        while distance < rows_count:
            steps = [distance] if 2 * distance >= rows_count else [distance, 2 * distance, 3 * distance]
            hops = [d ^ flip for d in steps] + ([1] if flip else [])
            others = [lax.ppermute(block, "row", [(r, r ^ d) for r in range(rows_count)]) for d in hops]
            block = others.pop() if flip else block
            for other in others:
                block = block + other
            distance *= 1 + len(steps)
            flip = 0
        return block

    def other_sum(block):
        return chip_sum(block, 1)

    low, high, keep, give = local_gram(matrix, [early, rows - early], step)
    far_raw = travel(low, outward)
    mine = chip_sum(keep + lax.ppermute(give, "row", core))
    other = lax.ppermute(mine, "row", core)
    turn_first, turn_second, gram = first_rotation(mine, other)

    sent_small = small_part(high, turn_first, small, step)
    far_small = travel(sent_small, outward)
    turn_main, sent_small, far_raw = lax.optimization_barrier((turn_first, sent_small, far_raw))
    sent_main, sent_last, second_gram = sent_parts(high, turn_main, turn_second, gram, small, last, step)
    far_main, far_last = travel(sent_main, outward), travel(sent_last, outward)
    turn_second, sent_main = lax.optimization_barrier((turn_second, sent_main))
    second_bulk, second_tail, first_raw = rest_parts([low, high], turn_first, turn_second, bulk, early, step)

    far_rotated, cross = raw_cross(far_raw, far_small, second_bulk, second_tail, step)
    far_main, cross = lax.optimization_barrier((far_main, cross))
    cross = more_cross(far_main, early + small, main, second_bulk, second_tail, cross, step, "main_cross")
    cross, later_bulk, later_tail = lax.optimization_barrier((cross, second_bulk, second_tail))
    far_bulk, far_tail = travel(later_bulk, inward), travel(later_tail, inward)
    cross = more_cross(far_last, rows - last, last, second_bulk, second_tail, cross, step, "last_cross")

    total = other_sum(cross)
    there = travel(total, outward)
    here = lax.ppermute(total, "row", core)
    turn_here = second_rotation(second_gram, far_last, here, there)
    turn_there = lax.ppermute(turn_here, "row", core)

    parts = (0, early, 0), (early, small, 2 * width), (early + small, main, 0), (rows - last, last, 0)
    first = [(array, *where) for array, where in zip((first_raw, sent_small, sent_main, sent_last), parts)]
    far_first = [(array, *where) for array, where in zip((far_rotated, far_small, far_main, far_last), parts)]
    second = [(second_bulk, 0, bulk, 0), (second_tail, bulk, rows - bulk, 0)]
    done = last_product(second, far_first, turn_here, None, first_slot, 0, rows, rows, step, "here_product")

    def other_slot():
        return 1 - first_slot()

    done = last_product(first, [(far_bulk, 0, bulk, 0)], turn_there, done, other_slot, 0, bulk, rows, step, "bulk_product")
    return last_product(
        first, [(far_tail, bulk, rows - bulk, 0)], turn_there, done, other_slot, bulk, rows - bulk, rows, step, "tail_product"
    )


def solution(mesh):
    spec = P(None, "row", "pair")
    run = functools.partial(body, mesh.shape["pair"], mesh.shape["row"])
    return jax.shard_map(run, mesh=mesh, in_specs=(spec,), out_specs=spec, check_vma=False)
```

```python
import functools

import jax
import jax.numpy as jnp
from jax import lax
from jax.experimental import pallas as pl
from jax.experimental.pallas import tpu as pltpu
from jax.sharding import PartitionSpec as P


F32 = jnp.float32
BF16 = jnp.bfloat16
SCOPED = 16 * 1024 * 1024
WHOLE = 54 * 1024 * 1024

RAW = 13
SMALL = 8
LAST = 4
BULK = 28
STEP = 4


def after(p, n):
    if p == 0:
        return 1
    if p % 2:
        return n - 2 if p == n - 1 else p + 2
    return p - 2


def halves(x):
    high = x.astype(BF16)
    return high, (x - high.astype(F32)).astype(BF16)


def dot(left, right, contract=((1,), (0,))):
    return lax.dot_general(left, right, (contract, ((), ())), preferred_element_type=F32)


def spread(x):
    twice = jnp.concatenate(halves(x), 1)
    return twice, jnp.concatenate([twice, twice], 0)


def product(left, right):
    width = right.shape[1] // 2
    both = dot(left, right)
    return both[:, :width] + both[:, width:]


def right_parts(right):
    high, low = halves(right)
    return jnp.concatenate([high, low], 1), high


def rows_product(left, parts):
    return halves_product(*halves(left), parts)


def halves_product(high, low, parts):
    width = parts[1].shape[1]
    both = dot(high, parts[0])
    return both[:, :width] + (both[:, width:] + dot(low, parts[1]))


def eye_of(width):
    rows = lax.broadcasted_iota(jnp.int32, (width, width), 0)
    cols = lax.broadcasted_iota(jnp.int32, (width, width), 1)
    return rows, cols


def polar(cross, sign):
    rows, cols = eye_of(cross.shape[0])
    unit = (rows == cols).astype(F32)
    damp = 1.0 / (1.0 + jnp.sqrt(jnp.sum(cross * cross, keepdims=True)))
    left, right = spread(cross)
    left_t, right_t = spread(cross.T)
    s = [product(left, right_t) * (damp * damp), product(left_t, right) * (damp * damp)]
    x = cross * (damp * sign)
    x_left = spread(x)[0]
    s_spread = [spread(a) for a in s]
    s2 = [product(*a) for a in s_spread]
    xs = product(x_left, s_spread[1][1])
    s2_spread = [spread(a) for a in s2]
    s3 = [product(a[0], b[1]) for a, b in zip(s2_spread, s_spread)]
    s4 = [product(*a) for a in s2_spread]
    xs2, xs3 = product(x_left, s2_spread[1][1]), product(spread(xs)[0], s2_spread[1][1])
    e = [0.75 * a - 0.25 * b for a, b in zip(s2, s3)]
    z = [unit - 0.5 * a + 0.5 * b - 0.25 * (0.75 * c - 0.25 * d) for a, b, c, d in zip(s, e, s3, s4)]
    w = [0.75 * unit + 0.25 * a for a in e]
    xw = 0.75 * x + 0.25 * (0.75 * xs2 - 0.25 * xs3)
    e2 = [product(*spread(a)) for a in e]
    zw = [product(spread(a)[0], spread(b)[1]) for a, b in zip(z, w)]
    z_right = spread(z[1])[1]
    xz, xwz = product(x_left, z_right), product(spread(xw)[0], z_right)
    e2_right = [spread(a)[1] for a in e2]
    upper, lower = [a + 0.5 * product(spread(b)[0], c) for a, b, c in zip(z, zw, e2_right)]
    return upper, xz + 0.5 * product(spread(xwz)[0], e2_right[1]), lower


def scaled(cross, down, across):
    return cross * lax.rsqrt(down + 1e-06) * lax.rsqrt(across + 1e-06)


def rotation_of(upper, cross, lower, sign):
    width = cross.shape[0]
    rows, cols = eye_of(width)
    same = rows == cols
    zero = jnp.zeros((width, width), F32)
    down = jnp.sum(jnp.where(same, upper, zero), 1, keepdims=True)
    across = jnp.sum(jnp.where(same, lower, zero), 0, keepdims=True)
    top, wide, bottom = polar(scaled(cross, down, across), sign)
    first = jnp.concatenate([jnp.concatenate([top, wide], 1), jnp.concatenate([-wide.T, bottom], 1)], 0)
    gram = jnp.concatenate(
        [jnp.concatenate([upper, cross], 1), jnp.concatenate([cross.T, lower], 1)], 0
    )
    turned = rows_product(gram, right_parts(first))
    second_cross = rows_product(first[:, :width].T, right_parts(turned[:, width:]))
    diagonal = jnp.sum(first * turned, 0, keepdims=True)
    down = jnp.sum(jnp.where(same, diagonal[:, :width], zero), 1, keepdims=True)
    top, wide, bottom = polar(scaled(second_cross, down, diagonal[:, width:]), sign)
    return gram, first, jnp.concatenate([top, -wide.T], 0), jnp.concatenate([wide, bottom], 0)


def core_of():
    return lax.rem(lax.axis_index("row"), 2)


def first_is_upper():
    p = lax.axis_index("pair")
    clock_upper = (p == 0) | (lax.rem(p, 2) == 1)
    return (core_of() == 0) == clock_upper


def call(kernel, outs, args, name, flops=0, scratch=(), aliases=None, limit=SCOPED):
    places = [place for _, place in args]
    outs = [(*out, F32)[:3] for out in outs]
    out_places = [place for _, place, _ in outs]
    return pl.pallas_call(
        kernel,
        in_specs=[pl.BlockSpec(memory_space=place) for place in places],
        out_specs=[pl.BlockSpec(memory_space=place) for place in out_places],
        out_shape=[
            place(shape, dtype) if place == HERE else jax.ShapeDtypeStruct(shape, dtype) for shape, place, dtype in outs
        ],
        scratch_shapes=list(scratch),
        input_output_aliases=aliases or {},
        compiler_params=pltpu.CompilerParams(vmem_limit_bytes=limit),
        cost_estimate=pl.CostEstimate(flops=flops if flops == LONG else 0, bytes_accessed=0, transcendentals=0),
        name=name,
    )(*[pltpu.with_memory_space_constraint(array, place) for array, place in args])


LONG = 11500000000
HERE = pltpu.VMEM
FAR = pltpu.HBM


class Rows:
    def __init__(self, *parts):
        self.parts = parts

    @classmethod
    def of(cls, refs, sizes):
        return cls(*[(ref, sum(sizes[:k]), sizes[k], 0) for k, ref in enumerate(refs)])

    def at(self, start, count):
        for ref, first, number, offset in self.parts:
            if first <= start and start + count <= first + number:
                return ref, pl.ds(offset + start - first, count)
        raise ValueError(start)

    def get(self, start, count):
        ref, rows = self.at(start, count)
        return ref[rows, :]

    def pair(self, start, count):
        ref, rows = self.at(start, count)
        return jnp.concatenate([ref[0, rows, :], ref[1, rows, :]], 1)


def spans(start, stop, step, *cuts):
    pieces = []
    while start < stop:
        count = min([step, stop - start] + [cut - start for cut in cuts if cut > start])
        pieces.append((start, count))
        start += count
    return pieces


def raw_rows(matrix, count):
    width = matrix.shape[2]

    def kernel(matrix_ref, out_ref, sems):
        copies = [
            pltpu.make_async_copy(matrix_ref.at[k, pl.ds(0, count)], out_ref.at[k], sems.at[k]) for k in range(2)
        ]
        for copy in copies:
            copy.start()
        for copy in copies:
            copy.wait()

    return call(
        kernel,
        [((2, count, width), HERE)],
        [(matrix, FAR)],
        "raw_rows",
        0,
        [pltpu.SemaphoreType.DMA((2,))],
        limit=WHOLE,
    )[0]


def local_gram(matrix, low, step):
    rows, width = matrix.shape[1:]
    early = low.shape[1]

    def kernel(matrix_ref, low_ref, high_ref, keep_ref, give_ref, sems):
        copies = []
        for k, (start, count) in enumerate(spans(early, rows, step)):
            place = pl.ds(start - early, count)
            copies.append(pltpu.make_async_copy(matrix_ref.at[:, pl.ds(start, count)], high_ref.at[:, place], sems.at[k]))
            copies[-1].start()
        local = Rows.of((low_ref, high_ref), (early, rows - early))
        total = jnp.zeros((2 * width, 4 * width), F32)
        for start, count in spans(0, rows, step, early):
            if start >= early:
                copies.pop(0).wait()
            high, low = halves(local.pair(start, count))
            total = total + dot(high, jnp.concatenate([high, low], 1), ((0,), (0,)))
        rest = total[:, 2 * width :]
        total = total[:, : 2 * width] + (rest + rest.T)
        upper, cross, lower = total[:width, :width], total[:width, width:], total[width:, width:]
        r, c = eye_of(width)
        diagonal = jnp.sum(jnp.where(r == c, lower, jnp.zeros_like(lower)), 0, keepdims=True)
        packed = jnp.where(r <= c, upper, lower)
        pad = jnp.broadcast_to(diagonal, (8, width))
        mine = core_of() == 0
        keep_ref[:width] = jnp.where(mine, cross, packed)
        give_ref[:width] = jnp.where(mine, packed, cross)
        keep_ref[width:] = pad
        give_ref[width:] = pad

    outs = [((2, rows - early, width), HERE)] + [((width + 8, width), HERE)] * 2
    return call(
        kernel,
        outs,
        [(matrix, FAR), (low, HERE)],
        "gram",
        16 * rows * width * width,
        [pltpu.SemaphoreType.DMA((len(spans(early, rows, step)),))],
        limit=WHOLE,
    )


def first_rotation(mine, other):
    width = mine.shape[1]

    def kernel(mine_ref, other_ref, first_ref, second_ref, gram_ref):
        holds_cross = core_of() == 0
        mine, other = mine_ref[...], other_ref[...]
        cross = jnp.where(holds_cross, mine[:width], other[:width])
        packed = jnp.where(holds_cross, other, mine)
        diagonal = packed[width : width + 1]
        packed = packed[:width]
        rows, cols = eye_of(width)
        flipped = packed.T
        upper = jnp.where(rows <= cols, packed, flipped)
        lower = jnp.where(rows > cols, packed, flipped)
        lower = jnp.where(rows == cols, diagonal, lower)
        gram, first, left, right = rotation_of(upper, cross, lower, 1.0)
        upper_first = first_is_upper()
        gram_ref[...] = gram
        first_ref[...] = rows_product(first, right_parts(jnp.where(upper_first, left, right)))
        second_ref[...] = rows_product(first, right_parts(jnp.where(upper_first, right, left)))

    half = ((2 * width, width), HERE)
    return call(kernel, [half, half, ((2 * width, 2 * width), HERE)], [(mine, HERE), (other, HERE)], "first_rotation")


def small_part(high, turn, small, step):
    width = turn.shape[1]

    def kernel(high_ref, turn_ref, out_ref):
        local = Rows((high_ref, 0, high.shape[1], 0))
        out_ref[: 2 * width] = turn_ref[...]
        parts = right_parts(turn_ref[...])
        for start, number in spans(0, small, step):
            out_ref[pl.ds(2 * width + start, number), :] = rows_product(local.pair(start, number), parts)

    return call(
        kernel, [((2 * width + small, width), HERE)], [(high, HERE), (turn, HERE)], "small_part", 12 * small * width * width
    )[0]


def sent_parts(high, first, second, gram, small, last, step):
    width = first.shape[1]
    count = high.shape[1]

    def kernel(high_ref, first_ref, second_ref, gram_ref, main_ref, last_ref, second_gram_ref):
        local = Rows((high_ref, 0, count, 0))
        out = Rows((main_ref, small, count - small - last, 0), (last_ref, count - last, last, 0))
        parts = right_parts(first_ref[...])
        for start, number in spans(small, count, step, count - last):
            ref, place = out.at(start, number)
            ref[place, :] = rows_product(local.pair(start, number), parts)
        gram = gram_ref[...]
        for turn_ref, place in ((first_ref, last_ref.at[pl.ds(last, width), :]), (second_ref, second_gram_ref)):
            turn = turn_ref[...]
            place[...] = rows_product(turn.T, right_parts(rows_product(gram, right_parts(turn))))

    return call(
        kernel,
        [((count - small - last, width), HERE), ((last + width, width), HERE), ((width, width), HERE)],
        [(high, HERE), (first, HERE), (second, HERE), (gram, HERE)],
        "sent_parts",
        12 * count * width * width,
    )


def rest_parts(low, high, first, second, sent, bulk, step):
    width = first.shape[1]
    sizes = low.shape[1], high.shape[1]
    early, rows = sizes[0], sum(sizes)
    arrays = [array for array, *_ in sent]

    def kernel(low_ref, high_ref, first_ref, second_ref, *refs):
        bulk_ref, tail_ref, high_half_ref, low_half_ref = refs[len(sent) :]
        here = Rows.of((low_ref, high_ref), sizes)
        there = Rows(*[(ref, *where) for ref, (_, *where) in zip(refs, sent)])
        out = Rows.of((bulk_ref, tail_ref), (bulk, rows - bulk))
        parts = right_parts(second_ref[...])
        for start, count in spans(0, rows, step, bulk, early):
            ref, place = out.at(start, count)
            ref[place, :] = rows_product(here.pair(start, count), parts)
        parts = right_parts(first_ref[...])
        for start, count in spans(0, rows, step, early, *[first for _, first, *_ in sent]):
            block = rows_product(here.pair(start, count), parts) if start < early else there.get(start, count)
            place = pl.ds(start, count)
            high_half_ref[place, :], low_half_ref[place, :] = halves(block)

    return call(
        kernel,
        [((bulk, width), HERE), ((rows - bulk, width), HERE)] + [((rows, width), HERE, BF16)] * 2,
        [(part, HERE) for part in (low, high, first, second, *arrays)],
        "rest_parts",
        12 * (rows + early) * width * width,
    )


def cross_term(high, low):
    width = high.shape[1] // 2
    own = jnp.concatenate([high[:, :width], low[:, :width]], 1)
    far = jnp.concatenate([high[:, width:], low[:, width:]], 1)
    return dot(own, far, ((0,), (0,)))


def cross_sum(total):
    width = total.shape[0] // 2
    return (total[:width, :width] + total[:width, width:]) + (total[width:, :width] + total[width:, width:])


def raw_cross(far_raw, far_small, bulk, tail, step):
    width = bulk.shape[1]
    early, small = far_raw.shape[1], far_small.shape[0] - 2 * width

    def kernel(raw_ref, small_ref, bulk_ref, tail_ref, high_ref, low_ref, out_ref):
        own = Rows.of((bulk_ref, tail_ref), (bulk.shape[0], tail.shape[0]))
        raw = Rows((raw_ref, 0, early, 0))
        far = Rows((small_ref, early, small, 2 * width))
        parts = right_parts(small_ref[: 2 * width])
        total = jnp.zeros((2 * width, 2 * width), F32)
        for start, count in spans(0, early + small, step, early, bulk.shape[0]):
            block = rows_product(raw.pair(start, count), parts) if start < early else far.get(start, count)
            high, low = halves(jnp.concatenate([own.get(start, count), block], 1))
            place = pl.ds(start, count)
            high_ref[place, :], low_ref[place, :] = high, low
            total = total + cross_term(high, low)
        out_ref[...] = cross_sum(total)

    return call(
        kernel,
        [((early + small, 2 * width), HERE, BF16)] * 2 + [((width, width), HERE)],
        [(far_raw, HERE), (far_small, HERE), (bulk, HERE), (tail, HERE)],
        "raw_cross",
        12 * (early + small) * width * width,
    )


def more_cross(far, first_row, count, bulk, tail, so_far, step, name):
    width = bulk.shape[1]

    def kernel(far_ref, bulk_ref, tail_ref, total_ref, high_ref, low_ref, out_ref):
        own = Rows.of((bulk_ref, tail_ref), (bulk.shape[0], tail.shape[0]))
        part = Rows((far_ref, first_row, count, 0))
        total = jnp.zeros((2 * width, 2 * width), F32)
        for start, number in spans(first_row, first_row + count, step, bulk.shape[0]):
            high, low = halves(jnp.concatenate([own.get(start, number), part.get(start, number)], 1))
            place = pl.ds(start - first_row, number)
            high_ref[place, :], low_ref[place, :] = high, low
            total = total + cross_term(high, low)
        out_ref[...] = total_ref[...] + cross_sum(total)

    return call(
        kernel,
        [((count, 2 * width), HERE, BF16)] * 2 + [((width, width), HERE)],
        [(far, HERE), (bulk, HERE), (tail, HERE), (so_far, HERE)],
        name,
        6 * count * width * width,
    )


def second_rotation(own_gram, far_sent, here, there):
    width = here.shape[1]
    place = far_sent.shape[0] - width

    def kernel(own_gram_ref, far_ref, here_ref, there_ref, out_ref):
        p, n = lax.axis_index("pair"), lax.axis_size("pair")
        odd = lax.rem(p, 2) == 1
        outward = core_of() == 1
        own_upper_out = (p == 0) | (odd & (p != n - 1))
        own_upper = (outward & own_upper_out) | (jnp.logical_not(outward) & jnp.logical_not(odd))
        sign = jnp.where(own_upper, 1.0, -1.0).astype(F32)
        cross = here_ref[...] + there_ref[...].T
        _, first, left, right = rotation_of(own_gram_ref[...], cross, far_ref[pl.ds(place, width), :], sign)
        keeps_own = (outward & (p == 0)) | (jnp.logical_not(outward) & (p == 1))
        out_ref[...] = rows_product(first, right_parts(jnp.where(keeps_own, left, right)))

    return call(
        kernel,
        [((2 * width, width), HERE)],
        [(own_gram, HERE), (far_sent, HERE), (here, HERE), (there, HERE)],
        "second_rotation",
        LONG,
    )[0]


def last_product(load, arrays, turn, done, slot_of, start, count, rows, step, cuts, name):
    width = turn.shape[1]
    pieces = spans(start, start + count, step, *cuts)

    def kernel(*refs):
        turn_ref = refs[len(arrays)]
        out_ref, stage_ref, sems = refs[-3:]
        parts = right_parts(turn_ref[...])
        slot = slot_of()
        copies = []
        for k, (row, number) in enumerate(pieces):
            place = pl.ds(row - start, number)
            stage_ref[place, :] = halves_product(*load(refs, row, number), parts)
            copies.append(
                pltpu.make_async_copy(stage_ref.at[place, :], out_ref.at[slot, pl.ds(row, number), :], sems.at[k])
            )
            copies[-1].start()
        for copy in copies:
            copy.wait()

    args = [(array, HERE) for array in (*arrays, turn)] + ([] if done is None else [(done, FAR)])
    return call(
        kernel,
        [((2, rows, width), FAR)],
        args,
        name,
        12 * count * width * width,
        [pltpu.VMEM((count, width), F32), pltpu.SemaphoreType.DMA((len(pieces),))],
        None if done is None else {len(args) - 1: 0},
    )[0]


def first_slot():
    return jnp.where(lax.rem(lax.axis_index("pair"), 2) == core_of(), 1, 0)


def body(pairs_count, rows_count, matrix):
    rows, width = matrix.shape[1:]
    unit = rows // 32
    early, small, last, bulk, step = (part * unit for part in (RAW, SMALL, LAST, BULK, STEP))
    main = rows - early - small - last
    flat = [(p, r) for p in range(pairs_count) for r in range(rows_count)]
    ahead = {p: after(p, pairs_count) for p in range(pairs_count)}
    behind = {q: p for p, q in ahead.items()}

    def route(moves):
        return [(p * rows_count + r, q * rows_count + t) for (p, r) in flat for (q, t) in [moves(p, r)]]

    outward = route(lambda p, r: (ahead[p] if r % 2 == 0 else behind[p], r))
    inward = route(lambda p, r: (behind[p] if r % 2 == 0 else ahead[p], r))

    core = [(r, r ^ 1) for r in range(rows_count)]

    def travel(block, moves):
        return lax.ppermute(block, ("pair", "row"), moves)

    def chip_sum(block, radix, flip=0):
        distance = 2
        while distance < rows_count:
            steps = [distance] if radix == 2 or 2 * distance >= rows_count else [distance, 2 * distance, 3 * distance]
            hops = [d ^ flip for d in steps] + ([1] if flip else [])
            others = [lax.ppermute(block, "row", [(r, r ^ d) for r in range(rows_count)]) for d in hops]
            block = others.pop() if flip else block
            for other in others:
                block = block + other
            distance *= 1 + len(steps)
            flip = 0
        return block

    def other_sum(block):
        return chip_sum(block, 4, 1)

    low = raw_rows(matrix, early)
    far_raw = travel(low, outward)
    high, keep, give = local_gram(matrix, low, step)
    mine = chip_sum(keep + lax.ppermute(give, "row", core), 4)
    other = lax.ppermute(mine, "row", core)
    turn_first, turn_second, gram = first_rotation(mine, other)

    sent_small = small_part(high, turn_first, small, step)
    far_small = travel(sent_small, outward)
    turn_main, sent_small, far_raw = lax.optimization_barrier((turn_first, sent_small, far_raw))
    sent_main, sent_last, second_gram = sent_parts(high, turn_main, turn_second, gram, small, last, step)
    far_main, far_last = travel(sent_main, outward), travel(sent_last, outward)
    turn_second, sent_main = lax.optimization_barrier((turn_second, sent_main))
    sent = [(sent_small, early, small, 2 * width), (sent_main, early + small, main, 0), (sent_last, rows - last, last, 0)]
    second_bulk, second_tail, *first_halves = rest_parts(low, high, turn_first, turn_second, sent, bulk, step)

    *raw_halves, cross = raw_cross(far_raw, far_small, second_bulk, second_tail, step)
    far_main, cross = lax.optimization_barrier((far_main, cross))
    *main_halves, cross = more_cross(
        far_main, early + small, main, second_bulk, second_tail, cross, step, "main_cross"
    )
    cross, later_bulk, later_tail = lax.optimization_barrier((cross, second_bulk, second_tail))
    far_bulk, far_tail = travel(later_bulk, inward), travel(later_tail, inward)
    *last_halves, cross = more_cross(far_last, rows - last, last, second_bulk, second_tail, cross, step, "last_cross")

    total = other_sum(cross)
    there = travel(total, outward)
    here = lax.ppermute(total, "row", core)
    turn_here = second_rotation(second_gram, far_last, here, there)
    turn_there = lax.ppermute(turn_here, "row", core)

    sizes = early + small, main, last

    def load_here(refs, row, number):
        return [Rows.of(refs[k : 6 : 2], sizes).get(row, number) for k in (0, 1)]

    def other_slot():
        return 1 - first_slot()

    def load_there(refs, row, number):
        place = pl.ds(row, number)
        far = halves(Rows.of(refs[2:4], (bulk, rows - bulk)).get(row, number))
        return [jnp.concatenate([ref[place, :], half], 1) for ref, half in zip(refs, far)]

    cuts = early + small, rows - last
    done = last_product(
        load_here, raw_halves + main_halves + last_halves, turn_here, None, first_slot, 0, rows, rows, step, cuts, "here_product"
    )

    def load_tail(refs, row, number):
        place = pl.ds(row, number)
        far = halves(Rows((refs[2], bulk, rows - bulk, 0)).get(row, number))
        return [jnp.concatenate([ref[place, :], half], 1) for ref, half in zip(refs, far)]

    done = last_product(
        load_there, [*first_halves, far_bulk, far_bulk], turn_there, done, other_slot, 0, bulk, rows, step, [], "bulk_product"
    )
    return last_product(
        load_tail, [*first_halves, far_tail], turn_there, done, other_slot, bulk, rows - bulk, rows, step, [], "tail_product"
    )


def solution(mesh):
    spec = P(None, "row", "pair")
    run = functools.partial(body, mesh.shape["pair"], mesh.shape["row"])
    return jax.shard_map(run, mesh=mesh, in_specs=(spec,), out_specs=spec, check_vma=False)
```

```python
import functools

import jax
import jax.numpy as jnp
from jax import lax
from jax.experimental import pallas as pl
from jax.experimental.pallas import tpu as pltpu
from jax.sharding import PartitionSpec as P


F32 = jnp.float32
BF16 = jnp.bfloat16
SCOPED = 16 * 1024 * 1024
WHOLE = 54 * 1024 * 1024

RAW = 14
SMALL = 7
LAST = 4
BULK = 28
STEP = 4
SHARE = 3


def after(p, n):
    if p == 0:
        return 1
    if p % 2:
        return n - 2 if p == n - 1 else p + 2
    return p - 2


def halves(x):
    high = x.astype(BF16)
    return high, (x - high.astype(F32)).astype(BF16)


def dot(left, right, contract=((1,), (0,))):
    return lax.dot_general(left, right, (contract, ((), ())), preferred_element_type=F32)


def spread(x):
    twice = jnp.concatenate(halves(x), 1)
    return twice, jnp.concatenate([twice, twice], 0)


def product(left, right):
    width = right.shape[1] // 2
    both = dot(left, right)
    return both[:, :width] + both[:, width:]


def right_parts(right):
    high, low = halves(right)
    return jnp.concatenate([high, low], 1), high


def rows_product(left, parts):
    return halves_product(*halves(left), parts)


def halves_product(high, low, parts):
    width = parts[1].shape[1]
    both = dot(high, parts[0])
    return both[:, :width] + (both[:, width:] + dot(low, parts[1]))


def eye_of(width):
    rows = lax.broadcasted_iota(jnp.int32, (width, width), 0)
    cols = lax.broadcasted_iota(jnp.int32, (width, width), 1)
    return rows, cols


def polar(cross, sign):
    rows, cols = eye_of(cross.shape[0])
    unit = (rows == cols).astype(F32)
    damp = 1.0 / (1.0 + jnp.sqrt(jnp.sum(cross * cross, keepdims=True)))
    left, right = spread(cross)
    left_t, right_t = spread(cross.T)
    s = [product(left, right_t) * (damp * damp), product(left_t, right) * (damp * damp)]
    x = cross * (damp * sign)
    x_left = spread(x)[0]
    s_spread = [spread(a) for a in s]
    s2 = [product(*a) for a in s_spread]
    xs = product(x_left, s_spread[1][1])
    s2_spread = [spread(a) for a in s2]
    s3 = [product(a[0], b[1]) for a, b in zip(s2_spread, s_spread)]
    s4 = [product(*a) for a in s2_spread]
    xs2, xs3 = product(x_left, s2_spread[1][1]), product(spread(xs)[0], s2_spread[1][1])
    e = [0.75 * a - 0.25 * b for a, b in zip(s2, s3)]
    z = [unit - 0.5 * a + 0.5 * b - 0.25 * (0.75 * c - 0.25 * d) for a, b, c, d in zip(s, e, s3, s4)]
    w = [0.75 * unit + 0.25 * a for a in e]
    xw = 0.75 * x + 0.25 * (0.75 * xs2 - 0.25 * xs3)
    e2 = [product(*spread(a)) for a in e]
    zw = [product(spread(a)[0], spread(b)[1]) for a, b in zip(z, w)]
    z_right = spread(z[1])[1]
    xz, xwz = product(x_left, z_right), product(spread(xw)[0], z_right)
    e2_right = [spread(a)[1] for a in e2]
    upper, lower = [a + 0.5 * product(spread(b)[0], c) for a, b, c in zip(z, zw, e2_right)]
    return upper, xz + 0.5 * product(spread(xwz)[0], e2_right[1]), lower


def scaled(cross, down, across):
    return cross * lax.rsqrt(down + 1e-06) * lax.rsqrt(across + 1e-06)


def rotation_of(upper, cross, lower, sign):
    width = cross.shape[0]
    rows, cols = eye_of(width)
    same = rows == cols
    zero = jnp.zeros((width, width), F32)
    down = jnp.sum(jnp.where(same, upper, zero), 1, keepdims=True)
    across = jnp.sum(jnp.where(same, lower, zero), 0, keepdims=True)
    top, wide, bottom = polar(scaled(cross, down, across), sign)
    first = jnp.concatenate([jnp.concatenate([top, wide], 1), jnp.concatenate([-wide.T, bottom], 1)], 0)
    gram = jnp.concatenate(
        [jnp.concatenate([upper, cross], 1), jnp.concatenate([cross.T, lower], 1)], 0
    )
    turned = rows_product(gram, right_parts(first))
    second_cross = rows_product(first[:, :width].T, right_parts(turned[:, width:]))
    diagonal = jnp.sum(first * turned, 0, keepdims=True)
    down = jnp.sum(jnp.where(same, diagonal[:, :width], zero), 1, keepdims=True)
    top, wide, bottom = polar(scaled(second_cross, down, diagonal[:, width:]), sign)
    return gram, first, jnp.concatenate([top, -wide.T], 0), jnp.concatenate([wide, bottom], 0)


def core_of():
    return lax.rem(lax.axis_index("row"), 2)


def first_is_upper():
    p = lax.axis_index("pair")
    clock_upper = (p == 0) | (lax.rem(p, 2) == 1)
    return (core_of() == 0) == clock_upper


def call(kernel, outs, args, name, flops=0, scratch=(), aliases=None, limit=SCOPED):
    places = [place for _, place in args]
    outs = [(*out, F32)[:3] for out in outs]
    out_places = [place for _, place, _ in outs]
    return pl.pallas_call(
        kernel,
        in_specs=[pl.BlockSpec(memory_space=place) for place in places],
        out_specs=[pl.BlockSpec(memory_space=place) for place in out_places],
        out_shape=[
            place(shape, dtype) if place == HERE else jax.ShapeDtypeStruct(shape, dtype) for shape, place, dtype in outs
        ],
        scratch_shapes=list(scratch),
        input_output_aliases=aliases or {},
        compiler_params=pltpu.CompilerParams(vmem_limit_bytes=limit),
        cost_estimate=pl.CostEstimate(flops=flops if flops == LONG else 0, bytes_accessed=0, transcendentals=0),
        name=name,
    )(*[pltpu.with_memory_space_constraint(array, place) for array, place in args])


LONG = 11500000000
HERE = pltpu.VMEM
FAR = pltpu.HBM


class Rows:
    def __init__(self, *parts):
        self.parts = parts

    @classmethod
    def of(cls, refs, sizes):
        return cls(*[(ref, sum(sizes[:k]), sizes[k], 0) for k, ref in enumerate(refs)])

    def at(self, start, count):
        for ref, first, number, offset in self.parts:
            if first <= start and start + count <= first + number:
                return ref, pl.ds(offset + start - first, count)
        raise ValueError(start)

    def get(self, start, count):
        ref, rows = self.at(start, count)
        return ref[rows, :]

    def pair(self, start, count):
        ref, rows = self.at(start, count)
        return jnp.concatenate([ref[0, rows, :], ref[1, rows, :]], 1)


def spans(start, stop, step, *cuts):
    pieces = []
    while start < stop:
        count = min([step, stop - start] + [cut - start for cut in cuts if cut > start])
        pieces.append((start, count))
        start += count
    return pieces


def raw_rows(matrix, count):
    width = matrix.shape[2]

    def kernel(matrix_ref, out_ref, sems):
        copies = [
            pltpu.make_async_copy(matrix_ref.at[k, pl.ds(0, count)], out_ref.at[k], sems.at[k]) for k in range(2)
        ]
        for copy in copies:
            copy.start()
        for copy in copies:
            copy.wait()

    return call(
        kernel,
        [((2, count, width), HERE)],
        [(matrix, FAR)],
        "raw_rows",
        0,
        [pltpu.SemaphoreType.DMA((2,))],
        limit=WHOLE,
    )[0]


def local_gram(matrix, low, step):
    rows, width = matrix.shape[1:]
    early = low.shape[1]

    def kernel(matrix_ref, low_ref, high_ref, keep_ref, give_ref, sems):
        copies = []
        for k, (start, count) in enumerate(spans(early, rows, step)):
            place = pl.ds(start - early, count)
            copies.append(pltpu.make_async_copy(matrix_ref.at[:, pl.ds(start, count)], high_ref.at[:, place], sems.at[k]))
            copies[-1].start()
        local = Rows.of((low_ref, high_ref), (early, rows - early))
        total = jnp.zeros((2 * width, 4 * width), F32)
        for start, count in spans(0, rows, step, early):
            if start >= early:
                copies.pop(0).wait()
            high, low = halves(local.pair(start, count))
            total = total + dot(high, jnp.concatenate([high, low], 1), ((0,), (0,)))
        rest = total[:, 2 * width :]
        total = total[:, : 2 * width] + (rest + rest.T)
        upper, cross, lower = total[:width, :width], total[:width, width:], total[width:, width:]
        r, c = eye_of(width)
        diagonal = jnp.sum(jnp.where(r == c, lower, jnp.zeros_like(lower)), 0, keepdims=True)
        packed = jnp.where(r <= c, upper, lower)
        pad = jnp.broadcast_to(diagonal, (8, width))
        mine = core_of() == 0
        keep_ref[:width] = jnp.where(mine, cross, packed)
        give_ref[:width] = jnp.where(mine, packed, cross)
        keep_ref[width:] = pad
        give_ref[width:] = pad

    outs = [((2, rows - early, width), HERE)] + [((width + 8, width), HERE)] * 2
    return call(
        kernel,
        outs,
        [(matrix, FAR), (low, HERE)],
        "gram",
        16 * rows * width * width,
        [pltpu.SemaphoreType.DMA((len(spans(early, rows, step)),))],
        limit=WHOLE,
    )


def first_rotation(mine, other):
    width = mine.shape[1]

    def kernel(mine_ref, other_ref, first_ref, second_ref, gram_ref):
        holds_cross = core_of() == 0
        mine, other = mine_ref[...], other_ref[...]
        cross = jnp.where(holds_cross, mine[:width], other[:width])
        packed = jnp.where(holds_cross, other, mine)
        diagonal = packed[width : width + 1]
        packed = packed[:width]
        rows, cols = eye_of(width)
        flipped = packed.T
        upper = jnp.where(rows <= cols, packed, flipped)
        lower = jnp.where(rows > cols, packed, flipped)
        lower = jnp.where(rows == cols, diagonal, lower)
        gram, first, left, right = rotation_of(upper, cross, lower, 1.0)
        upper_first = first_is_upper()
        gram_ref[...] = gram
        first_ref[...] = rows_product(first, right_parts(jnp.where(upper_first, left, right)))
        second_ref[...] = rows_product(first, right_parts(jnp.where(upper_first, right, left)))

    half = ((2 * width, width), HERE)
    return call(kernel, [half, half, ((2 * width, 2 * width), HERE)], [(mine, HERE), (other, HERE)], "first_rotation")


def share_of():
    return lax.rem(lax.div(lax.axis_index("row"), 2), 2)


def rotated_gram(gram, turn):
    return rows_product(turn.T, right_parts(rows_product(gram, right_parts(turn))))


def small_part(high, turn, gram, small, step):
    width = turn.shape[1]
    turn_share, gram_share = width, width // 2

    def kernel(high_ref, turn_ref, gram_ref, out_ref, square_ref):
        place = share_of()
        local = Rows((high_ref, 0, high.shape[1], 0))
        parts = right_parts(turn_ref[...])
        for start, number in spans(0, small, step):
            out_ref[pl.ds(SHARE * width // 2 + start, number), :] = rows_product(local.pair(start, number), parts)
        square_ref[...] = rotated_gram(gram_ref[...], turn_ref[...])
        out_ref[:turn_share] = turn_ref[pl.ds(pl.multiple_of(place * turn_share, turn_share), turn_share), :]
        out_ref[turn_share : turn_share + gram_share] = square_ref[
            pl.ds(pl.multiple_of(place * gram_share, gram_share), gram_share), :
        ]

    return call(
        kernel,
        [((SHARE * width // 2 + small, width), HERE)],
        [(high, HERE), (turn, HERE), (gram, HERE)],
        "small_part",
        12 * small * width * width,
        [pltpu.VMEM((width, width), F32)],
    )[0]


def sent_parts(high, first, second, gram, small, last, step):
    width = first.shape[1]
    count = high.shape[1]

    def kernel(high_ref, first_ref, second_ref, gram_ref, main_ref, last_ref, second_gram_ref):
        local = Rows((high_ref, 0, count, 0))
        out = Rows((main_ref, small, count - small - last, 0), (last_ref, count - last, last, 0))
        parts = right_parts(first_ref[...])
        for start, number in spans(small, count, step, count - last):
            ref, place = out.at(start, number)
            ref[place, :] = rows_product(local.pair(start, number), parts)
        second_gram_ref[...] = rotated_gram(gram_ref[...], second_ref[...])

    return call(
        kernel,
        [((count - small - last, width), HERE), ((last, width), HERE), ((width, width), HERE)],
        [(high, HERE), (first, HERE), (second, HERE), (gram, HERE)],
        "sent_parts",
        12 * count * width * width,
    )


def rest_parts(low, high, first, second, sent, bulk, step):
    width = first.shape[1]
    sizes = low.shape[1], high.shape[1]
    early, rows = sizes[0], sum(sizes)
    arrays = [array for array, *_ in sent]

    def kernel(low_ref, high_ref, first_ref, second_ref, *refs):
        bulk_ref, tail_ref, high_half_ref, low_half_ref = refs[len(sent) :]
        here = Rows.of((low_ref, high_ref), sizes)
        there = Rows(*[(ref, *where) for ref, (_, *where) in zip(refs, sent)])
        out = Rows.of((bulk_ref, tail_ref), (bulk, rows - bulk))
        parts = right_parts(second_ref[...])
        for start, count in spans(0, rows, step, bulk, early):
            ref, place = out.at(start, count)
            ref[place, :] = rows_product(here.pair(start, count), parts)
        parts = right_parts(first_ref[...])
        for start, count in spans(0, rows, step, early, *[first for _, first, *_ in sent]):
            block = rows_product(here.pair(start, count), parts) if start < early else there.get(start, count)
            place = pl.ds(start, count)
            high_half_ref[place, :], low_half_ref[place, :] = halves(block)

    return call(
        kernel,
        [((bulk, width), HERE), ((rows - bulk, width), HERE)] + [((rows, width), HERE, BF16)] * 2,
        [(part, HERE) for part in (low, high, first, second, *arrays)],
        "rest_parts",
        12 * (rows + early) * width * width,
    )


def cross_term(high, low):
    width = high.shape[1] // 2
    own = jnp.concatenate([high[:, :width], low[:, :width]], 1)
    far = jnp.concatenate([high[:, width:], low[:, width:]], 1)
    return dot(own, far, ((0,), (0,)))


def cross_sum(total):
    width = total.shape[0] // 2
    return (total[:width, :width] + total[:width, width:]) + (total[width:, :width] + total[width:, width:])


def raw_cross(far_raw, far_small, share, bulk, tail, step):
    width = bulk.shape[1]
    offset = SHARE * width // 2
    early, small = far_raw.shape[1], far_small.shape[0] - offset
    turn_share, gram_share = width, width // 2

    def kernel(
        raw_ref, small_ref, share_ref, bulk_ref, tail_ref, high_ref, low_ref, gram_ref, out_ref, turn_ref
    ):
        for place, ref in ((share_of(), small_ref), (1 - share_of(), share_ref)):
            turn_ref[pl.ds(pl.multiple_of(place * turn_share, turn_share), turn_share), :] = ref[:turn_share]
            gram_ref[pl.ds(pl.multiple_of(place * gram_share, gram_share), gram_share), :] = ref[
                turn_share : turn_share + gram_share
            ]
        own = Rows.of((bulk_ref, tail_ref), (bulk.shape[0], tail.shape[0]))
        raw = Rows((raw_ref, 0, early, 0))
        far = Rows((small_ref, early, small, offset))
        parts = right_parts(turn_ref[...])
        total = jnp.zeros((2 * width, 2 * width), F32)
        for start, count in spans(0, early + small, step, early, bulk.shape[0]):
            block = rows_product(raw.pair(start, count), parts) if start < early else far.get(start, count)
            high, low = halves(jnp.concatenate([own.get(start, count), block], 1))
            place = pl.ds(start, count)
            high_ref[place, :], low_ref[place, :] = high, low
            total = total + cross_term(high, low)
        out_ref[...] = cross_sum(total)

    return call(
        kernel,
        [((early + small, 2 * width), HERE, BF16)] * 2 + [((width, width), HERE)] * 2,
        [(part, HERE) for part in (far_raw, far_small, share, bulk, tail)],
        "raw_cross",
        12 * (early + small) * width * width,
        [pltpu.VMEM((2 * width, width), F32)],
    )


def more_cross(far, first_row, count, bulk, tail, so_far, step, name):
    width = bulk.shape[1]

    def kernel(far_ref, bulk_ref, tail_ref, total_ref, high_ref, low_ref, out_ref):
        own = Rows.of((bulk_ref, tail_ref), (bulk.shape[0], tail.shape[0]))
        part = Rows((far_ref, first_row, count, 0))
        total = jnp.zeros((2 * width, 2 * width), F32)
        for start, number in spans(first_row, first_row + count, step, bulk.shape[0]):
            high, low = halves(jnp.concatenate([own.get(start, number), part.get(start, number)], 1))
            place = pl.ds(start - first_row, number)
            high_ref[place, :], low_ref[place, :] = high, low
            total = total + cross_term(high, low)
        out_ref[...] = total_ref[...] + cross_sum(total)

    return call(
        kernel,
        [((count, 2 * width), HERE, BF16)] * 2 + [((width, width), HERE)],
        [(far, HERE), (bulk, HERE), (tail, HERE), (so_far, HERE)],
        name,
        6 * count * width * width,
    )


def second_rotation(own_gram, far_gram, here, there):
    width = here.shape[1]

    def kernel(own_gram_ref, far_ref, here_ref, there_ref, out_ref):
        p, n = lax.axis_index("pair"), lax.axis_size("pair")
        odd = lax.rem(p, 2) == 1
        outward = core_of() == 1
        own_upper_out = (p == 0) | (odd & (p != n - 1))
        own_upper = (outward & own_upper_out) | (jnp.logical_not(outward) & jnp.logical_not(odd))
        sign = jnp.where(own_upper, 1.0, -1.0).astype(F32)
        cross = here_ref[...] + there_ref[...].T
        _, first, left, right = rotation_of(own_gram_ref[...], cross, far_ref[...], sign)
        keeps_own = (outward & (p == 0)) | (jnp.logical_not(outward) & (p == 1))
        out_ref[...] = rows_product(first, right_parts(jnp.where(keeps_own, left, right)))

    return call(
        kernel,
        [((2 * width, width), HERE)],
        [(own_gram, HERE), (far_gram, HERE), (here, HERE), (there, HERE)],
        "second_rotation",
        LONG,
    )[0]


def last_product(load, arrays, turn, done, slot_of, start, count, rows, step, cuts, name):
    width = turn.shape[1]
    pieces = spans(start, start + count, step, *cuts)

    def kernel(*refs):
        turn_ref = refs[len(arrays)]
        out_ref, stage_ref, sems = refs[-3:]
        parts = right_parts(turn_ref[...])
        slot = slot_of()
        copies = []
        for k, (row, number) in enumerate(pieces):
            place = pl.ds(row - start, number)
            stage_ref[place, :] = halves_product(*load(refs, row, number), parts)
            copies.append(
                pltpu.make_async_copy(stage_ref.at[place, :], out_ref.at[slot, pl.ds(row, number), :], sems.at[k])
            )
            copies[-1].start()
        for copy in copies:
            copy.wait()

    args = [(array, HERE) for array in (*arrays, turn)] + ([] if done is None else [(done, FAR)])
    return call(
        kernel,
        [((2, rows, width), FAR)],
        args,
        name,
        12 * count * width * width,
        [pltpu.VMEM((count, width), F32), pltpu.SemaphoreType.DMA((len(pieces),))],
        None if done is None else {len(args) - 1: 0},
    )[0]


def first_slot():
    return jnp.where(lax.rem(lax.axis_index("pair"), 2) == core_of(), 1, 0)


def body(pairs_count, rows_count, matrix):
    rows, width = matrix.shape[1:]
    unit = rows // 32
    early, small, last, bulk, step = (part * unit for part in (RAW, SMALL, LAST, BULK, STEP))
    main = rows - early - small - last
    offset = SHARE * width // 2
    flat = [(p, r) for p in range(pairs_count) for r in range(rows_count)]
    ahead = {p: after(p, pairs_count) for p in range(pairs_count)}
    behind = {q: p for p, q in ahead.items()}

    def route(moves):
        return [(p * rows_count + r, q * rows_count + t) for (p, r) in flat for (q, t) in [moves(p, r)]]

    outward = route(lambda p, r: (ahead[p] if r % 2 == 0 else behind[p], r))
    inward = route(lambda p, r: (behind[p] if r % 2 == 0 else ahead[p], r))

    core = [(r, r ^ 1) for r in range(rows_count)]

    def travel(block, moves):
        return lax.ppermute(block, ("pair", "row"), moves)

    def chip_sum(block, radix, flip=0):
        distance = 2
        while distance < rows_count:
            steps = [distance] if radix == 2 or 2 * distance >= rows_count else [distance, 2 * distance, 3 * distance]
            hops = [d ^ flip for d in steps] + ([1] if flip else [])
            others = [lax.ppermute(block, "row", [(r, r ^ d) for r in range(rows_count)]) for d in hops]
            block = others.pop() if flip else block
            for other in others:
                block = block + other
            distance *= 1 + len(steps)
            flip = 0
        return block

    def other_sum(block):
        return chip_sum(block, 4, 1)

    low = raw_rows(matrix, early)
    far_raw = travel(low, outward)
    high, keep, give = local_gram(matrix, low, step)
    mine = chip_sum(keep + lax.ppermute(give, "row", core), 4)
    other = lax.ppermute(mine, "row", core)
    turn_first, turn_second, gram = first_rotation(mine, other)

    sent_small = small_part(high, turn_first, gram, small, step)
    far_small = travel(sent_small, outward)
    turn_main, sent_small, far_raw = lax.optimization_barrier((turn_first, sent_small, far_raw))
    sent_main, sent_last, second_gram = sent_parts(high, turn_main, turn_second, gram, small, last, step)
    far_main, far_last = travel(sent_main, outward), travel(sent_last, outward)
    turn_second, sent_main = lax.optimization_barrier((turn_second, sent_main))
    sent = [(sent_small, early, small, offset), (sent_main, early + small, main, 0), (sent_last, rows - last, last, 0)]
    second_bulk, second_tail, *first_halves = rest_parts(low, high, turn_first, turn_second, sent, bulk, step)

    far_small, second_bulk = lax.optimization_barrier((far_small, second_bulk))
    share = lax.ppermute(far_small[:offset], "row", [(r, r ^ 2) for r in range(rows_count)])
    share, later_bulk, later_tail = lax.optimization_barrier((share, second_bulk, second_tail))
    *raw_halves, far_gram, cross = raw_cross(far_raw, far_small, share, second_bulk, second_tail, step)
    far_main, cross = lax.optimization_barrier((far_main, cross))
    *main_halves, cross = more_cross(
        far_main, early + small, main, second_bulk, second_tail, cross, step, "main_cross"
    )
    far_bulk, far_tail = travel(later_bulk, inward), travel(later_tail, inward)
    *last_halves, cross = more_cross(far_last, rows - last, last, second_bulk, second_tail, cross, step, "last_cross")

    total = other_sum(cross)
    there = travel(total, outward)
    here = lax.ppermute(total, "row", core)
    turn_here = second_rotation(second_gram, far_gram, here, there)
    turn_there = lax.ppermute(turn_here, "row", core)

    sizes = early + small, main, last

    def load_here(refs, row, number):
        return [Rows.of(refs[k : 6 : 2], sizes).get(row, number) for k in (0, 1)]

    def other_slot():
        return 1 - first_slot()

    def load_there(refs, row, number):
        place = pl.ds(row, number)
        far = halves(Rows.of(refs[2:4], (bulk, rows - bulk)).get(row, number))
        return [jnp.concatenate([ref[place, :], half], 1) for ref, half in zip(refs, far)]

    cuts = early + small, rows - last
    done = last_product(
        load_here, raw_halves + main_halves + last_halves, turn_here, None, first_slot, 0, rows, rows, step, cuts, "here_product"
    )

    def load_tail(refs, row, number):
        place = pl.ds(row, number)
        far = halves(Rows((refs[2], bulk, rows - bulk, 0)).get(row, number))
        return [jnp.concatenate([ref[place, :], half], 1) for ref, half in zip(refs, far)]

    done = last_product(
        load_there, [*first_halves, far_bulk, far_bulk], turn_there, done, other_slot, 0, bulk, rows, step, [], "bulk_product"
    )
    return last_product(
        load_tail, [*first_halves, far_tail], turn_there, done, other_slot, bulk, rows - bulk, rows, step, [], "tail_product"
    )


def solution(mesh):
    spec = P(None, "row", "pair")
    run = functools.partial(body, mesh.shape["pair"], mesh.shape["row"])
    return jax.shard_map(run, mesh=mesh, in_specs=(spec,), out_specs=spec, check_vma=False)
```

```python
import functools

import jax
import jax.numpy as jnp
from jax import lax
from jax.experimental import pallas as pl
from jax.experimental.pallas import tpu as pltpu
from jax.sharding import PartitionSpec as P


F32 = jnp.float32
BF16 = jnp.bfloat16
SCOPED = 16 * 1024 * 1024
WHOLE = 54 * 1024 * 1024

RAW = 14
SMALL = 7
LAST = 4
BULK = 28
STEP = 4
SHARE = 3


def after(p, n):
    if p == 0:
        return 1
    if p % 2:
        return n - 2 if p == n - 1 else p + 2
    return p - 2


def halves(x):
    high = x.astype(BF16)
    return high, (x - high.astype(F32)).astype(BF16)


def dot(left, right, contract=((1,), (0,))):
    return lax.dot_general(left, right, (contract, ((), ())), preferred_element_type=F32)


def spread(x):
    twice = jnp.concatenate(halves(x), 1)
    return twice, jnp.concatenate([twice, twice], 0)


def product(left, right):
    width = right.shape[1] // 2
    both = dot(left, right)
    return both[:, :width] + both[:, width:]


def right_parts(right):
    high, low = halves(right)
    return jnp.concatenate([high, low], 1), high


def rows_product(left, parts):
    return halves_product(*halves(left), parts)


def halves_product(high, low, parts):
    width = parts[1].shape[1]
    both = dot(high, parts[0])
    return both[:, :width] + (both[:, width:] + dot(low, parts[1]))


def eye_of(width):
    rows = lax.broadcasted_iota(jnp.int32, (width, width), 0)
    cols = lax.broadcasted_iota(jnp.int32, (width, width), 1)
    return rows, cols


def polar(cross, sign):
    rows, cols = eye_of(cross.shape[0])
    unit = (rows == cols).astype(F32)
    damp = 1.0 / (1.0 + jnp.sqrt(jnp.sum(cross * cross, keepdims=True)))
    left, right = spread(cross)
    left_t, right_t = spread(cross.T)
    s = [product(left, right_t) * (damp * damp), product(left_t, right) * (damp * damp)]
    x = cross * (damp * sign)
    x_left = spread(x)[0]
    s_spread = [spread(a) for a in s]
    s2 = [product(*a) for a in s_spread]
    xs = product(x_left, s_spread[1][1])
    s2_spread = [spread(a) for a in s2]
    s3 = [product(a[0], b[1]) for a, b in zip(s2_spread, s_spread)]
    s4 = [product(*a) for a in s2_spread]
    xs2, xs3 = product(x_left, s2_spread[1][1]), product(spread(xs)[0], s2_spread[1][1])
    e = [0.75 * a - 0.25 * b for a, b in zip(s2, s3)]
    z = [unit - 0.5 * a + 0.5 * b - 0.25 * (0.75 * c - 0.25 * d) for a, b, c, d in zip(s, e, s3, s4)]
    w = [0.75 * unit + 0.25 * a for a in e]
    xw = 0.75 * x + 0.25 * (0.75 * xs2 - 0.25 * xs3)
    e2 = [product(*spread(a)) for a in e]
    zw = [product(spread(a)[0], spread(b)[1]) for a, b in zip(z, w)]
    z_right = spread(z[1])[1]
    xz, xwz = product(x_left, z_right), product(spread(xw)[0], z_right)
    e2_right = [spread(a)[1] for a in e2]
    upper, lower = [a + 0.5 * product(spread(b)[0], c) for a, b, c in zip(z, zw, e2_right)]
    return upper, xz + 0.5 * product(spread(xwz)[0], e2_right[1]), lower


def scaled(cross, down, across):
    return cross * lax.rsqrt(down + 1e-06) * lax.rsqrt(across + 1e-06)


def rotation_of(upper, cross, lower, sign):
    width = cross.shape[0]
    rows, cols = eye_of(width)
    same = rows == cols
    zero = jnp.zeros((width, width), F32)
    down = jnp.sum(jnp.where(same, upper, zero), 1, keepdims=True)
    across = jnp.sum(jnp.where(same, lower, zero), 0, keepdims=True)
    top, wide, bottom = polar(scaled(cross, down, across), sign)
    first = jnp.concatenate([jnp.concatenate([top, wide], 1), jnp.concatenate([-wide.T, bottom], 1)], 0)
    gram = jnp.concatenate(
        [jnp.concatenate([upper, cross], 1), jnp.concatenate([cross.T, lower], 1)], 0
    )
    turned = rows_product(gram, right_parts(first))
    second_cross = rows_product(first[:, :width].T, right_parts(turned[:, width:]))
    diagonal = jnp.sum(first * turned, 0, keepdims=True)
    down = jnp.sum(jnp.where(same, diagonal[:, :width], zero), 1, keepdims=True)
    top, wide, bottom = polar(scaled(second_cross, down, diagonal[:, width:]), sign)
    return gram, first, jnp.concatenate([top, -wide.T], 0), jnp.concatenate([wide, bottom], 0)


def core_of():
    return lax.rem(lax.axis_index("row"), 2)


def first_is_upper():
    p = lax.axis_index("pair")
    clock_upper = (p == 0) | (lax.rem(p, 2) == 1)
    return (core_of() == 0) == clock_upper


def call(kernel, outs, args, name, flops=0, scratch=(), aliases=None, limit=SCOPED):
    places = [place for _, place in args]
    outs = [(*out, F32)[:3] for out in outs]
    out_places = [place for _, place, _ in outs]
    return pl.pallas_call(
        kernel,
        in_specs=[pl.BlockSpec(memory_space=place) for place in places],
        out_specs=[pl.BlockSpec(memory_space=place) for place in out_places],
        out_shape=[
            place(shape, dtype) if place == HERE else jax.ShapeDtypeStruct(shape, dtype) for shape, place, dtype in outs
        ],
        scratch_shapes=list(scratch),
        input_output_aliases=aliases or {},
        compiler_params=pltpu.CompilerParams(vmem_limit_bytes=limit),
        cost_estimate=pl.CostEstimate(flops=flops if flops == LONG else 0, bytes_accessed=0, transcendentals=0),
        name=name,
    )(*[pltpu.with_memory_space_constraint(array, place) for array, place in args])


LONG = 11500000000
HERE = pltpu.VMEM
FAR = pltpu.HBM


class Rows:
    def __init__(self, *parts):
        self.parts = parts

    @classmethod
    def of(cls, refs, sizes):
        return cls(*[(ref, sum(sizes[:k]), sizes[k], 0) for k, ref in enumerate(refs)])

    def at(self, start, count):
        for ref, first, number, offset in self.parts:
            if first <= start and start + count <= first + number:
                return ref, pl.ds(offset + start - first, count)
        raise ValueError(start)

    def get(self, start, count):
        ref, rows = self.at(start, count)
        return ref[rows, :]

    def pair(self, start, count):
        ref, rows = self.at(start, count)
        return jnp.concatenate([ref[0, rows, :], ref[1, rows, :]], 1)


def spans(start, stop, step, *cuts):
    pieces = []
    while start < stop:
        count = min([step, stop - start] + [cut - start for cut in cuts if cut > start])
        pieces.append((start, count))
        start += count
    return pieces


def raw_rows(matrix, count):
    width = matrix.shape[2]

    def kernel(matrix_ref, out_ref, sems):
        copies = [
            pltpu.make_async_copy(matrix_ref.at[k, pl.ds(0, count)], out_ref.at[k], sems.at[k]) for k in range(2)
        ]
        for copy in copies:
            copy.start()
        for copy in copies:
            copy.wait()

    return call(
        kernel,
        [((2, count, width), HERE)],
        [(matrix, FAR)],
        "raw_rows",
        0,
        [pltpu.SemaphoreType.DMA((2,))],
        limit=WHOLE,
    )[0]


def local_gram(matrix, step):
    rows, width = matrix.shape[1:]

    def kernel(matrix_ref, keep_ref, give_ref):
        local = Rows((matrix_ref, 0, rows, 0))
        total = jnp.zeros((2 * width, 4 * width), F32)
        for start, count in spans(0, rows, step):
            high, low = halves(local.pair(start, count))
            total = total + dot(high, jnp.concatenate([high, low], 1), ((0,), (0,)))
        rest = total[:, 2 * width :]
        total = total[:, : 2 * width] + (rest + rest.T)
        upper, cross, lower = total[:width, :width], total[:width, width:], total[width:, width:]
        r, c = eye_of(width)
        diagonal = jnp.sum(jnp.where(r == c, lower, jnp.zeros_like(lower)), 0, keepdims=True)
        packed = jnp.where(r <= c, upper, lower)
        pad = jnp.broadcast_to(diagonal, (8, width))
        mine = core_of() == 0
        keep_ref[:width] = jnp.where(mine, cross, packed)
        give_ref[:width] = jnp.where(mine, packed, cross)
        keep_ref[width:] = pad
        give_ref[width:] = pad

    return call(
        kernel, [((width + 8, width), HERE)] * 2, [(matrix, HERE)], "gram", 16 * rows * width * width
    )


def first_rotation(mine, other):
    width = mine.shape[1]

    def kernel(mine_ref, other_ref, first_ref, second_ref, gram_ref):
        holds_cross = core_of() == 0
        mine, other = mine_ref[...], other_ref[...]
        cross = jnp.where(holds_cross, mine[:width], other[:width])
        packed = jnp.where(holds_cross, other, mine)
        diagonal = packed[width : width + 1]
        packed = packed[:width]
        rows, cols = eye_of(width)
        flipped = packed.T
        upper = jnp.where(rows <= cols, packed, flipped)
        lower = jnp.where(rows > cols, packed, flipped)
        lower = jnp.where(rows == cols, diagonal, lower)
        gram, first, left, right = rotation_of(upper, cross, lower, 1.0)
        upper_first = first_is_upper()
        gram_ref[...] = gram
        first_ref[...] = rows_product(first, right_parts(jnp.where(upper_first, left, right)))
        second_ref[...] = rows_product(first, right_parts(jnp.where(upper_first, right, left)))

    half = ((2 * width, width), HERE)
    return call(kernel, [half, half, ((2 * width, 2 * width), HERE)], [(mine, HERE), (other, HERE)], "first_rotation")


def share_of():
    return lax.rem(lax.div(lax.axis_index("row"), 2), 2)


def rotated_gram(gram, turn):
    return rows_product(turn.T, right_parts(rows_product(gram, right_parts(turn))))


def small_part(matrix, early, turn, gram, small, step):
    width = turn.shape[1]
    turn_share, gram_share = width, width // 2

    def kernel(matrix_ref, turn_ref, gram_ref, out_ref, square_ref):
        place = share_of()
        local = Rows((matrix_ref, -early, matrix.shape[1], 0))
        parts = right_parts(turn_ref[...])
        for start, number in spans(0, small, step):
            out_ref[pl.ds(SHARE * width // 2 + start, number), :] = rows_product(local.pair(start, number), parts)
        square_ref[...] = rotated_gram(gram_ref[...], turn_ref[...])
        out_ref[:turn_share] = turn_ref[pl.ds(pl.multiple_of(place * turn_share, turn_share), turn_share), :]
        out_ref[turn_share : turn_share + gram_share] = square_ref[
            pl.ds(pl.multiple_of(place * gram_share, gram_share), gram_share), :
        ]

    return call(
        kernel,
        [((SHARE * width // 2 + small, width), HERE)],
        [(matrix, HERE), (turn, HERE), (gram, HERE)],
        "small_part",
        12 * small * width * width,
        [pltpu.VMEM((width, width), F32)],
    )[0]


def sent_parts(matrix, early, first, second, gram, small, last, step):
    width = first.shape[1]
    count = matrix.shape[1] - early

    def kernel(matrix_ref, first_ref, second_ref, gram_ref, main_ref, last_ref, second_gram_ref):
        local = Rows((matrix_ref, -early, matrix.shape[1], 0))
        out = Rows((main_ref, small, count - small - last, 0), (last_ref, count - last, last, 0))
        parts = right_parts(first_ref[...])
        for start, number in spans(small, count, step, count - last):
            ref, place = out.at(start, number)
            ref[place, :] = rows_product(local.pair(start, number), parts)
        second_gram_ref[...] = rotated_gram(gram_ref[...], second_ref[...])

    return call(
        kernel,
        [((count - small - last, width), HERE), ((last, width), HERE), ((width, width), HERE)],
        [(matrix, HERE), (first, HERE), (second, HERE), (gram, HERE)],
        "sent_parts",
        12 * count * width * width,
    )


def rest_parts(matrix, early, first, second, sent, bulk, step):
    width = first.shape[1]
    rows = matrix.shape[1]
    arrays = [array for array, *_ in sent]

    def kernel(matrix_ref, first_ref, second_ref, *refs):
        bulk_ref, tail_ref, high_half_ref, low_half_ref = refs[len(sent) :]
        here = Rows((matrix_ref, 0, rows, 0))
        there = Rows(*[(ref, *where) for ref, (_, *where) in zip(refs, sent)])
        out = Rows.of((bulk_ref, tail_ref), (bulk, rows - bulk))
        parts = right_parts(second_ref[...])
        for start, count in spans(0, rows, step, bulk, early):
            ref, place = out.at(start, count)
            ref[place, :] = rows_product(here.pair(start, count), parts)
        parts = right_parts(first_ref[...])
        for start, count in spans(0, rows, step, early, *[first for _, first, *_ in sent]):
            block = rows_product(here.pair(start, count), parts) if start < early else there.get(start, count)
            place = pl.ds(start, count)
            high_half_ref[place, :], low_half_ref[place, :] = halves(block)

    return call(
        kernel,
        [((bulk, width), HERE), ((rows - bulk, width), HERE)] + [((rows, width), HERE, BF16)] * 2,
        [(part, HERE) for part in (matrix, first, second, *arrays)],
        "rest_parts",
        12 * (rows + early) * width * width,
    )


def cross_term(high, low):
    width = high.shape[1] // 2
    own = jnp.concatenate([high[:, :width], low[:, :width]], 1)
    far = jnp.concatenate([high[:, width:], low[:, width:]], 1)
    return dot(own, far, ((0,), (0,)))


def cross_sum(total):
    width = total.shape[0] // 2
    return (total[:width, :width] + total[:width, width:]) + (total[width:, :width] + total[width:, width:])


def raw_cross(far_raw, far_small, share, bulk, tail, step):
    width = bulk.shape[1]
    offset = SHARE * width // 2
    early, small = far_raw.shape[1], far_small.shape[0] - offset
    turn_share, gram_share = width, width // 2

    def kernel(
        raw_ref, small_ref, share_ref, bulk_ref, tail_ref, high_ref, low_ref, gram_ref, out_ref, turn_ref
    ):
        for place, ref in ((share_of(), small_ref), (1 - share_of(), share_ref)):
            turn_ref[pl.ds(pl.multiple_of(place * turn_share, turn_share), turn_share), :] = ref[:turn_share]
            gram_ref[pl.ds(pl.multiple_of(place * gram_share, gram_share), gram_share), :] = ref[
                turn_share : turn_share + gram_share
            ]
        own = Rows.of((bulk_ref, tail_ref), (bulk.shape[0], tail.shape[0]))
        raw = Rows((raw_ref, 0, early, 0))
        far = Rows((small_ref, early, small, offset))
        parts = right_parts(turn_ref[...])
        total = jnp.zeros((2 * width, 2 * width), F32)
        for start, count in spans(0, early + small, step, early, bulk.shape[0]):
            block = rows_product(raw.pair(start, count), parts) if start < early else far.get(start, count)
            high, low = halves(jnp.concatenate([own.get(start, count), block], 1))
            place = pl.ds(start, count)
            high_ref[place, :], low_ref[place, :] = high, low
            total = total + cross_term(high, low)
        out_ref[...] = cross_sum(total)

    return call(
        kernel,
        [((early + small, 2 * width), HERE, BF16)] * 2 + [((width, width), HERE)] * 2,
        [(part, HERE) for part in (far_raw, far_small, share, bulk, tail)],
        "raw_cross",
        12 * (early + small) * width * width,
        [pltpu.VMEM((2 * width, width), F32)],
    )


def more_cross(far, first_row, count, bulk, tail, so_far, step, name):
    width = bulk.shape[1]

    def kernel(far_ref, bulk_ref, tail_ref, total_ref, high_ref, low_ref, out_ref):
        own = Rows.of((bulk_ref, tail_ref), (bulk.shape[0], tail.shape[0]))
        part = Rows((far_ref, first_row, count, 0))
        total = jnp.zeros((2 * width, 2 * width), F32)
        for start, number in spans(first_row, first_row + count, step, bulk.shape[0]):
            high, low = halves(jnp.concatenate([own.get(start, number), part.get(start, number)], 1))
            place = pl.ds(start - first_row, number)
            high_ref[place, :], low_ref[place, :] = high, low
            total = total + cross_term(high, low)
        out_ref[...] = total_ref[...] + cross_sum(total)

    return call(
        kernel,
        [((count, 2 * width), HERE, BF16)] * 2 + [((width, width), HERE)],
        [(far, HERE), (bulk, HERE), (tail, HERE), (so_far, HERE)],
        name,
        6 * count * width * width,
    )


def second_rotation(own_gram, far_gram, here, there):
    width = here.shape[1]

    def kernel(own_gram_ref, far_ref, here_ref, there_ref, out_ref):
        p, n = lax.axis_index("pair"), lax.axis_size("pair")
        odd = lax.rem(p, 2) == 1
        outward = core_of() == 1
        own_upper_out = (p == 0) | (odd & (p != n - 1))
        own_upper = (outward & own_upper_out) | (jnp.logical_not(outward) & jnp.logical_not(odd))
        sign = jnp.where(own_upper, 1.0, -1.0).astype(F32)
        cross = here_ref[...] + there_ref[...].T
        _, first, left, right = rotation_of(own_gram_ref[...], cross, far_ref[...], sign)
        keeps_own = (outward & (p == 0)) | (jnp.logical_not(outward) & (p == 1))
        out_ref[...] = rows_product(first, right_parts(jnp.where(keeps_own, left, right)))

    return call(
        kernel,
        [((2 * width, width), HERE)],
        [(own_gram, HERE), (far_gram, HERE), (here, HERE), (there, HERE)],
        "second_rotation",
        LONG,
    )[0]


def last_product(load, arrays, turn, done, slot_of, start, count, rows, step, cuts, name):
    width = turn.shape[1]
    pieces = spans(start, start + count, step, *cuts)

    def kernel(*refs):
        turn_ref = refs[len(arrays)]
        out_ref, stage_ref, sems = refs[-3:]
        parts = right_parts(turn_ref[...])
        slot = slot_of()
        copies = []
        for k, (row, number) in enumerate(pieces):
            place = pl.ds(row - start, number)
            stage_ref[place, :] = halves_product(*load(refs, row, number), parts)
            copies.append(
                pltpu.make_async_copy(stage_ref.at[place, :], out_ref.at[slot, pl.ds(row, number), :], sems.at[k])
            )
            copies[-1].start()
        for copy in copies:
            copy.wait()

    args = [(array, HERE) for array in (*arrays, turn)] + ([] if done is None else [(done, FAR)])
    return call(
        kernel,
        [((2, rows, width), FAR)],
        args,
        name,
        12 * count * width * width,
        [pltpu.VMEM((count, width), F32), pltpu.SemaphoreType.DMA((len(pieces),))],
        None if done is None else {len(args) - 1: 0},
    )[0]


def first_slot():
    return jnp.where(lax.rem(lax.axis_index("pair"), 2) == core_of(), 1, 0)


def body(pairs_count, rows_count, matrix):
    rows, width = matrix.shape[1:]
    unit = rows // 32
    early, small, last, bulk, step = (part * unit for part in (RAW, SMALL, LAST, BULK, STEP))
    main = rows - early - small - last
    offset = SHARE * width // 2
    flat = [(p, r) for p in range(pairs_count) for r in range(rows_count)]
    ahead = {p: after(p, pairs_count) for p in range(pairs_count)}
    behind = {q: p for p, q in ahead.items()}

    def route(moves):
        return [(p * rows_count + r, q * rows_count + t) for (p, r) in flat for (q, t) in [moves(p, r)]]

    outward = route(lambda p, r: (ahead[p] if r % 2 == 0 else behind[p], r))
    inward = route(lambda p, r: (behind[p] if r % 2 == 0 else ahead[p], r))

    core = [(r, r ^ 1) for r in range(rows_count)]

    def travel(block, moves):
        return lax.ppermute(block, ("pair", "row"), moves)

    def chip_sum(block, radix, flip=0):
        distance = 2
        while distance < rows_count:
            steps = [distance] if radix == 2 or 2 * distance >= rows_count else [distance, 2 * distance, 3 * distance]
            hops = [d ^ flip for d in steps] + ([1] if flip else [])
            others = [lax.ppermute(block, "row", [(r, r ^ d) for r in range(rows_count)]) for d in hops]
            block = others.pop() if flip else block
            for other in others:
                block = block + other
            distance *= 1 + len(steps)
            flip = 0
        return block

    def other_sum(block):
        return chip_sum(block, 4, 1)

    low = raw_rows(matrix, early)
    far_raw = travel(low, outward)
    keep, give = local_gram(matrix, step)
    mine = chip_sum(keep + lax.ppermute(give, "row", core), 4)
    other = lax.ppermute(mine, "row", core)
    turn_first, turn_second, gram = first_rotation(mine, other)

    sent_small = small_part(matrix, early, turn_first, gram, small, step)
    far_small = travel(sent_small, outward)
    turn_main, sent_small, far_raw = lax.optimization_barrier((turn_first, sent_small, far_raw))
    sent_main, sent_last, second_gram = sent_parts(matrix, early, turn_main, turn_second, gram, small, last, step)
    far_main, far_last = travel(sent_main, outward), travel(sent_last, outward)
    turn_second, sent_main = lax.optimization_barrier((turn_second, sent_main))
    sent = [(sent_small, early, small, offset), (sent_main, early + small, main, 0), (sent_last, rows - last, last, 0)]
    second_bulk, second_tail, *first_halves = rest_parts(matrix, early, turn_first, turn_second, sent, bulk, step)

    far_small, second_bulk = lax.optimization_barrier((far_small, second_bulk))
    share = lax.ppermute(far_small[:offset], "row", [(r, r ^ 2) for r in range(rows_count)])
    share, later_bulk, later_tail = lax.optimization_barrier((share, second_bulk, second_tail))
    *raw_halves, far_gram, cross = raw_cross(far_raw, far_small, share, second_bulk, second_tail, step)
    far_main, cross = lax.optimization_barrier((far_main, cross))
    *main_halves, cross = more_cross(
        far_main, early + small, main, second_bulk, second_tail, cross, step, "main_cross"
    )
    far_bulk, far_tail = travel(later_bulk, inward), travel(later_tail, inward)
    *last_halves, cross = more_cross(far_last, rows - last, last, second_bulk, second_tail, cross, step, "last_cross")

    total = other_sum(cross)
    there = travel(total, outward)
    here = lax.ppermute(total, "row", core)
    turn_here = second_rotation(second_gram, far_gram, here, there)
    turn_there = lax.ppermute(turn_here, "row", core)

    sizes = early + small, main, last

    def load_here(refs, row, number):
        return [Rows.of(refs[k : 6 : 2], sizes).get(row, number) for k in (0, 1)]

    def other_slot():
        return 1 - first_slot()

    def load_there(refs, row, number):
        place = pl.ds(row, number)
        far = halves(Rows.of(refs[2:4], (bulk, rows - bulk)).get(row, number))
        return [jnp.concatenate([ref[place, :], half], 1) for ref, half in zip(refs, far)]

    cuts = early + small, rows - last
    done = last_product(
        load_here, raw_halves + main_halves + last_halves, turn_here, None, first_slot, 0, rows, rows, step, cuts, "here_product"
    )

    def load_tail(refs, row, number):
        place = pl.ds(row, number)
        far = halves(Rows((refs[2], bulk, rows - bulk, 0)).get(row, number))
        return [jnp.concatenate([ref[place, :], half], 1) for ref, half in zip(refs, far)]

    done = last_product(
        load_there, [*first_halves, far_bulk, far_bulk], turn_there, done, other_slot, 0, bulk, rows, step, [], "bulk_product"
    )
    return last_product(
        load_tail, [*first_halves, far_tail], turn_there, done, other_slot, bulk, rows - bulk, rows, step, [], "tail_product"
    )


def solution(mesh):
    spec = P(None, "row", "pair")
    run = functools.partial(body, mesh.shape["pair"], mesh.shape["row"])
    return jax.shard_map(run, mesh=mesh, in_specs=(spec,), out_specs=spec, check_vma=False)
```

```python
import functools

import jax
import jax.numpy as jnp
from jax import lax
from jax.experimental import pallas as pl
from jax.experimental.pallas import tpu as pltpu
from jax.sharding import PartitionSpec as P


F32 = jnp.float32
BF16 = jnp.bfloat16
SCOPED = 16 * 1024 * 1024
WHOLE = 54 * 1024 * 1024

RAW = 14
SMALL = 7
LAST = 4
BULK = 28
STEP = 4
SHARE = 3


def after(p, n):
    if p == 0:
        return 1
    if p % 2:
        return n - 2 if p == n - 1 else p + 2
    return p - 2


def halves(x):
    high = x.astype(BF16)
    return high, (x - high.astype(F32)).astype(BF16)


def dot(left, right, contract=((1,), (0,))):
    return lax.dot_general(left, right, (contract, ((), ())), preferred_element_type=F32)


def spread(x):
    twice = jnp.concatenate(halves(x), 1)
    return twice, jnp.concatenate([twice, twice], 0)


def product(left, right):
    width = right.shape[1] // 2
    both = dot(left, right)
    return both[:, :width] + both[:, width:]


def right_parts(right):
    high, low = halves(right)
    return jnp.concatenate([high, low], 1), high


def rows_product(left, parts):
    return halves_product(*halves(left), parts)


def halves_product(high, low, parts):
    width = parts[1].shape[1]
    both = dot(high, parts[0])
    return both[:, :width] + (both[:, width:] + dot(low, parts[1]))


def eye_of(width):
    rows = lax.broadcasted_iota(jnp.int32, (width, width), 0)
    cols = lax.broadcasted_iota(jnp.int32, (width, width), 1)
    return rows, cols


def polar(cross, sign):
    rows, cols = eye_of(cross.shape[0])
    unit = (rows == cols).astype(F32)
    damp = 1.0 / (1.0 + jnp.sqrt(jnp.sum(cross * cross, keepdims=True)))
    left, right = spread(cross)
    left_t, right_t = spread(cross.T)
    s = [product(left, right_t) * (damp * damp), product(left_t, right) * (damp * damp)]
    x = cross * (damp * sign)
    x_left = spread(x)[0]
    s_spread = [spread(a) for a in s]
    s2 = [product(*a) for a in s_spread]
    xs = product(x_left, s_spread[1][1])
    s2_spread = [spread(a) for a in s2]
    s3 = [product(a[0], b[1]) for a, b in zip(s2_spread, s_spread)]
    s4 = [product(*a) for a in s2_spread]
    xs2, xs3 = product(x_left, s2_spread[1][1]), product(spread(xs)[0], s2_spread[1][1])
    e = [0.75 * a - 0.25 * b for a, b in zip(s2, s3)]
    z = [unit - 0.5 * a + 0.5 * b - 0.25 * (0.75 * c - 0.25 * d) for a, b, c, d in zip(s, e, s3, s4)]
    w = [0.75 * unit + 0.25 * a for a in e]
    xw = 0.75 * x + 0.25 * (0.75 * xs2 - 0.25 * xs3)
    e2 = [product(*spread(a)) for a in e]
    zw = [product(spread(a)[0], spread(b)[1]) for a, b in zip(z, w)]
    z_right = spread(z[1])[1]
    xz, xwz = product(x_left, z_right), product(spread(xw)[0], z_right)
    e2_right = [spread(a)[1] for a in e2]
    upper, lower = [a + 0.5 * product(spread(b)[0], c) for a, b, c in zip(z, zw, e2_right)]
    return upper, xz + 0.5 * product(spread(xwz)[0], e2_right[1]), lower


def scaled(cross, down, across):
    return cross * lax.rsqrt(down + 1e-06) * lax.rsqrt(across + 1e-06)


def rotation_of(upper, cross, lower, sign):
    width = cross.shape[0]
    rows, cols = eye_of(width)
    same = rows == cols
    zero = jnp.zeros((width, width), F32)
    down = jnp.sum(jnp.where(same, upper, zero), 1, keepdims=True)
    across = jnp.sum(jnp.where(same, lower, zero), 0, keepdims=True)
    top, wide, bottom = polar(scaled(cross, down, across), sign)
    first = jnp.concatenate([jnp.concatenate([top, wide], 1), jnp.concatenate([-wide.T, bottom], 1)], 0)
    gram = jnp.concatenate(
        [jnp.concatenate([upper, cross], 1), jnp.concatenate([cross.T, lower], 1)], 0
    )
    turned = rows_product(gram, right_parts(first))
    second_cross = rows_product(first[:, :width].T, right_parts(turned[:, width:]))
    diagonal = jnp.sum(first * turned, 0, keepdims=True)
    down = jnp.sum(jnp.where(same, diagonal[:, :width], zero), 1, keepdims=True)
    top, wide, bottom = polar(scaled(second_cross, down, diagonal[:, width:]), sign)
    return gram, first, jnp.concatenate([top, -wide.T], 0), jnp.concatenate([wide, bottom], 0)


def core_of():
    return lax.rem(lax.axis_index("row"), 2)


def first_is_upper():
    p = lax.axis_index("pair")
    clock_upper = (p == 0) | (lax.rem(p, 2) == 1)
    return (core_of() == 0) == clock_upper


def call(kernel, outs, args, name, flops=0, scratch=(), aliases=None, limit=SCOPED):
    places = [place for _, place in args]
    outs = [(*out, F32)[:3] for out in outs]
    out_places = [place for _, place, _ in outs]
    return pl.pallas_call(
        kernel,
        in_specs=[pl.BlockSpec(memory_space=place) for place in places],
        out_specs=[pl.BlockSpec(memory_space=place) for place in out_places],
        out_shape=[
            place(shape, dtype) if place == HERE else jax.ShapeDtypeStruct(shape, dtype) for shape, place, dtype in outs
        ],
        scratch_shapes=list(scratch),
        input_output_aliases=aliases or {},
        compiler_params=pltpu.CompilerParams(vmem_limit_bytes=limit),
        cost_estimate=pl.CostEstimate(flops=flops if flops == LONG else 0, bytes_accessed=0, transcendentals=0),
        name=name,
    )(*[pltpu.with_memory_space_constraint(array, place) for array, place in args])


LONG = 11500000000
HERE = pltpu.VMEM
FAR = pltpu.HBM


class Rows:
    def __init__(self, *parts):
        self.parts = parts

    @classmethod
    def of(cls, refs, sizes):
        return cls(*[(ref, sum(sizes[:k]), sizes[k], 0) for k, ref in enumerate(refs)])

    def at(self, start, count):
        for ref, first, number, offset in self.parts:
            if first <= start and start + count <= first + number:
                return ref, pl.ds(offset + start - first, count)
        raise ValueError(start)

    def get(self, start, count):
        ref, rows = self.at(start, count)
        return ref[rows, :]

    def pair(self, start, count):
        ref, rows = self.at(start, count)
        return jnp.concatenate([ref[0, rows, :], ref[1, rows, :]], 1)


def spans(start, stop, step, *cuts):
    pieces = []
    while start < stop:
        count = min([step, stop - start] + [cut - start for cut in cuts if cut > start])
        pieces.append((start, count))
        start += count
    return pieces


def raw_rows(matrix, count):
    width = matrix.shape[2]

    def kernel(matrix_ref, out_ref, sems):
        copies = [
            pltpu.make_async_copy(matrix_ref.at[k, pl.ds(0, count)], out_ref.at[k], sems.at[k]) for k in range(2)
        ]
        for copy in copies:
            copy.start()
        for copy in copies:
            copy.wait()

    return call(
        kernel,
        [((2, count, width), HERE)],
        [(matrix, FAR)],
        "raw_rows",
        0,
        [pltpu.SemaphoreType.DMA((2,))],
        limit=WHOLE,
    )[0]


def tapered(start, stop, step, unit, *cuts):
    pieces = []
    while start < stop:
        count = min(step, max(unit, (stop - start) // 2 // unit * unit))
        pieces += spans(start, start + count, step, *cuts)
        start += count
    return pieces


def local_gram(matrix, step):
    rows, width = matrix.shape[1:]

    def kernel(matrix_ref, keep_ref, give_ref):
        local = Rows((matrix_ref, 0, rows, 0))
        total = jnp.zeros((2 * width, 4 * width), F32)
        for start, count in spans(0, rows, step):
            high, low = halves(local.pair(start, count))
            total = total + dot(high, jnp.concatenate([high, low], 1), ((0,), (0,)))
        rest = total[:, 2 * width :]
        total = total[:, : 2 * width] + (rest + rest.T)
        upper, cross, lower = total[:width, :width], total[:width, width:], total[width:, width:]
        r, c = eye_of(width)
        diagonal = jnp.sum(jnp.where(r == c, lower, jnp.zeros_like(lower)), 0, keepdims=True)
        packed = jnp.where(r <= c, upper, lower)
        pad = jnp.broadcast_to(diagonal, (8, width))
        mine = core_of() == 0
        keep_ref[:width] = jnp.where(mine, cross, packed)
        give_ref[:width] = jnp.where(mine, packed, cross)
        keep_ref[width:] = pad
        give_ref[width:] = pad

    return call(
        kernel, [((width + 8, width), HERE)] * 2, [(matrix, HERE)], "gram", 16 * rows * width * width
    )


def first_rotation(mine, other):
    width = mine.shape[1]

    def kernel(mine_ref, other_ref, first_ref, second_ref, gram_ref):
        holds_cross = core_of() == 0
        mine, other = mine_ref[...], other_ref[...]
        cross = jnp.where(holds_cross, mine[:width], other[:width])
        packed = jnp.where(holds_cross, other, mine)
        diagonal = packed[width : width + 1]
        packed = packed[:width]
        rows, cols = eye_of(width)
        flipped = packed.T
        upper = jnp.where(rows <= cols, packed, flipped)
        lower = jnp.where(rows > cols, packed, flipped)
        lower = jnp.where(rows == cols, diagonal, lower)
        gram, first, left, right = rotation_of(upper, cross, lower, 1.0)
        upper_first = first_is_upper()
        gram_ref[...] = gram
        first_ref[...] = rows_product(first, right_parts(jnp.where(upper_first, left, right)))
        second_ref[...] = rows_product(first, right_parts(jnp.where(upper_first, right, left)))

    half = ((2 * width, width), HERE)
    return call(kernel, [half, half, ((2 * width, 2 * width), HERE)], [(mine, HERE), (other, HERE)], "first_rotation")


def share_of():
    return lax.rem(lax.div(lax.axis_index("row"), 2), 2)


def rotated_gram(gram, turn):
    return rows_product(turn.T, right_parts(rows_product(gram, right_parts(turn))))


def small_part(matrix, early, turn, gram, small, step):
    width = turn.shape[1]
    turn_share, gram_share = width, width // 2

    def kernel(matrix_ref, turn_ref, gram_ref, out_ref, square_ref):
        place = share_of()
        local = Rows((matrix_ref, -early, matrix.shape[1], 0))
        parts = right_parts(turn_ref[...])
        for start, number in spans(0, small, step):
            out_ref[pl.ds(SHARE * width // 2 + start, number), :] = rows_product(local.pair(start, number), parts)
        square_ref[...] = rotated_gram(gram_ref[...], turn_ref[...])
        out_ref[:turn_share] = turn_ref[pl.ds(pl.multiple_of(place * turn_share, turn_share), turn_share), :]
        out_ref[turn_share : turn_share + gram_share] = square_ref[
            pl.ds(pl.multiple_of(place * gram_share, gram_share), gram_share), :
        ]

    return call(
        kernel,
        [((SHARE * width // 2 + small, width), HERE)],
        [(matrix, HERE), (turn, HERE), (gram, HERE)],
        "small_part",
        12 * small * width * width,
        [pltpu.VMEM((width, width), F32)],
    )[0]


def sent_parts(matrix, early, first, second, gram, small, last, step):
    width = first.shape[1]
    count = matrix.shape[1] - early

    def kernel(matrix_ref, first_ref, second_ref, gram_ref, main_ref, last_ref, second_gram_ref):
        local = Rows((matrix_ref, -early, matrix.shape[1], 0))
        out = Rows((main_ref, small, count - small - last, 0), (last_ref, count - last, last, 0))
        parts = right_parts(first_ref[...])
        for start, number in spans(small, count, step, count - last):
            ref, place = out.at(start, number)
            ref[place, :] = rows_product(local.pair(start, number), parts)
        second_gram_ref[...] = rotated_gram(gram_ref[...], second_ref[...])

    return call(
        kernel,
        [((count - small - last, width), HERE), ((last, width), HERE), ((width, width), HERE)],
        [(matrix, HERE), (first, HERE), (second, HERE), (gram, HERE)],
        "sent_parts",
        12 * count * width * width,
    )


def rest_parts(matrix, early, first, second, sent, bulk, step):
    width = first.shape[1]
    rows = matrix.shape[1]
    arrays = [array for array, *_ in sent]

    def kernel(matrix_ref, first_ref, second_ref, *refs):
        bulk_ref, tail_ref, high_half_ref, low_half_ref = refs[len(sent) :]
        here = Rows((matrix_ref, 0, rows, 0))
        there = Rows(*[(ref, *where) for ref, (_, *where) in zip(refs, sent)])
        out = Rows.of((bulk_ref, tail_ref), (bulk, rows - bulk))
        parts = right_parts(second_ref[...])
        for start, count in spans(0, rows, step, bulk, early):
            ref, place = out.at(start, count)
            ref[place, :] = rows_product(here.pair(start, count), parts)
        parts = right_parts(first_ref[...])
        for start, count in spans(0, rows, step, early, *[first for _, first, *_ in sent]):
            block = rows_product(here.pair(start, count), parts) if start < early else there.get(start, count)
            place = pl.ds(start, count)
            high_half_ref[place, :], low_half_ref[place, :] = halves(block)

    return call(
        kernel,
        [((bulk, width), HERE), ((rows - bulk, width), HERE)] + [((rows, width), HERE, BF16)] * 2,
        [(part, HERE) for part in (matrix, first, second, *arrays)],
        "rest_parts",
        12 * (rows + early) * width * width,
    )


def cross_term(high, low):
    width = high.shape[1] // 2
    own = jnp.concatenate([high[:, :width], low[:, :width]], 1)
    far = jnp.concatenate([high[:, width:], low[:, width:]], 1)
    return dot(own, far, ((0,), (0,)))


def cross_sum(total):
    width = total.shape[0] // 2
    return (total[:width, :width] + total[:width, width:]) + (total[width:, :width] + total[width:, width:])


def raw_cross(far_raw, far_small, share, bulk, tail, step):
    width = bulk.shape[1]
    offset = SHARE * width // 2
    early, small = far_raw.shape[1], far_small.shape[0] - offset
    turn_share, gram_share = width, width // 2

    def kernel(
        raw_ref, small_ref, share_ref, bulk_ref, tail_ref, high_ref, low_ref, gram_ref, out_ref, turn_ref
    ):
        for place, ref in ((share_of(), small_ref), (1 - share_of(), share_ref)):
            turn_ref[pl.ds(pl.multiple_of(place * turn_share, turn_share), turn_share), :] = ref[:turn_share]
            gram_ref[pl.ds(pl.multiple_of(place * gram_share, gram_share), gram_share), :] = ref[
                turn_share : turn_share + gram_share
            ]
        own = Rows.of((bulk_ref, tail_ref), (bulk.shape[0], tail.shape[0]))
        raw = Rows((raw_ref, 0, early, 0))
        far = Rows((small_ref, early, small, offset))
        parts = right_parts(turn_ref[...])
        total = jnp.zeros((2 * width, 2 * width), F32)
        for start, count in spans(0, early + small, step, early, bulk.shape[0]):
            block = rows_product(raw.pair(start, count), parts) if start < early else far.get(start, count)
            high, low = halves(jnp.concatenate([own.get(start, count), block], 1))
            place = pl.ds(start, count)
            high_ref[place, :], low_ref[place, :] = high, low
            total = total + cross_term(high, low)
        out_ref[...] = cross_sum(total)

    return call(
        kernel,
        [((early + small, 2 * width), HERE, BF16)] * 2 + [((width, width), HERE)] * 2,
        [(part, HERE) for part in (far_raw, far_small, share, bulk, tail)],
        "raw_cross",
        12 * (early + small) * width * width,
        [pltpu.VMEM((2 * width, width), F32)],
    )


def more_cross(far, first_row, count, bulk, tail, so_far, step, name):
    width = bulk.shape[1]

    def kernel(far_ref, bulk_ref, tail_ref, total_ref, high_ref, low_ref, out_ref):
        own = Rows.of((bulk_ref, tail_ref), (bulk.shape[0], tail.shape[0]))
        part = Rows((far_ref, first_row, count, 0))
        total = jnp.zeros((2 * width, 2 * width), F32)
        for start, number in spans(first_row, first_row + count, step, bulk.shape[0]):
            high, low = halves(jnp.concatenate([own.get(start, number), part.get(start, number)], 1))
            place = pl.ds(start - first_row, number)
            high_ref[place, :], low_ref[place, :] = high, low
            total = total + cross_term(high, low)
        out_ref[...] = total_ref[...] + cross_sum(total)

    return call(
        kernel,
        [((count, 2 * width), HERE, BF16)] * 2 + [((width, width), HERE)],
        [(far, HERE), (bulk, HERE), (tail, HERE), (so_far, HERE)],
        name,
        6 * count * width * width,
    )


def second_rotation(own_gram, far_gram, here, there):
    width = here.shape[1]

    def kernel(own_gram_ref, far_ref, here_ref, there_ref, out_ref):
        p, n = lax.axis_index("pair"), lax.axis_size("pair")
        odd = lax.rem(p, 2) == 1
        outward = core_of() == 1
        own_upper_out = (p == 0) | (odd & (p != n - 1))
        own_upper = (outward & own_upper_out) | (jnp.logical_not(outward) & jnp.logical_not(odd))
        sign = jnp.where(own_upper, 1.0, -1.0).astype(F32)
        cross = here_ref[...] + there_ref[...].T
        _, first, left, right = rotation_of(own_gram_ref[...], cross, far_ref[...], sign)
        keeps_own = (outward & (p == 0)) | (jnp.logical_not(outward) & (p == 1))
        out_ref[...] = rows_product(first, right_parts(jnp.where(keeps_own, left, right)))

    return call(
        kernel,
        [((2 * width, width), HERE)],
        [(own_gram, HERE), (far_gram, HERE), (here, HERE), (there, HERE)],
        "second_rotation",
        LONG,
    )[0]


def last_product(load, arrays, turn, done, slot_of, start, count, rows, step, cuts, name):
    width = turn.shape[1]
    pieces = tapered(start, start + count, 2 * step, step // STEP, *cuts)

    def kernel(*refs):
        turn_ref = refs[len(arrays)]
        out_ref, stage_ref, sems = refs[-3:]
        parts = right_parts(turn_ref[...])
        slot = slot_of()
        copies = []
        for k, (row, number) in enumerate(pieces):
            place = pl.ds(row - start, number)
            stage_ref[place, :] = halves_product(*load(refs, row, number), parts)
            copies.append(
                pltpu.make_async_copy(stage_ref.at[place, :], out_ref.at[slot, pl.ds(row, number), :], sems.at[k])
            )
            copies[-1].start()
        for copy in copies:
            copy.wait()

    args = [(array, HERE) for array in (*arrays, turn)] + ([] if done is None else [(done, FAR)])
    return call(
        kernel,
        [((2, rows, width), FAR)],
        args,
        name,
        12 * count * width * width,
        [pltpu.VMEM((count, width), F32), pltpu.SemaphoreType.DMA((len(pieces),))],
        None if done is None else {len(args) - 1: 0},
    )[0]


def first_slot():
    return jnp.where(lax.rem(lax.axis_index("pair"), 2) == core_of(), 1, 0)


def body(pairs_count, rows_count, matrix):
    rows, width = matrix.shape[1:]
    unit = rows // 32
    early, small, last, bulk, step = (part * unit for part in (RAW, SMALL, LAST, BULK, STEP))
    main = rows - early - small - last
    offset = SHARE * width // 2
    flat = [(p, r) for p in range(pairs_count) for r in range(rows_count)]
    ahead = {p: after(p, pairs_count) for p in range(pairs_count)}
    behind = {q: p for p, q in ahead.items()}

    def route(moves):
        return [(p * rows_count + r, q * rows_count + t) for (p, r) in flat for (q, t) in [moves(p, r)]]

    outward = route(lambda p, r: (ahead[p] if r % 2 == 0 else behind[p], r))
    inward = route(lambda p, r: (behind[p] if r % 2 == 0 else ahead[p], r))

    core = [(r, r ^ 1) for r in range(rows_count)]

    def travel(block, moves):
        return lax.ppermute(block, ("pair", "row"), moves)

    def chip_sum(block, radix, flip=0):
        distance = 2
        while distance < rows_count:
            steps = [distance] if radix == 2 or 2 * distance >= rows_count else [distance, 2 * distance, 3 * distance]
            hops = [d ^ flip for d in steps] + ([1] if flip else [])
            others = [lax.ppermute(block, "row", [(r, r ^ d) for r in range(rows_count)]) for d in hops]
            block = others.pop() if flip else block
            for other in others:
                block = block + other
            distance *= 1 + len(steps)
            flip = 0
        return block

    def other_sum(block):
        return chip_sum(block, 4, 1)

    low = raw_rows(matrix, early)
    far_raw = travel(low, outward)
    keep, give = local_gram(matrix, step)
    mine = chip_sum(keep + lax.ppermute(give, "row", core), 4)
    other = lax.ppermute(mine, "row", core)
    turn_first, turn_second, gram = first_rotation(mine, other)

    sent_small = small_part(matrix, early, turn_first, gram, small, step)
    far_small = travel(sent_small, outward)
    turn_main, sent_small, far_raw = lax.optimization_barrier((turn_first, sent_small, far_raw))
    sent_main, sent_last, second_gram = sent_parts(matrix, early, turn_main, turn_second, gram, small, last, step)
    far_main, far_last = travel(sent_main, outward), travel(sent_last, outward)
    turn_second, sent_main = lax.optimization_barrier((turn_second, sent_main))
    sent = [(sent_small, early, small, offset), (sent_main, early + small, main, 0), (sent_last, rows - last, last, 0)]
    second_bulk, second_tail, *first_halves = rest_parts(matrix, early, turn_first, turn_second, sent, bulk, step)

    far_small, second_bulk = lax.optimization_barrier((far_small, second_bulk))
    share = lax.ppermute(far_small[:offset], "row", [(r, r ^ 2) for r in range(rows_count)])
    share, later_bulk, later_tail = lax.optimization_barrier((share, second_bulk, second_tail))
    *raw_halves, far_gram, cross = raw_cross(far_raw, far_small, share, second_bulk, second_tail, step)
    far_main, cross = lax.optimization_barrier((far_main, cross))
    *main_halves, cross = more_cross(
        far_main, early + small, main, second_bulk, second_tail, cross, step, "main_cross"
    )
    far_bulk, far_tail = travel(later_bulk, inward), travel(later_tail, inward)
    *last_halves, cross = more_cross(far_last, rows - last, last, second_bulk, second_tail, cross, step, "last_cross")

    total = other_sum(cross)
    there = travel(total, outward)
    here = lax.ppermute(total, "row", core)
    turn_here = second_rotation(second_gram, far_gram, here, there)
    turn_there = lax.ppermute(turn_here, "row", core)

    sizes = early + small, main, last

    def load_here(refs, row, number):
        return [Rows.of(refs[k : 6 : 2], sizes).get(row, number) for k in (0, 1)]

    def other_slot():
        return 1 - first_slot()

    def load_there(refs, row, number):
        place = pl.ds(row, number)
        far = halves(Rows.of(refs[2:4], (bulk, rows - bulk)).get(row, number))
        return [jnp.concatenate([ref[place, :], half], 1) for ref, half in zip(refs, far)]

    cuts = early + small, rows - last
    done = last_product(
        load_here, raw_halves + main_halves + last_halves, turn_here, None, first_slot, 0, rows, rows, step, cuts, "here_product"
    )

    def load_tail(refs, row, number):
        place = pl.ds(row, number)
        far = halves(Rows((refs[2], bulk, rows - bulk, 0)).get(row, number))
        return [jnp.concatenate([ref[place, :], half], 1) for ref, half in zip(refs, far)]

    done = last_product(
        load_there, [*first_halves, far_bulk, far_bulk], turn_there, done, other_slot, 0, bulk, rows, step, [], "bulk_product"
    )
    return last_product(
        load_tail, [*first_halves, far_tail], turn_there, done, other_slot, bulk, rows - bulk, rows, step, [], "tail_product"
    )


def solution(mesh):
    spec = P(None, "row", "pair")
    run = functools.partial(body, mesh.shape["pair"], mesh.shape["row"])
    return jax.shard_map(run, mesh=mesh, in_specs=(spec,), out_specs=spec, check_vma=False)
```

```python
import functools

import jax
import jax.numpy as jnp
from jax import lax
from jax.experimental import pallas as pl
from jax.experimental.pallas import tpu as pltpu
from jax.sharding import PartitionSpec as P


F32 = jnp.float32
BF16 = jnp.bfloat16
SCOPED = 16 * 1024 * 1024
WHOLE = 54 * 1024 * 1024

RAW = 14
SMALL = 7
LAST = 4
BULK = 28
STEP = 4
SHARE = 3


def after(p, n):
    if p == 0:
        return 1
    if p % 2:
        return n - 2 if p == n - 1 else p + 2
    return p - 2


def halves(x):
    high = x.astype(BF16)
    return high, (x - high.astype(F32)).astype(BF16)


def dot(left, right, contract=((1,), (0,))):
    return lax.dot_general(left, right, (contract, ((), ())), preferred_element_type=F32)


def spread(x):
    twice = jnp.concatenate(halves(x), 1)
    return twice, jnp.concatenate([twice, twice], 0)


def product(left, right):
    width = right.shape[1] // 2
    both = dot(left, right)
    return both[:, :width] + both[:, width:]


def right_parts(right):
    high, low = halves(right)
    return jnp.concatenate([high, low], 1), high


def rows_product(left, parts):
    return halves_product(*halves(left), parts)


def halves_product(high, low, parts):
    width = parts[1].shape[1]
    both = dot(high, parts[0])
    return both[:, :width] + (both[:, width:] + dot(low, parts[1]))


def eye_of(width):
    rows = lax.broadcasted_iota(jnp.int32, (width, width), 0)
    cols = lax.broadcasted_iota(jnp.int32, (width, width), 1)
    return rows, cols


def polar(cross, sign):
    rows, cols = eye_of(cross.shape[0])
    unit = (rows == cols).astype(F32)
    damp = 1.0 / (1.0 + jnp.sqrt(jnp.sum(cross * cross, keepdims=True)))
    left, right = spread(cross)
    left_t, right_t = spread(cross.T)
    s = [product(left, right_t) * (damp * damp), product(left_t, right) * (damp * damp)]
    x = cross * (damp * sign)
    x_left = spread(x)[0]
    s_spread = [spread(a) for a in s]
    s2 = [product(*a) for a in s_spread]
    xs = product(x_left, s_spread[1][1])
    s2_spread = [spread(a) for a in s2]
    s3 = [product(a[0], b[1]) for a, b in zip(s2_spread, s_spread)]
    s4 = [product(*a) for a in s2_spread]
    xs2, xs3 = product(x_left, s2_spread[1][1]), product(spread(xs)[0], s2_spread[1][1])
    e = [0.75 * a - 0.25 * b for a, b in zip(s2, s3)]
    z = [unit - 0.5 * a + 0.5 * b - 0.25 * (0.75 * c - 0.25 * d) for a, b, c, d in zip(s, e, s3, s4)]
    w = [0.75 * unit + 0.25 * a for a in e]
    xw = 0.75 * x + 0.25 * (0.75 * xs2 - 0.25 * xs3)
    e2 = [product(*spread(a)) for a in e]
    zw = [product(spread(a)[0], spread(b)[1]) for a, b in zip(z, w)]
    z_right = spread(z[1])[1]
    xz, xwz = product(x_left, z_right), product(spread(xw)[0], z_right)
    e2_right = [spread(a)[1] for a in e2]
    upper, lower = [a + 0.5 * product(spread(b)[0], c) for a, b, c in zip(z, zw, e2_right)]
    return upper, xz + 0.5 * product(spread(xwz)[0], e2_right[1]), lower


def scaled(cross, down, across):
    return cross * lax.rsqrt(down + 1e-06) * lax.rsqrt(across + 1e-06)


def rotation_of(upper, cross, lower, sign):
    width = cross.shape[0]
    rows, cols = eye_of(width)
    same = rows == cols
    zero = jnp.zeros((width, width), F32)
    down = jnp.sum(jnp.where(same, upper, zero), 1, keepdims=True)
    across = jnp.sum(jnp.where(same, lower, zero), 0, keepdims=True)
    top, wide, bottom = polar(scaled(cross, down, across), sign)
    first = jnp.concatenate([jnp.concatenate([top, wide], 1), jnp.concatenate([-wide.T, bottom], 1)], 0)
    gram = jnp.concatenate(
        [jnp.concatenate([upper, cross], 1), jnp.concatenate([cross.T, lower], 1)], 0
    )
    turned = rows_product(gram, right_parts(first))
    second_cross = rows_product(first[:, :width].T, right_parts(turned[:, width:]))
    diagonal = jnp.sum(first * turned, 0, keepdims=True)
    down = jnp.sum(jnp.where(same, diagonal[:, :width], zero), 1, keepdims=True)
    top, wide, bottom = polar(scaled(second_cross, down, diagonal[:, width:]), sign)
    return gram, first, jnp.concatenate([top, -wide.T], 0), jnp.concatenate([wide, bottom], 0)


def core_of():
    return lax.rem(lax.axis_index("row"), 2)


def first_is_upper():
    p = lax.axis_index("pair")
    clock_upper = (p == 0) | (lax.rem(p, 2) == 1)
    return (core_of() == 0) == clock_upper


def call(kernel, outs, args, name, flops=0, scratch=(), aliases=None, limit=SCOPED):
    places = [place for _, place in args]
    outs = [(*out, F32)[:3] for out in outs]
    out_places = [place for _, place, _ in outs]
    return pl.pallas_call(
        kernel,
        in_specs=[pl.BlockSpec(memory_space=place) for place in places],
        out_specs=[pl.BlockSpec(memory_space=place) for place in out_places],
        out_shape=[
            place(shape, dtype) if place == HERE else jax.ShapeDtypeStruct(shape, dtype) for shape, place, dtype in outs
        ],
        scratch_shapes=list(scratch),
        input_output_aliases=aliases or {},
        compiler_params=pltpu.CompilerParams(vmem_limit_bytes=limit),
        cost_estimate=pl.CostEstimate(flops=flops if flops == LONG else 0, bytes_accessed=0, transcendentals=0),
        name=name,
    )(*[pltpu.with_memory_space_constraint(array, place) for array, place in args])


LONG = 11500000000
HERE = pltpu.VMEM
FAR = pltpu.HBM


class Rows:
    def __init__(self, *parts):
        self.parts = parts

    @classmethod
    def of(cls, refs, sizes):
        return cls(*[(ref, sum(sizes[:k]), sizes[k], 0) for k, ref in enumerate(refs)])

    def at(self, start, count):
        for ref, first, number, offset in self.parts:
            if first <= start and start + count <= first + number:
                return ref, pl.ds(offset + start - first, count)
        raise ValueError(start)

    def get(self, start, count):
        ref, rows = self.at(start, count)
        return ref[rows, :]

    def pair(self, start, count):
        ref, rows = self.at(start, count)
        return jnp.concatenate([ref[0, rows, :], ref[1, rows, :]], 1)


def spans(start, stop, step, *cuts):
    pieces = []
    while start < stop:
        count = min([step, stop - start] + [cut - start for cut in cuts if cut > start])
        pieces.append((start, count))
        start += count
    return pieces


def raw_rows(matrix, count):
    width = matrix.shape[2]

    def kernel(matrix_ref, out_ref, sems):
        copies = [
            pltpu.make_async_copy(matrix_ref.at[k, pl.ds(0, count)], out_ref.at[k], sems.at[k]) for k in range(2)
        ]
        for copy in copies:
            copy.start()
        for copy in copies:
            copy.wait()

    return call(
        kernel,
        [((2, count, width), HERE)],
        [(matrix, FAR)],
        "raw_rows",
        0,
        [pltpu.SemaphoreType.DMA((2,))],
        limit=WHOLE,
    )[0]


def tapered(start, stop, step, unit, *cuts):
    pieces = []
    while start < stop:
        count = min(step, max(unit, (stop - start) // 2 // unit * unit))
        pieces += spans(start, start + count, step, *cuts)
        start += count
    return pieces


def local_gram(matrix, step):
    rows, width = matrix.shape[1:]

    def kernel(matrix_ref, keep_ref, give_ref):
        local = Rows((matrix_ref, 0, rows, 0))
        total = jnp.zeros((2 * width, 4 * width), F32)
        for start, count in spans(0, rows, step):
            high, low = halves(local.pair(start, count))
            total = total + dot(high, jnp.concatenate([high, low], 1), ((0,), (0,)))
        rest = total[:, 2 * width :]
        total = total[:, : 2 * width] + (rest + rest.T)
        upper, cross, lower = total[:width, :width], total[:width, width:], total[width:, width:]
        r, c = eye_of(width)
        diagonal = jnp.sum(jnp.where(r == c, lower, jnp.zeros_like(lower)), 0, keepdims=True)
        packed = jnp.where(r <= c, upper, lower)
        pad = jnp.broadcast_to(diagonal, (8, width))
        mine = core_of() == 0
        keep_ref[:width] = jnp.where(mine, cross, packed)
        give_ref[:width] = jnp.where(mine, packed, cross)
        keep_ref[width:] = pad
        give_ref[width:] = pad

    return call(
        kernel, [((width + 8, width), HERE)] * 2, [(matrix, HERE)], "gram", 16 * rows * width * width
    )


def first_rotation(mine, other):
    width = mine.shape[1]

    def kernel(mine_ref, other_ref, first_ref, base_ref, half_ref, gram_ref):
        holds_cross = core_of() == 0
        mine, other = mine_ref[...], other_ref[...]
        cross = jnp.where(holds_cross, mine[:width], other[:width])
        packed = jnp.where(holds_cross, other, mine)
        diagonal = packed[width : width + 1]
        packed = packed[:width]
        rows, cols = eye_of(width)
        flipped = packed.T
        upper = jnp.where(rows <= cols, packed, flipped)
        lower = jnp.where(rows > cols, packed, flipped)
        lower = jnp.where(rows == cols, diagonal, lower)
        gram, first, left, right = rotation_of(upper, cross, lower, 1.0)
        upper_first = first_is_upper()
        gram_ref[...] = gram
        first_ref[...] = rows_product(first, right_parts(jnp.where(upper_first, left, right)))
        base_ref[...] = first
        half_ref[...] = jnp.where(upper_first, right, left)

    half = ((2 * width, width), HERE)
    square = ((2 * width, 2 * width), HERE)
    return call(kernel, [half, square, half, square], [(mine, HERE), (other, HERE)], "first_rotation")


def share_of():
    return lax.rem(lax.div(lax.axis_index("row"), 2), 2)


def rotated_gram(gram, turn):
    return rows_product(turn.T, right_parts(rows_product(gram, right_parts(turn))))


def small_part(matrix, early, turn, gram, small, step):
    width = turn.shape[1]
    turn_share, gram_share = width, width // 2

    def kernel(matrix_ref, turn_ref, gram_ref, out_ref, square_ref):
        place = share_of()
        local = Rows((matrix_ref, -early, matrix.shape[1], 0))
        parts = right_parts(turn_ref[...])
        for start, number in spans(0, small, step):
            out_ref[pl.ds(SHARE * width // 2 + start, number), :] = rows_product(local.pair(start, number), parts)
        square_ref[...] = rotated_gram(gram_ref[...], turn_ref[...])
        out_ref[:turn_share] = turn_ref[pl.ds(pl.multiple_of(place * turn_share, turn_share), turn_share), :]
        out_ref[turn_share : turn_share + gram_share] = square_ref[
            pl.ds(pl.multiple_of(place * gram_share, gram_share), gram_share), :
        ]

    return call(
        kernel,
        [((SHARE * width // 2 + small, width), HERE)],
        [(matrix, HERE), (turn, HERE), (gram, HERE)],
        "small_part",
        12 * small * width * width,
        [pltpu.VMEM((width, width), F32)],
    )[0]


def sent_parts(matrix, early, first, base, half, gram, small, last, step):
    width = first.shape[1]
    count = matrix.shape[1] - early

    def kernel(matrix_ref, first_ref, base_ref, half_ref, gram_ref, main_ref, last_ref, second_ref, second_gram_ref):
        local = Rows((matrix_ref, -early, matrix.shape[1], 0))
        out = Rows((main_ref, small, count - small - last, 0), (last_ref, count - last, last, 0))
        parts = right_parts(first_ref[...])
        for start, number in spans(small, count, step, count - last):
            ref, place = out.at(start, number)
            ref[place, :] = rows_product(local.pair(start, number), parts)
        second = rows_product(base_ref[...], right_parts(half_ref[...]))
        second_ref[...] = second
        second_gram_ref[...] = rotated_gram(gram_ref[...], second)

    return call(
        kernel,
        [((count - small - last, width), HERE), ((last, width), HERE), ((2 * width, width), HERE), ((width, width), HERE)],
        [(part, HERE) for part in (matrix, first, base, half, gram)],
        "sent_parts",
        12 * count * width * width,
    )


def rest_parts(matrix, early, first, second, sent, bulk, step):
    width = first.shape[1]
    rows = matrix.shape[1]
    arrays = [array for array, *_ in sent]

    def kernel(matrix_ref, first_ref, second_ref, *refs):
        bulk_ref, tail_ref, high_half_ref, low_half_ref = refs[len(sent) :]
        here = Rows((matrix_ref, 0, rows, 0))
        there = Rows(*[(ref, *where) for ref, (_, *where) in zip(refs, sent)])
        out = Rows.of((bulk_ref, tail_ref), (bulk, rows - bulk))
        parts = right_parts(second_ref[...])
        for start, count in spans(0, rows, step, bulk, early):
            ref, place = out.at(start, count)
            ref[place, :] = rows_product(here.pair(start, count), parts)
        parts = right_parts(first_ref[...])
        for start, count in spans(0, rows, step, early, *[first for _, first, *_ in sent]):
            block = rows_product(here.pair(start, count), parts) if start < early else there.get(start, count)
            place = pl.ds(start, count)
            high_half_ref[place, :], low_half_ref[place, :] = halves(block)

    return call(
        kernel,
        [((bulk, width), HERE), ((rows - bulk, width), HERE)] + [((rows, width), HERE, BF16)] * 2,
        [(part, HERE) for part in (matrix, first, second, *arrays)],
        "rest_parts",
        12 * (rows + early) * width * width,
    )


def cross_term(high, low):
    width = high.shape[1] // 2
    own = jnp.concatenate([high[:, :width], low[:, :width]], 1)
    far = jnp.concatenate([high[:, width:], low[:, width:]], 1)
    return dot(own, far, ((0,), (0,)))


def cross_sum(total):
    width = total.shape[0] // 2
    return (total[:width, :width] + total[:width, width:]) + (total[width:, :width] + total[width:, width:])


def raw_cross(far_raw, far_small, share, bulk, tail, step):
    width = bulk.shape[1]
    offset = SHARE * width // 2
    early, small = far_raw.shape[1], far_small.shape[0] - offset
    turn_share, gram_share = width, width // 2

    def kernel(
        raw_ref, small_ref, share_ref, bulk_ref, tail_ref, high_ref, low_ref, gram_ref, out_ref, turn_ref
    ):
        for place, ref in ((share_of(), small_ref), (1 - share_of(), share_ref)):
            turn_ref[pl.ds(pl.multiple_of(place * turn_share, turn_share), turn_share), :] = ref[:turn_share]
            gram_ref[pl.ds(pl.multiple_of(place * gram_share, gram_share), gram_share), :] = ref[
                turn_share : turn_share + gram_share
            ]
        own = Rows.of((bulk_ref, tail_ref), (bulk.shape[0], tail.shape[0]))
        raw = Rows((raw_ref, 0, early, 0))
        far = Rows((small_ref, early, small, offset))
        parts = right_parts(turn_ref[...])
        total = jnp.zeros((2 * width, 2 * width), F32)
        for start, count in spans(0, early + small, step, early, bulk.shape[0]):
            block = rows_product(raw.pair(start, count), parts) if start < early else far.get(start, count)
            high, low = halves(jnp.concatenate([own.get(start, count), block], 1))
            place = pl.ds(start, count)
            high_ref[place, :], low_ref[place, :] = high, low
            total = total + cross_term(high, low)
        out_ref[...] = cross_sum(total)

    return call(
        kernel,
        [((early + small, 2 * width), HERE, BF16)] * 2 + [((width, width), HERE)] * 2,
        [(part, HERE) for part in (far_raw, far_small, share, bulk, tail)],
        "raw_cross",
        12 * (early + small) * width * width,
        [pltpu.VMEM((2 * width, width), F32)],
    )


def more_cross(far, first_row, count, bulk, tail, so_far, step, name):
    width = bulk.shape[1]

    def kernel(far_ref, bulk_ref, tail_ref, total_ref, high_ref, low_ref, out_ref):
        own = Rows.of((bulk_ref, tail_ref), (bulk.shape[0], tail.shape[0]))
        part = Rows((far_ref, first_row, count, 0))
        total = jnp.zeros((2 * width, 2 * width), F32)
        for start, number in spans(first_row, first_row + count, step, bulk.shape[0]):
            high, low = halves(jnp.concatenate([own.get(start, number), part.get(start, number)], 1))
            place = pl.ds(start - first_row, number)
            high_ref[place, :], low_ref[place, :] = high, low
            total = total + cross_term(high, low)
        out_ref[...] = total_ref[...] + cross_sum(total)

    return call(
        kernel,
        [((count, 2 * width), HERE, BF16)] * 2 + [((width, width), HERE)],
        [(far, HERE), (bulk, HERE), (tail, HERE), (so_far, HERE)],
        name,
        6 * count * width * width,
    )


def second_rotation(own_gram, far_gram, here, there):
    width = here.shape[1]

    def kernel(own_gram_ref, far_ref, here_ref, there_ref, out_ref):
        p, n = lax.axis_index("pair"), lax.axis_size("pair")
        odd = lax.rem(p, 2) == 1
        outward = core_of() == 1
        own_upper_out = (p == 0) | (odd & (p != n - 1))
        own_upper = (outward & own_upper_out) | (jnp.logical_not(outward) & jnp.logical_not(odd))
        sign = jnp.where(own_upper, 1.0, -1.0).astype(F32)
        cross = here_ref[...] + there_ref[...].T
        _, first, left, right = rotation_of(own_gram_ref[...], cross, far_ref[...], sign)
        keeps_own = (outward & (p == 0)) | (jnp.logical_not(outward) & (p == 1))
        out_ref[...] = rows_product(first, right_parts(jnp.where(keeps_own, left, right)))

    return call(
        kernel,
        [((2 * width, width), HERE)],
        [(own_gram, HERE), (far_gram, HERE), (here, HERE), (there, HERE)],
        "second_rotation",
        LONG,
    )[0]


def last_product(load, arrays, turn, done, slot_of, start, count, rows, step, cuts, name):
    width = turn.shape[1]
    pieces = tapered(start, start + count, 2 * step, step // STEP, *cuts)

    def kernel(*refs):
        turn_ref = refs[len(arrays)]
        out_ref, stage_ref, sems = refs[-3:]
        parts = right_parts(turn_ref[...])
        slot = slot_of()
        copies = []
        for k, (row, number) in enumerate(pieces):
            place = pl.ds(row - start, number)
            stage_ref[place, :] = halves_product(*load(refs, row, number), parts)
            copies.append(
                pltpu.make_async_copy(stage_ref.at[place, :], out_ref.at[slot, pl.ds(row, number), :], sems.at[k])
            )
            copies[-1].start()
        for copy in copies:
            copy.wait()

    args = [(array, HERE) for array in (*arrays, turn)] + ([] if done is None else [(done, FAR)])
    return call(
        kernel,
        [((2, rows, width), FAR)],
        args,
        name,
        12 * count * width * width,
        [pltpu.VMEM((count, width), F32), pltpu.SemaphoreType.DMA((len(pieces),))],
        None if done is None else {len(args) - 1: 0},
    )[0]


def first_slot():
    return jnp.where(lax.rem(lax.axis_index("pair"), 2) == core_of(), 1, 0)


def body(pairs_count, rows_count, matrix):
    rows, width = matrix.shape[1:]
    unit = rows // 32
    early, small, last, bulk, step = (part * unit for part in (RAW, SMALL, LAST, BULK, STEP))
    main = rows - early - small - last
    offset = SHARE * width // 2
    flat = [(p, r) for p in range(pairs_count) for r in range(rows_count)]
    ahead = {p: after(p, pairs_count) for p in range(pairs_count)}
    behind = {q: p for p, q in ahead.items()}

    def route(moves):
        return [(p * rows_count + r, q * rows_count + t) for (p, r) in flat for (q, t) in [moves(p, r)]]

    outward = route(lambda p, r: (ahead[p] if r % 2 == 0 else behind[p], r))
    inward = route(lambda p, r: (behind[p] if r % 2 == 0 else ahead[p], r))

    core = [(r, r ^ 1) for r in range(rows_count)]

    def travel(block, moves):
        return lax.ppermute(block, ("pair", "row"), moves)

    def chip_sum(block, radix, flip=0):
        distance = 2
        while distance < rows_count:
            steps = [distance] if radix == 2 or 2 * distance >= rows_count else [distance, 2 * distance, 3 * distance]
            hops = [d ^ flip for d in steps] + ([1] if flip else [])
            others = [lax.ppermute(block, "row", [(r, r ^ d) for r in range(rows_count)]) for d in hops]
            block = others.pop() if flip else block
            for other in others:
                block = block + other
            distance *= 1 + len(steps)
            flip = 0
        return block

    def other_sum(block):
        return chip_sum(block, 4, 1)

    low = raw_rows(matrix, early)
    far_raw = travel(low, outward)
    keep, give = local_gram(matrix, step)
    mine = chip_sum(keep + lax.ppermute(give, "row", core), 4)
    other = lax.ppermute(mine, "row", core)
    turn_first, base, half, gram = first_rotation(mine, other)

    sent_small = small_part(matrix, early, turn_first, gram, small, step)
    far_small = travel(sent_small, outward)
    turn_main, sent_small, far_raw = lax.optimization_barrier((turn_first, sent_small, far_raw))
    sent_main, sent_last, turn_second, second_gram = sent_parts(matrix, early, turn_main, base, half, gram, small, last, step)
    far_main, far_last = travel(sent_main, outward), travel(sent_last, outward)
    turn_second, sent_main = lax.optimization_barrier((turn_second, sent_main))
    sent = [(sent_small, early, small, offset), (sent_main, early + small, main, 0), (sent_last, rows - last, last, 0)]
    second_bulk, second_tail, *first_halves = rest_parts(matrix, early, turn_first, turn_second, sent, bulk, step)

    far_small, second_bulk = lax.optimization_barrier((far_small, second_bulk))
    share = lax.ppermute(far_small[:offset], "row", [(r, r ^ 2) for r in range(rows_count)])
    share, later_bulk, later_tail = lax.optimization_barrier((share, second_bulk, second_tail))
    *raw_halves, far_gram, cross = raw_cross(far_raw, far_small, share, second_bulk, second_tail, step)
    far_main, cross = lax.optimization_barrier((far_main, cross))
    *main_halves, cross = more_cross(
        far_main, early + small, main, second_bulk, second_tail, cross, step, "main_cross"
    )
    far_bulk, far_tail = travel(later_bulk, inward), travel(later_tail, inward)
    *last_halves, cross = more_cross(far_last, rows - last, last, second_bulk, second_tail, cross, step, "last_cross")

    total = other_sum(cross)
    there = travel(total, outward)
    here = lax.ppermute(total, "row", core)
    turn_here = second_rotation(second_gram, far_gram, here, there)
    turn_there = lax.ppermute(turn_here, "row", core)

    sizes = early + small, main, last

    def load_here(refs, row, number):
        return [Rows.of(refs[k : 6 : 2], sizes).get(row, number) for k in (0, 1)]

    def other_slot():
        return 1 - first_slot()

    def load_there(refs, row, number):
        place = pl.ds(row, number)
        far = halves(Rows.of(refs[2:4], (bulk, rows - bulk)).get(row, number))
        return [jnp.concatenate([ref[place, :], half], 1) for ref, half in zip(refs, far)]

    cuts = early + small, rows - last
    done = last_product(
        load_here, raw_halves + main_halves + last_halves, turn_here, None, first_slot, 0, rows, rows, step, cuts, "here_product"
    )

    def load_tail(refs, row, number):
        place = pl.ds(row, number)
        far = halves(Rows((refs[2], bulk, rows - bulk, 0)).get(row, number))
        return [jnp.concatenate([ref[place, :], half], 1) for ref, half in zip(refs, far)]

    done = last_product(
        load_there, [*first_halves, far_bulk, far_bulk], turn_there, done, other_slot, 0, bulk, rows, step, [], "bulk_product"
    )
    return last_product(
        load_tail, [*first_halves, far_tail], turn_there, done, other_slot, bulk, rows - bulk, rows, step, [], "tail_product"
    )


def solution(mesh):
    spec = P(None, "row", "pair")
    run = functools.partial(body, mesh.shape["pair"], mesh.shape["row"])
    return jax.shard_map(run, mesh=mesh, in_specs=(spec,), out_specs=spec, check_vma=False)
```

```python
import functools

import jax
import jax.numpy as jnp
from jax import lax
from jax.experimental import pallas as pl
from jax.experimental.pallas import tpu as pltpu
from jax.sharding import PartitionSpec as P


F32 = jnp.float32
BF16 = jnp.bfloat16
SCOPED = 16 * 1024 * 1024
WHOLE = 54 * 1024 * 1024

RAW = 14
SMALL = 7
LAST = 4
BULK = 29
STEP = 4
SHARE = 3


def after(p, n):
    if p == 0:
        return 1
    if p % 2:
        return n - 2 if p == n - 1 else p + 2
    return p - 2


def halves(x):
    high = x.astype(BF16)
    return high, (x - high.astype(F32)).astype(BF16)


def dot(left, right, contract=((1,), (0,))):
    return lax.dot_general(left, right, (contract, ((), ())), preferred_element_type=F32)


def spread(x):
    twice = jnp.concatenate(halves(x), 1)
    return twice, jnp.concatenate([twice, twice], 0)


def product(left, right):
    width = right.shape[1] // 2
    both = dot(left, right)
    return both[:, :width] + both[:, width:]


def right_parts(right):
    high, low = halves(right)
    return jnp.concatenate([high, low], 1), high


def rows_product(left, parts):
    return halves_product(*halves(left), parts)


def halves_product(high, low, parts):
    width = parts[1].shape[1]
    both = dot(high, parts[0])
    return both[:, :width] + (both[:, width:] + dot(low, parts[1]))


def eye_of(width):
    rows = lax.broadcasted_iota(jnp.int32, (width, width), 0)
    cols = lax.broadcasted_iota(jnp.int32, (width, width), 1)
    return rows, cols


def polar(cross, sign):
    rows, cols = eye_of(cross.shape[0])
    unit = (rows == cols).astype(F32)
    damp = 1.0 / (1.0 + jnp.sqrt(jnp.sum(cross * cross, keepdims=True)))
    left, right = spread(cross)
    left_t, right_t = spread(cross.T)
    s = [product(left, right_t) * (damp * damp), product(left_t, right) * (damp * damp)]
    x = cross * (damp * sign)
    x_left = spread(x)[0]
    s_spread = [spread(a) for a in s]
    s2 = [product(*a) for a in s_spread]
    xs = product(x_left, s_spread[1][1])
    s2_spread = [spread(a) for a in s2]
    s3 = [product(a[0], b[1]) for a, b in zip(s2_spread, s_spread)]
    s4 = [product(*a) for a in s2_spread]
    xs2, xs3 = product(x_left, s2_spread[1][1]), product(spread(xs)[0], s2_spread[1][1])
    e = [0.75 * a - 0.25 * b for a, b in zip(s2, s3)]
    z = [unit - 0.5 * a + 0.5 * b - 0.25 * (0.75 * c - 0.25 * d) for a, b, c, d in zip(s, e, s3, s4)]
    w = [0.75 * unit + 0.25 * a for a in e]
    xw = 0.75 * x + 0.25 * (0.75 * xs2 - 0.25 * xs3)
    e2 = [product(*spread(a)) for a in e]
    zw = [product(spread(a)[0], spread(b)[1]) for a, b in zip(z, w)]
    z_right = spread(z[1])[1]
    xz, xwz = product(x_left, z_right), product(spread(xw)[0], z_right)
    e2_right = [spread(a)[1] for a in e2]
    upper, lower = [a + 0.5 * product(spread(b)[0], c) for a, b, c in zip(z, zw, e2_right)]
    return upper, xz + 0.5 * product(spread(xwz)[0], e2_right[1]), lower


def scaled(cross, down, across):
    return cross * lax.rsqrt(down + 1e-06) * lax.rsqrt(across + 1e-06)


def rotation_of(upper, cross, lower, sign):
    width = cross.shape[0]
    rows, cols = eye_of(width)
    same = rows == cols
    zero = jnp.zeros((width, width), F32)
    down = jnp.sum(jnp.where(same, upper, zero), 1, keepdims=True)
    across = jnp.sum(jnp.where(same, lower, zero), 0, keepdims=True)
    top, wide, bottom = polar(scaled(cross, down, across), sign)
    first = jnp.concatenate([jnp.concatenate([top, wide], 1), jnp.concatenate([-wide.T, bottom], 1)], 0)
    gram = jnp.concatenate(
        [jnp.concatenate([upper, cross], 1), jnp.concatenate([cross.T, lower], 1)], 0
    )
    turned = rows_product(gram, right_parts(first))
    second_cross = rows_product(first[:, :width].T, right_parts(turned[:, width:]))
    diagonal = jnp.sum(first * turned, 0, keepdims=True)
    down = jnp.sum(jnp.where(same, diagonal[:, :width], zero), 1, keepdims=True)
    top, wide, bottom = polar(scaled(second_cross, down, diagonal[:, width:]), sign)
    return gram, first, jnp.concatenate([top, -wide.T], 0), jnp.concatenate([wide, bottom], 0)


def core_of():
    return lax.rem(lax.axis_index("row"), 2)


def first_is_upper():
    p = lax.axis_index("pair")
    clock_upper = (p == 0) | (lax.rem(p, 2) == 1)
    return (core_of() == 0) == clock_upper


def call(kernel, outs, args, name, flops=0, scratch=(), aliases=None, limit=SCOPED):
    places = [place for _, place in args]
    outs = [(*out, F32)[:3] for out in outs]
    out_places = [place for _, place, _ in outs]
    return pl.pallas_call(
        kernel,
        in_specs=[pl.BlockSpec(memory_space=place) for place in places],
        out_specs=[pl.BlockSpec(memory_space=place) for place in out_places],
        out_shape=[
            place(shape, dtype) if place == HERE else jax.ShapeDtypeStruct(shape, dtype) for shape, place, dtype in outs
        ],
        scratch_shapes=list(scratch),
        input_output_aliases=aliases or {},
        compiler_params=pltpu.CompilerParams(vmem_limit_bytes=limit),
        cost_estimate=pl.CostEstimate(flops=flops if flops == LONG else 0, bytes_accessed=0, transcendentals=0),
        name=name,
    )(*[pltpu.with_memory_space_constraint(array, place) for array, place in args])


LONG = 12650000000
HERE = pltpu.VMEM
FAR = pltpu.HBM


class Rows:
    def __init__(self, *parts):
        self.parts = parts

    @classmethod
    def of(cls, refs, sizes):
        return cls(*[(ref, sum(sizes[:k]), sizes[k], 0) for k, ref in enumerate(refs)])

    def at(self, start, count):
        for ref, first, number, offset in self.parts:
            if first <= start and start + count <= first + number:
                return ref, pl.ds(offset + start - first, count)
        raise ValueError(start)

    def get(self, start, count):
        ref, rows = self.at(start, count)
        return ref[rows, :]

    def pair(self, start, count):
        ref, rows = self.at(start, count)
        return jnp.concatenate([ref[0, rows, :], ref[1, rows, :]], 1)


def spans(start, stop, step, *cuts):
    pieces = []
    while start < stop:
        count = min([step, stop - start] + [cut - start for cut in cuts if cut > start])
        pieces.append((start, count))
        start += count
    return pieces


def raw_rows(matrix, count):
    width = matrix.shape[2]

    def kernel(matrix_ref, out_ref, sems):
        copies = [
            pltpu.make_async_copy(matrix_ref.at[k, pl.ds(0, count)], out_ref.at[k], sems.at[k]) for k in range(2)
        ]
        for copy in copies:
            copy.start()
        for copy in copies:
            copy.wait()

    return call(
        kernel,
        [((2, count, width), HERE)],
        [(matrix, FAR)],
        "raw_rows",
        0,
        [pltpu.SemaphoreType.DMA((2,))],
        limit=WHOLE,
    )[0]


def tapered(start, stop, step, unit, *cuts):
    pieces = []
    while start < stop:
        count = min(step, max(unit, (stop - start) // 2 // unit * unit))
        pieces += spans(start, start + count, step, *cuts)
        start += count
    return pieces


def local_gram(matrix, step):
    rows, width = matrix.shape[1:]

    def kernel(matrix_ref, keep_ref, give_ref):
        local = Rows((matrix_ref, 0, rows, 0))
        total = jnp.zeros((2 * width, 4 * width), F32)
        for start, count in spans(0, rows, step):
            high, low = halves(local.pair(start, count))
            total = total + dot(high, jnp.concatenate([high, low], 1), ((0,), (0,)))
        rest = total[:, 2 * width :]
        total = total[:, : 2 * width] + (rest + rest.T)
        upper, cross, lower = total[:width, :width], total[:width, width:], total[width:, width:]
        r, c = eye_of(width)
        diagonal = jnp.sum(jnp.where(r == c, lower, jnp.zeros_like(lower)), 0, keepdims=True)
        packed = jnp.where(r <= c, upper, lower)
        pad = jnp.broadcast_to(diagonal, (8, width))
        mine = core_of() == 0
        keep_ref[:width] = jnp.where(mine, cross, packed)
        give_ref[:width] = jnp.where(mine, packed, cross)
        keep_ref[width:] = pad
        give_ref[width:] = pad

    return call(
        kernel, [((width + 8, width), HERE)] * 2, [(matrix, HERE)], "gram", 16 * rows * width * width
    )


def first_rotation(mine, other):
    width = mine.shape[1]

    def kernel(mine_ref, other_ref, first_ref, second_ref, gram_ref):
        holds_cross = core_of() == 0
        mine, other = mine_ref[...], other_ref[...]
        cross = jnp.where(holds_cross, mine[:width], other[:width])
        packed = jnp.where(holds_cross, other, mine)
        diagonal = packed[width : width + 1]
        packed = packed[:width]
        rows, cols = eye_of(width)
        flipped = packed.T
        upper = jnp.where(rows <= cols, packed, flipped)
        lower = jnp.where(rows > cols, packed, flipped)
        lower = jnp.where(rows == cols, diagonal, lower)
        gram, first, left, right = rotation_of(upper, cross, lower, 1.0)
        upper_first = first_is_upper()
        gram_ref[...] = gram
        first_ref[...] = rows_product(first, right_parts(jnp.where(upper_first, left, right)))
        second_ref[...] = rows_product(first, right_parts(jnp.where(upper_first, right, left)))

    half = ((2 * width, width), HERE)
    return call(kernel, [half, half, ((2 * width, 2 * width), HERE)], [(mine, HERE), (other, HERE)], "first_rotation")


def share_of():
    return lax.rem(lax.div(lax.axis_index("row"), 2), 2)


def rotated_gram(gram, turn):
    return rows_product(turn.T, right_parts(rows_product(gram, right_parts(turn))))


def small_part(matrix, early, turn, gram, small, step):
    width = turn.shape[1]
    turn_share, gram_share = width, width // 2

    def kernel(matrix_ref, turn_ref, gram_ref, out_ref, square_ref):
        place = share_of()
        local = Rows((matrix_ref, -early, matrix.shape[1], 0))
        parts = right_parts(turn_ref[...])
        for start, number in spans(0, small, step):
            out_ref[pl.ds(SHARE * width // 2 + start, number), :] = rows_product(local.pair(start, number), parts)
        square_ref[...] = rotated_gram(gram_ref[...], turn_ref[...])
        out_ref[:turn_share] = turn_ref[pl.ds(pl.multiple_of(place * turn_share, turn_share), turn_share), :]
        out_ref[turn_share : turn_share + gram_share] = square_ref[
            pl.ds(pl.multiple_of(place * gram_share, gram_share), gram_share), :
        ]

    return call(
        kernel,
        [((SHARE * width // 2 + small, width), HERE)],
        [(matrix, HERE), (turn, HERE), (gram, HERE)],
        "small_part",
        12 * small * width * width,
        [pltpu.VMEM((width, width), F32)],
    )[0]


def sent_parts(matrix, early, first, second, gram, small, last, step):
    width = first.shape[1]
    count = matrix.shape[1] - early

    def kernel(matrix_ref, first_ref, second_ref, gram_ref, main_ref, last_ref, second_gram_ref):
        local = Rows((matrix_ref, -early, matrix.shape[1], 0))
        out = Rows((main_ref, small, count - small - last, 0), (last_ref, count - last, last, 0))
        parts = right_parts(first_ref[...])
        for start, number in spans(small, count, step, count - last):
            ref, place = out.at(start, number)
            ref[place, :] = rows_product(local.pair(start, number), parts)
        second_gram_ref[...] = rotated_gram(gram_ref[...], second_ref[...])

    return call(
        kernel,
        [((count - small - last, width), HERE), ((last, width), HERE), ((width, width), HERE)],
        [(matrix, HERE), (first, HERE), (second, HERE), (gram, HERE)],
        "sent_parts",
        12 * count * width * width,
    )


def rest_parts(matrix, early, first, second, sent, bulk, step):
    width = first.shape[1]
    rows = matrix.shape[1]
    arrays = [array for array, *_ in sent]

    def kernel(matrix_ref, first_ref, second_ref, *refs):
        bulk_ref, tail_ref, high_half_ref, low_half_ref = refs[len(sent) :]
        here = Rows((matrix_ref, 0, rows, 0))
        there = Rows(*[(ref, *where) for ref, (_, *where) in zip(refs, sent)])
        out = Rows.of((bulk_ref, tail_ref), (bulk, rows - bulk))
        parts = right_parts(second_ref[...])
        for start, count in spans(0, rows, step, bulk, early):
            ref, place = out.at(start, count)
            ref[place, :] = rows_product(here.pair(start, count), parts)
        parts = right_parts(first_ref[...])
        for start, count in spans(0, rows, step, early, *[first for _, first, *_ in sent]):
            block = rows_product(here.pair(start, count), parts) if start < early else there.get(start, count)
            place = pl.ds(start, count)
            high_half_ref[place, :], low_half_ref[place, :] = halves(block)

    return call(
        kernel,
        [((bulk, width), HERE), ((rows - bulk, width), HERE)] + [((rows, width), HERE, BF16)] * 2,
        [(part, HERE) for part in (matrix, first, second, *arrays)],
        "rest_parts",
        12 * (rows + early) * width * width,
    )


def cross_term(high, low):
    width = high.shape[1] // 2
    own = jnp.concatenate([high[:, :width], low[:, :width]], 1)
    far = jnp.concatenate([high[:, width:], low[:, width:]], 1)
    return dot(own, far, ((0,), (0,)))


def cross_sum(total):
    width = total.shape[0] // 2
    return (total[:width, :width] + total[:width, width:]) + (total[width:, :width] + total[width:, width:])


def raw_cross(far_raw, far_small, share, bulk, tail, step):
    width = bulk.shape[1]
    offset = SHARE * width // 2
    early, small = far_raw.shape[1], far_small.shape[0] - offset
    turn_share, gram_share = width, width // 2

    def kernel(
        raw_ref, small_ref, share_ref, bulk_ref, tail_ref, high_ref, low_ref, gram_ref, out_ref, turn_ref
    ):
        for place, ref in ((share_of(), small_ref), (1 - share_of(), share_ref)):
            turn_ref[pl.ds(pl.multiple_of(place * turn_share, turn_share), turn_share), :] = ref[:turn_share]
            gram_ref[pl.ds(pl.multiple_of(place * gram_share, gram_share), gram_share), :] = ref[
                turn_share : turn_share + gram_share
            ]
        own = Rows.of((bulk_ref, tail_ref), (bulk.shape[0], tail.shape[0]))
        raw = Rows((raw_ref, 0, early, 0))
        far = Rows((small_ref, early, small, offset))
        parts = right_parts(turn_ref[...])
        total = jnp.zeros((2 * width, 2 * width), F32)
        for start, count in spans(0, early + small, step, early, bulk.shape[0]):
            block = rows_product(raw.pair(start, count), parts) if start < early else far.get(start, count)
            high, low = halves(jnp.concatenate([own.get(start, count), block], 1))
            place = pl.ds(start, count)
            high_ref[place, :], low_ref[place, :] = high, low
            total = total + cross_term(high, low)
        out_ref[...] = cross_sum(total)

    return call(
        kernel,
        [((early + small, 2 * width), HERE, BF16)] * 2 + [((width, width), HERE)] * 2,
        [(part, HERE) for part in (far_raw, far_small, share, bulk, tail)],
        "raw_cross",
        12 * (early + small) * width * width,
        [pltpu.VMEM((2 * width, width), F32)],
    )


def more_cross(far, first_row, count, bulk, tail, so_far, step, name):
    width = bulk.shape[1]

    def kernel(far_ref, bulk_ref, tail_ref, total_ref, high_ref, low_ref, out_ref):
        own = Rows.of((bulk_ref, tail_ref), (bulk.shape[0], tail.shape[0]))
        part = Rows((far_ref, first_row, count, 0))
        total = jnp.zeros((2 * width, 2 * width), F32)
        for start, number in spans(first_row, first_row + count, step, bulk.shape[0]):
            high, low = halves(jnp.concatenate([own.get(start, number), part.get(start, number)], 1))
            place = pl.ds(start - first_row, number)
            high_ref[place, :], low_ref[place, :] = high, low
            total = total + cross_term(high, low)
        out_ref[...] = total_ref[...] + cross_sum(total)

    return call(
        kernel,
        [((count, 2 * width), HERE, BF16)] * 2 + [((width, width), HERE)],
        [(far, HERE), (bulk, HERE), (tail, HERE), (so_far, HERE)],
        name,
        6 * count * width * width,
    )


def second_rotation(own_gram, far_gram, here, there):
    width = here.shape[1]

    def kernel(own_gram_ref, far_ref, here_ref, there_ref, out_ref):
        p, n = lax.axis_index("pair"), lax.axis_size("pair")
        odd = lax.rem(p, 2) == 1
        outward = core_of() == 1
        own_upper_out = (p == 0) | (odd & (p != n - 1))
        own_upper = (outward & own_upper_out) | (jnp.logical_not(outward) & jnp.logical_not(odd))
        sign = jnp.where(own_upper, 1.0, -1.0).astype(F32)
        cross = here_ref[...] + there_ref[...].T
        _, first, left, right = rotation_of(own_gram_ref[...], cross, far_ref[...], sign)
        keeps_own = (outward & (p == 0)) | (jnp.logical_not(outward) & (p == 1))
        out_ref[...] = rows_product(first, right_parts(jnp.where(keeps_own, left, right)))

    return call(
        kernel,
        [((2 * width, width), HERE)],
        [(own_gram, HERE), (far_gram, HERE), (here, HERE), (there, HERE)],
        "second_rotation",
        LONG,
    )[0]


def last_product(load, arrays, turn, done, slot_of, start, count, rows, step, cuts, name):
    width = turn.shape[1]
    pieces = tapered(start, start + count, 2 * step, step // STEP, *cuts)

    def kernel(*refs):
        turn_ref = refs[len(arrays)]
        out_ref, stage_ref, sems = refs[-3:]
        parts = right_parts(turn_ref[...])
        slot = slot_of()
        copies = []
        for k, (row, number) in enumerate(pieces):
            place = pl.ds(row - start, number)
            stage_ref[place, :] = halves_product(*load(refs, row, number), parts)
            copies.append(
                pltpu.make_async_copy(stage_ref.at[place, :], out_ref.at[slot, pl.ds(row, number), :], sems.at[k])
            )
            copies[-1].start()
        for copy in copies:
            copy.wait()

    args = [(array, HERE) for array in (*arrays, turn)] + ([] if done is None else [(done, FAR)])
    return call(
        kernel,
        [((2, rows, width), FAR)],
        args,
        name,
        12 * count * width * width,
        [pltpu.VMEM((count, width), F32), pltpu.SemaphoreType.DMA((len(pieces),))],
        None if done is None else {len(args) - 1: 0},
    )[0]


def first_slot():
    return jnp.where(lax.rem(lax.axis_index("pair"), 2) == core_of(), 1, 0)


def body(pairs_count, rows_count, matrix):
    rows, width = matrix.shape[1:]
    unit = rows // 32
    early, small, last, bulk, step = (part * unit for part in (RAW, SMALL, LAST, BULK, STEP))
    main = rows - early - small - last
    offset = SHARE * width // 2
    flat = [(p, r) for p in range(pairs_count) for r in range(rows_count)]
    ahead = {p: after(p, pairs_count) for p in range(pairs_count)}
    behind = {q: p for p, q in ahead.items()}

    def route(moves):
        return [(p * rows_count + r, q * rows_count + t) for (p, r) in flat for (q, t) in [moves(p, r)]]

    outward = route(lambda p, r: (ahead[p] if r % 2 == 0 else behind[p], r))
    inward = route(lambda p, r: (behind[p] if r % 2 == 0 else ahead[p], r))

    core = [(r, r ^ 1) for r in range(rows_count)]

    def travel(block, moves):
        return lax.ppermute(block, ("pair", "row"), moves)

    def chip_sum(block, radix, flip=0):
        distance = 2
        while distance < rows_count:
            steps = [distance] if radix == 2 or 2 * distance >= rows_count else [distance, 2 * distance, 3 * distance]
            hops = [d ^ flip for d in steps] + ([1] if flip else [])
            others = [lax.ppermute(block, "row", [(r, r ^ d) for r in range(rows_count)]) for d in hops]
            block = others.pop() if flip else block
            for other in others:
                block = block + other
            distance *= 1 + len(steps)
            flip = 0
        return block

    def other_sum(block):
        return chip_sum(block, 4, 1)

    low = raw_rows(matrix, early)
    far_raw = travel(low, outward)
    keep, give = local_gram(matrix, step)
    mine = chip_sum(keep + lax.ppermute(give, "row", core), 4)
    other = lax.ppermute(mine, "row", core)
    turn_first, turn_second, gram = first_rotation(mine, other)

    sent_small = small_part(matrix, early, turn_first, gram, small, step)
    far_small = travel(sent_small, outward)
    turn_main, sent_small, far_raw = lax.optimization_barrier((turn_first, sent_small, far_raw))
    sent_main, sent_last, second_gram = sent_parts(matrix, early, turn_main, turn_second, gram, small, last, step)
    far_main, far_last = travel(sent_main, outward), travel(sent_last, outward)
    turn_second, sent_main = lax.optimization_barrier((turn_second, sent_main))
    sent = [(sent_small, early, small, offset), (sent_main, early + small, main, 0), (sent_last, rows - last, last, 0)]
    second_bulk, second_tail, *first_halves = rest_parts(matrix, early, turn_first, turn_second, sent, bulk, step)

    far_small, second_bulk = lax.optimization_barrier((far_small, second_bulk))
    share = lax.ppermute(far_small[:offset], "row", [(r, r ^ 2) for r in range(rows_count)])
    share, later_bulk, later_tail = lax.optimization_barrier((share, second_bulk, second_tail))
    *raw_halves, far_gram, cross = raw_cross(far_raw, far_small, share, second_bulk, second_tail, step)
    far_main, cross = lax.optimization_barrier((far_main, cross))
    *main_halves, cross = more_cross(
        far_main, early + small, main, second_bulk, second_tail, cross, step, "main_cross"
    )
    far_bulk, far_tail = travel(later_bulk, inward), travel(later_tail, inward)
    *last_halves, cross = more_cross(far_last, rows - last, last, second_bulk, second_tail, cross, step, "last_cross")

    total = other_sum(cross)
    there = travel(total, outward)
    here = lax.ppermute(total, "row", core)
    turn_here = second_rotation(second_gram, far_gram, here, there)
    turn_there = lax.ppermute(turn_here, "row", core)

    sizes = early + small, main, last

    def load_here(refs, row, number):
        return [Rows.of(refs[k : 6 : 2], sizes).get(row, number) for k in (0, 1)]

    def other_slot():
        return 1 - first_slot()

    def load_there(refs, row, number):
        place = pl.ds(row, number)
        far = halves(Rows.of(refs[2:4], (bulk, rows - bulk)).get(row, number))
        return [jnp.concatenate([ref[place, :], half], 1) for ref, half in zip(refs, far)]

    cuts = early + small, rows - last
    done = last_product(
        load_here, raw_halves + main_halves + last_halves, turn_here, None, first_slot, 0, rows, rows, step, cuts, "here_product"
    )

    def load_tail(refs, row, number):
        place = pl.ds(row, number)
        far = halves(Rows((refs[2], bulk, rows - bulk, 0)).get(row, number))
        return [jnp.concatenate([ref[place, :], half], 1) for ref, half in zip(refs, far)]

    done = last_product(
        load_there, [*first_halves, far_bulk, far_bulk], turn_there, done, other_slot, 0, bulk, rows, step, [], "bulk_product"
    )
    return last_product(
        load_tail, [*first_halves, far_tail], turn_there, done, other_slot, bulk, rows - bulk, rows, step, [], "tail_product"
    )


def solution(mesh):
    spec = P(None, "row", "pair")
    run = functools.partial(body, mesh.shape["pair"], mesh.shape["row"])
    return jax.shard_map(run, mesh=mesh, in_specs=(spec,), out_specs=spec, check_vma=False)
```
